256 devices in a mesh: dp: 2 (over z_hi), row: 32 (over y, x, core), col: 4 (over z_lo).
Axes of the slice: x: 4, y: 4, z: 8 (z_hi: 2, z_lo: 4; z = z_hi * 4 + z_lo), core: 2. Of those that a mesh axis runs over, the one named last changes fastest.
Arguments:
- saved_input: bfloat16 [24576, 2048], P(('dp', 'row'), 'col'), may hold values from -16 to 16
- cotangent: bfloat16 [24576, 2048], P(('dp', 'row'), 'col'), may hold values from -16 to 16
- weight_in: bfloat16 [2048, 4096], P('row', 'col'), may hold values from -0.125 to 0.125
- weight_out: bfloat16 [4096, 2048], P('col', 'row'), may hold values from -0.09375 to 0.09375
- in_row_moment: float32 [2048], P('row'), may hold values from 96 to 6144
- in_col_moment: float32 [4096], P('col'), may hold values from 96 to 6144
- out_row_moment: float32 [4096], P('col'), may hold values from 98304 to 1572864
- out_col_moment: float32 [2048], P('row'), may hold values from 98304 to 1572864
Outputs:
- input_grad: bfloat16 [24576, 2048], P(('dp', 'row'), 'col')
- in_update: float32 [2048, 4096], P('row', 'col')
- out_update: float32 [4096, 2048], P('col', 'row')
- in_row_new: float32 [2048], P('row')
- in_col_new: float32 [4096], P('col')
- out_row_new: float32 [4096], P('col')
- out_col_new: float32 [2048], P('row')
The draws below stay inside these ranges and needn't reach their ends.
All inputs are finite; a program needn't handle non-finite values.
Results may differ from the reference program's by a relative error of at most 0.0049.
Values may be sent and summed in bfloat16 or wider, within the bound.
A program may use at most 128 MiB of HBM per device.

```python
import math
import jax
import jax.numpy as jnp
from jax import lax

D = 2048
FF = 4096
TOKENS = 24576


def strengthened(values, stream_key, source, target, shards_of, factor):
    def block_of(position):
        return (jnp.arange(values.shape[position]) // (values.shape[position] // shards_of)).reshape((-1,) + (1,) * (values.ndim - 1 - position))

    one_side = jax.random.permutation(stream_key, shards_of)[block_of(target)]
    other_side = (block_of(target) + shards_of // 2) % shards_of
    return jnp.where((block_of(source) == one_side) | (block_of(source) == other_side), factor * values, values)


def steps_of(key, extent, cuts, low, top_value):
    gain, own = 1.0, jax.random.fold_in(key, 6)
    for dim, parts in cuts:
        steps = jnp.exp(jax.random.uniform(jax.random.fold_in(own, dim), (parts,), jnp.float32, low / len(cuts), top_value / len(cuts)))
        gain = gain * jnp.repeat(steps, extent[dim] // parts).reshape([-1 if axis == dim else 1 for axis in range(len(extent))])
    return gain


def gaussian(own_key, shape, deviation, bound, cuts=(), kind=jnp.bfloat16):
    entries = deviation * jax.random.normal(own_key, shape, jnp.float32)
    if cuts:
        entries = entries * steps_of(own_key, shape, cuts, -0.22, 0.18)
    return jnp.clip(entries, -bound, bound).astype(kind)


def heavy_noise(stream_key, shape, width, reach, shards, heavy, held_as=jnp.bfloat16):
    entries = width * jax.random.normal(stream_key, shape, jnp.float32)
    if shards:
        entries = entries * steps_of(stream_key, shape, shards, -0.22, 0.18)
    return jnp.clip(strengthened(entries, jax.random.fold_in(stream_key, 3), *heavy), -reach, reach).astype(held_as)


def setup_inputs(seed: int = 0) -> dict:
    seeds = jax.random.split(jax.random.key(seed), 9)
    saved_input = heavy_noise(seeds[0], (TOKENS, D), 1.0, 16.0, ((0, 64), (1, 4)), (0, 1, 64, 4.0))
    cotangent = heavy_noise(seeds[1], (TOKENS, D), 1.0, 16.0, ((0, 64), (1, 4)), (0, 1, 64, 4.0))
    weight_in = gaussian(seeds[2], (D, FF), D ** -0.5, 0.125, ((0, 32), (1, 4)))
    weight_out = gaussian(seeds[3], (FF, D), FF ** -0.5, 0.09375, ((0, 4), (1, 32)))
    in_row_moment = jnp.clip(jnp.exp(math.log(6144.0) - 4.158883 * jax.random.uniform(seeds[4], (D,), jnp.float32) ** steps_of(seeds[4], (D,), ((0, 32),), -0.2, 0.2)), 96.0, 6144.0)
    in_col_moment = jnp.clip(jnp.exp(math.log(6144.0) - 4.158883 * jax.random.uniform(seeds[5], (FF,), jnp.float32) ** steps_of(seeds[5], (FF,), ((0, 4),), -0.2, 0.2)), 96.0, 6144.0)
    out_row_moment = jnp.clip(jnp.exp(math.log(1572864) - 2.7725887 * jax.random.uniform(seeds[6], (FF,), jnp.float32) ** steps_of(seeds[6], (FF,), ((0, 4),), -0.2, 0.2)), 98304.0, 1572864)
    out_col_moment = jnp.clip(jnp.exp(math.log(1572864) - 2.7725887 * jax.random.uniform(seeds[7], (D,), jnp.float32) ** steps_of(seeds[7], (D,), ((0, 32),), -0.2, 0.2)), 98304.0, 1572864)
    return {"saved_input": saved_input, "cotangent": cotangent, "weight_in": weight_in, "weight_out": weight_out, "in_row_moment": in_row_moment, "in_col_moment": in_col_moment, "out_row_moment": out_row_moment, "out_col_moment": out_col_moment}


GELU_SCALE = 0.7978845608028654
GELU_CUBIC = 0.044715
MOMENT_DECAY = 0.8
CLIP_LIMIT = 1.0
EPSILON_SQ = 1e-30

def gelu_parts(values):
    inner = GELU_SCALE * (values + GELU_CUBIC * values * values * values)
    tangent = jnp.tanh(inner)
    output = 0.5 * values * (1.0 + tangent)
    slope = 0.5 * (1.0 + tangent) + 0.5 * values * (1.0 - tangent * tangent) * GELU_SCALE * (1.0 + 3.0 * GELU_CUBIC * values * values)
    return (output, slope)

def adafactor(gradient, row_old, col_old):
    squared = gradient * gradient
    row_new = MOMENT_DECAY * row_old + (1.0 - MOMENT_DECAY) * (lax.optimization_barrier(jnp.mean(squared, axis=1)) + EPSILON_SQ)
    col_new = MOMENT_DECAY * col_old + (1.0 - MOMENT_DECAY) * (lax.optimization_barrier(jnp.mean(squared, axis=0)) + EPSILON_SQ)
    scaling = row_new[:, None] * col_new[None, :] / jnp.mean(row_new)
    raw_update = gradient / jnp.sqrt(scaling)
    rms_value = jnp.sqrt(jnp.mean(raw_update * raw_update))
    update = raw_update / jnp.maximum(1.0, rms_value / CLIP_LIMIT)
    return (update, row_new, col_new)

def reference(saved_input, cotangent, weight_in, weight_out, in_row_moment, in_col_moment, out_row_moment, out_col_moment):
    preact = jnp.dot(saved_input, weight_in, preferred_element_type=jnp.float32)
    output, slope = gelu_parts(preact)
    hidden = output.astype(jnp.bfloat16)
    hidden_grad = jnp.dot(cotangent, weight_out.T, preferred_element_type=jnp.float32)
    preact_grad = (hidden_grad * slope).astype(jnp.bfloat16)
    input_grad = jnp.dot(preact_grad, weight_in.T, preferred_element_type=jnp.float32).astype(jnp.bfloat16)
    grad_in = jnp.dot(saved_input.T, preact_grad, preferred_element_type=jnp.float32)
    grad_out = jnp.dot(hidden.T, cotangent, preferred_element_type=jnp.float32)
    in_update, in_row_new, in_col_new = adafactor(grad_in, in_row_moment, in_col_moment)
    out_update, out_row_new, out_col_new = adafactor(grad_out, out_row_moment, out_col_moment)
    return (input_grad, in_update, out_update, in_row_new, in_col_new, out_row_new, out_col_new)
```

```python
import jax
import jax.numpy as jnp
from jax import lax
from jax.experimental import pallas as pl
from jax.experimental.pallas import tpu as pltpu
from jax.sharding import PartitionSpec as P

MESH = pl.DeviceIdType.MESH
F32 = jnp.float32
BF16 = jnp.bfloat16

GELU_SCALE = 0.7978845608028654
GELU_CUBIC = 0.044715
MOMENT_DECAY = 0.8
CLIP_LIMIT = 1.0
EPSILON_SQ = 1e-30

TOK, WIDTH, UNITS, BLK = 384, 2048, 1024, 512
ALL_UNITS = 4096
ENTRIES = WIDTH * ALL_UNITS

CORE_G, STAGE1, STAGE2, DP, SUMS, SWAP, MOM = 0, 8, 20, 32, 40, 80, 82
W_SWAP, W_RING1, W_RING2, W_PART, LINE, BACK = 83, 85, 89, 105, 121, 145
N_SEM = 157
CHUNKS = ((0, 256), (256, 128), (0, 384))


def gelu_parts(values):
    inner = GELU_SCALE * (values + GELU_CUBIC * values * values * values)
    tangent = jnp.tanh(inner)
    output = 0.5 * values * (1.0 + tangent)
    slope = 0.5 * (1.0 + tangent) + 0.5 * values * (1.0 - tangent * tangent) * GELU_SCALE * (
        1.0 + 3.0 * GELU_CUBIC * values * values
    )
    return (output, slope)


def kernel(
    x_ref, cot_ref, win_ref, wout_ref, in_row_ref, in_col_ref, out_row_ref, out_col_ref,
    ig_ref, in_upd_ref, out_upd_ref, in_row_out, in_col_out, out_row_out, out_col_out,
    dmom_ref, full, w_ref, acc, tr, act, g_own, g_send, g_recv, s1, r1, s2, r2, dp_s, dp_z, dp_r, dmom_in,
    za, xa, zb, xb, ratio, swap_u, swap_v, back_s, back_r, it_own, ig_s,
    ss, rs, local,
):
    d = lax.axis_index("dp")
    r = lax.axis_index("row")
    c = lax.axis_index("col")
    core = lax.rem(r, 2)
    x = lax.rem(r // 2, 4)
    y = r // 8
    p1 = x + core * (y - x)
    p2 = y + core * (x - y)
    k1, k2 = 2 + 6 * core, 8 - 6 * core
    t1, t2 = 1 + 3 * core, 4 - 3 * core
    m = core
    other = 1 - core

    def ring(position, step):
        return lax.rem(position + step, 4)

    def rowdev(q1, q2):
        return {"row": q1 * k1 + q2 * k2 + core}

    partner = {"row": r + 1 - 2 * core}
    right1, left1 = rowdev(ring(p1, 1), p2), rowdev(ring(p1, 3), p2)
    right2, left2 = rowdev(p1, ring(p2, 1)), rowdev(p1, ring(p2, 3))
    up2 = {"dp": lax.rem(d + c // 2, 2), "col": ring(c, 2)}
    down2 = {"dp": lax.rem(d + 1 - c // 2, 2), "col": ring(c, 2)}

    chip = y * 4 + x

    def along_xy(k):
        return {"row": lax.rem(chip + k, 16) * 2 + core}

    def along_z(k):
        return {"col": ring(c, k)}

    def along_z_and_cores(k):
        place = lax.rem(core * 4 + c + k, 8)
        return {"row": r - core + place // 4, "col": lax.rem(place, 4)}

    barrier = pltpu.get_barrier_semaphore()
    peers = [{"dp": 1 - d, "col": ring(c, 2)}]
    peers += [along_z_and_cores(k) for k in range(1, 8)]
    peers += [along_xy(k) for k in range(1, 16)]
    for peer in peers:
        pl.semaphore_signal(barrier, inc=1, device_id=peer, device_id_type=MESH)

    def chip_rows(q1, q2):
        return pl.ds(pl.multiple_of((q1 * t1 + q2 * t2) * 128, 128), 128)

    def half_rows(q1, q2, h):
        return pl.ds(pl.multiple_of((q1 * t1 + q2 * t2) * 128 + h * 64, 64), 64)

    own_rows = half_rows(p1, p2, core)
    loads = [
        pltpu.make_async_copy(x_ref, full.at[0, c], local.at[0]),
        pltpu.make_async_copy(cot_ref, full.at[1, c], local.at[1]),
        pltpu.make_async_copy(win_ref, w_ref.at[0, own_rows, :], local.at[2]),
        pltpu.make_async_copy(wout_ref, w_ref.at[1, own_rows, :], local.at[3]),
    ]
    for copy in loads:
        copy.start()
    for i, ref in enumerate((in_row_ref, out_col_ref)):
        dmom_ref[i] = jnp.broadcast_to(jnp.concatenate([ref[...], ref[...]], axis=1), (8, 128))

    for copy in loads:
        copy.wait()
    pl.semaphore_wait(barrier, len(peers))

    def send(src, dst, number, device):
        copy = pltpu.make_async_remote_copy(
            src_ref=src, dst_ref=dst, send_sem=ss.at[number], recv_sem=rs.at[number],
            device_id=device, device_id_type=MESH,
        )
        copy.start()
        return copy

    pending = []

    def start(src, dst, number, device):
        copy = send(src, dst, number, device)
        pending.append(copy)
        return copy

    def arrived(dst, number):
        pltpu.make_async_remote_copy(
            src_ref=dst, dst_ref=dst, send_sem=ss.at[number], recv_sem=rs.at[number],
            device_id=partner, device_id_type=MESH,
        ).wait_recv()

    def line_number(leftward, k, i, j):
        return LINE + ((leftward * 3 + k - 1) * 2 + j) * 2 + i

    def line_copy(leftward, k, i, j):
        rows = pl.ds(*CHUNKS[j])
        owner = c + (k - 1) if leftward else c - (k - 1)
        number = line_number(leftward, k, i, j)
        return pltpu.make_async_remote_copy(
            src_ref=full.at[i, owner, rows, :], dst_ref=full.at[i, owner, rows, :], send_sem=ss.at[number], recv_sem=rs.at[number],
            device_id={"col": ring(c, 3 if leftward else 1)}, device_id_type=MESH,
        )

    def line_sends(leftward, k):
        return (c > 0) & (c + (k - 1) <= 3) if leftward else (c < 3) & (c - (k - 1) >= 0)

    def line_gets(leftward, k):
        return c + k <= 3 if leftward else c - k >= 0

    def line_start(k, j):
        for leftward in (0, 1):
            @pl.when(line_sends(leftward, k))
            def _(leftward=leftward):
                for i in range(2):
                    line_copy(leftward, k, i, j).start()

    def hand_on(k, j, here=None):
        for i in range(2):
            for leftward in (0, 1):
                gets, sends = line_gets(leftward, k), line_sends(leftward, k + 1)
                if here is not None:
                    gets, sends = gets & here, sends & here

                @pl.when(gets)
                def _(i=i, leftward=leftward):
                    owner = c + k if leftward else c - k
                    arrived(full.at[i, owner, pl.ds(*CHUNKS[j]), :], line_number(leftward, k, i, j))

                if k < 3:
                    @pl.when(sends)
                    def _(i=i, leftward=leftward):
                        line_copy(leftward, k + 1, i, j).start()

    at_an_end = (c == 0) | (c == 3)
    inside = (c == 1) | (c == 2)
    line_start(1, 0)

    swaps = [start(w_ref.at[i, own_rows, :], w_ref.at[i, own_rows, :], W_SWAP + i, partner) for i in range(2)]
    mom = start(dmom_ref.at[other], dmom_in, MOM, partner)
    def weight_copy(q1, q2, number, device):
        block = w_ref.at[m, chip_rows(q1, q2), :]
        return start(block, block, number, device)

    def half_copy(q1, q2, h, number, device):
        block = w_ref.at[m, half_rows(q1, q2, h), :]
        return start(block, block, number, device)

    def second_ring(e):
        q1 = ring(p1, e)
        weight_copy(q1, p2, W_RING2 + e, right2)
        weight_copy(q1, p2, W_RING2 + 4 + e, left2)

    def second_ring_on(e):
        q1 = ring(p1, e)
        arrived(w_ref.at[m, chip_rows(q1, ring(p2, 3)), :], W_RING2 + e)
        half_copy(q1, ring(p2, 3), 0, W_RING2 + 8 + e, right2)
        arrived(w_ref.at[m, chip_rows(q1, ring(p2, 1)), :], W_RING2 + 4 + e)
        half_copy(q1, ring(p2, 1), 1, W_RING2 + 12 + e, left2)
        to_partner(e, 3)
        to_partner(e, 1)

    def to_partner(e, f):
        weight_copy(ring(p1, e), ring(p2, f), W_PART + 4 * e + f, partner)

    for i in range(2):
        swaps[i].wait_recv()
    weight_copy(p1, p2, W_RING1, right1)
    weight_copy(p1, p2, W_RING1 + 1, left1)
    second_ring(0)

    def transposed(b, j):
        first, count = CHUNKS[j]
        for i in range(2):
            for n in range(4):
                tr[i, b * 4 + n, :, first:first + count] = full[i, b, first:first + count, n * 128:(n + 1) * 128].T

    transposed(c, 0)
    arrived(w_ref.at[m, chip_rows(ring(p1, 3), p2), :], W_RING1)
    half_copy(ring(p1, 3), p2, 0, W_RING1 + 2, right1)
    arrived(w_ref.at[m, chip_rows(ring(p1, 1), p2), :], W_RING1 + 1)
    half_copy(ring(p1, 1), p2, 1, W_RING1 + 3, left1)
    second_ring(3)
    second_ring(1)
    to_partner(3, 0)
    to_partner(1, 0)
    second_ring_on(0)
    line_start(1, 1)
    hand_on(1, 0)
    for h in range(2):
        arrived(w_ref.at[m, half_rows(ring(p1, 2), p2, h), :], W_RING1 + 2 + h)
    second_ring(2)
    to_partner(2, 0)
    transposed(c, 1)
    second_ring_on(3)
    second_ring_on(1)
    second_ring_on(2)

    def both_sides(k, j, *work):
        for owner, there in ((c - k, c - k >= 0), (c + k, c + k <= 3)):
            @pl.when(there)
            def _(owner=owner):
                for part in work:
                    part(owner, j)

    hand_on(2, 0)
    both_sides(1, 0, transposed)
    for e in (0, 3, 1, 2):
        for h in range(2):
            arrived(w_ref.at[m, half_rows(ring(p1, e), ring(p2, 2), h), :], W_RING2 + 8 + 4 * h + e)
        to_partner(e, 2)

    def products(b, j, first=False):
        part = pl.ds(pl.multiple_of(b * BLK, BLK), BLK)
        rows = pl.ds(*CHUNKS[j])

        @pl.loop(0, 4)
        def _(n):
            cols = pl.ds(pl.multiple_of(n * 256, 256), 256)
            for i in range(2):
                value = jnp.dot(full[i, b, rows, :], w_ref[i, part, cols], preferred_element_type=F32)
                if first:
                    acc[i, rows, cols] = value
                else:
                    acc[i, rows, cols] += value

    def activate(j):
        rows = pl.ds(*CHUNKS[j])

        @pl.loop(0, 4)
        def _(n):
            cols = pl.ds(pl.multiple_of(n * 256, 256), 256)
            output, slope = gelu_parts(acc[0, rows, cols])
            act[1, rows, cols] = output.astype(BF16)
            act[0, rows, cols] = (acc[1, rows, cols] * slope).astype(BF16)

    def terms(t, j, store):
        rows = pl.ds(*CHUNKS[j])

        @pl.loop(0, 2)
        def _(n):
            inner = pl.ds(pl.multiple_of(n * 256, 256), 256)
            part = pl.ds(pl.multiple_of(t * BLK + n * 256, 256), 256)
            store(inner, lax.dot_general(
                act[0, rows, :], w_ref[0, part, :], (((1,), (1,)), ((), ())), preferred_element_type=F32))

    def back_copy(leftward, k, j):
        rows = pl.ds(*CHUNKS[j])
        number = BACK + (leftward * 3 + k - 1) * 2 + j
        return pltpu.make_async_remote_copy(
            src_ref=back_s.at[leftward, k - 1, rows, :], dst_ref=back_r.at[leftward, k - 1, rows, :],
            send_sem=ss.at[number], recv_sem=rs.at[number],
            device_id={"col": ring(c, 3 if leftward else 1)}, device_id_type=MESH,
        )

    def back_arrived(leftward, k, j):
        arrived(back_r.at[leftward, k, pl.ds(*CHUNKS[j]), :], BACK + (leftward * 3 + k) * 2 + j)

    def back_first(k, j):
        rows = pl.ds(*CHUNKS[j])
        for leftward in (0, 1):
            @pl.when(c == (3 if leftward else 0))
            def _(leftward=leftward):
                def keep(inner, value):
                    back_s[leftward, k - 1, rows, inner] = value.astype(BF16)

                terms(c - k if leftward else c + k, j, keep)
                back_copy(leftward, k, j).start()

    def back_on(k, j):
        rows = pl.ds(*CHUNKS[j])
        for leftward in (0, 1):
            sends = (c < 3) & (c - k >= 0) if leftward else (c > 0) & (c + k <= 3)

            @pl.when(sends)
            def _(leftward=leftward):
                back_arrived(leftward, k, j)

                def keep(inner, value):
                    back_s[leftward, k - 1, rows, inner] = (
                        value + back_r[leftward, k, rows, inner].astype(F32)).astype(BF16)

                terms(c - k if leftward else c + k, j, keep)
                back_copy(leftward, k, j).start()

    hand_on(1, 1)
    for e in range(4):
        for f in range(4):
            if e or f:
                there = pl.ds(pl.multiple_of((ring(p2, e) * t2 + ring(p1, f) * t1) * 128, 128), 128)
                arrived(w_ref.at[other, there, :], W_PART + 4 * e + f)
    products(c, 2, first=True)
    both_sides(1, 1, transposed)
    both_sides(1, 2, products)
    hand_on(2, 1, inside)
    both_sides(2, 0, transposed, products)
    hand_on(3, 0)
    both_sides(3, 0, transposed, products)
    activate(0)
    for k in (3, 2, 1):
        back_first(k, 0)
    hand_on(2, 1, at_an_end)
    both_sides(2, 1, transposed, products)
    hand_on(3, 1)
    both_sides(3, 1, transposed, products)
    activate(1)

    offsets = (2, 1, 3, 0)

    def group_product(matrix, chips, piece, store):
        lhs = jnp.concatenate([tr[matrix, chip] for chip in chips], axis=0)

        @pl.loop(2 * piece, 2 * piece + 2)
        def _(n):
            cols = pl.ds(pl.multiple_of(n * 256, 256), 256)
            store(n, jnp.dot(lhs, act[matrix, :, cols], preferred_element_type=F32))

    core_copies = {}

    def group(piece, g):
        theirs, mine = ring(p2, offsets[g]), ring(p1, offsets[g])

        def keep_sent(n, value):
            g_send[g, n] = value.astype(BF16)

        def keep_own(n, value):
            g_own[g, n] = value

        group_product(other, [theirs * t2 + q * t1 for q in range(4)], piece, keep_sent)
        pair = pl.ds(2 * piece, 2)
        core_copies[piece, g] = start(g_send.at[g, pair], g_recv.at[g, pair], CORE_G + 2 * g + piece, partner)
        group_product(m, [mine * t1 + q * t2 for q in range(4)], piece, keep_own)

    def reduced(dst, parts, rows):
        @pl.loop(0, rows // 128)
        def _(i):
            at = pl.ds(pl.multiple_of(i * 128, 128), 128)
            total = parts[0][at, :].astype(F32)
            for part in parts[1:]:
                total += part[at, :].astype(F32)
            dst[at, :] = total.astype(dst.dtype)

    ring1 = {}

    def chip_sum(g, n):
        return [g_own.at[g, n], g_recv.at[g, n]]

    def ring1_send(piece, g, h, which, device, extra=()):
        n = 2 * piece + h
        reduced(s1.at[g, n], chip_sum(g, n) + list(extra), BLK)
        ring1[piece, which] = start(s1.at[g, n], r1.at[which, piece], STAGE1 + 2 * which + piece, device)

    def first(piece):
        core_copies[piece, 0].wait_recv()
        ring1_send(piece, 0, 0, 0, right1)
        ring1_send(piece, 0, 1, 1, left1)

    def second(piece):
        core_copies[piece, 1].wait_recv()
        ring1_send(piece, 1, 1, 3, right1)
        core_copies[piece, 2].wait_recv()
        ring1_send(piece, 2, 0, 4, left1)

    def third(piece):
        ring1[piece, 0].wait_recv()
        ring1_send(piece, 1, 0, 2, right1, [r1.at[0, piece]])
        ring1[piece, 1].wait_recv()
        ring1_send(piece, 2, 1, 5, left1, [r1.at[1, piece]])

    ring2 = {}
    opp, nxt, prv = ring(p2, 2), ring(p2, 1), ring(p2, 3)

    def block(q, piece, h):
        at = pl.ds(pl.multiple_of(q * 128, 128), 128)
        return [
            ref.at[at, :] for ref in chip_sum(3, 2 * piece + h) + [r1.at[2 + h, piece], r1.at[4 + h, piece]]
        ]

    def ring2_send(piece, g, h, which, device, extra=()):
        n = 2 * piece + h
        reduced(s2.at[g, n], block((opp, nxt, prv)[g], piece, h) + list(extra), 128)
        ring2[piece, which] = start(s2.at[g, n], r2.at[which, piece], STAGE2 + 2 * which + piece, device)

    def ring2_first(piece):
        core_copies[piece, 3].wait_recv()
        for which in (3, 4, 2, 5):
            ring1[piece, which].wait_recv()
        ring2_send(piece, 0, 0, 0, right2)
        ring2_send(piece, 0, 1, 1, left2)
        ring2_send(piece, 1, 1, 3, right2)
        ring2_send(piece, 2, 0, 4, left2)

    def ring2_second(piece):
        ring2[piece, 0].wait_recv()
        ring2_send(piece, 1, 0, 2, right2, [r2.at[0, piece]])
        ring2[piece, 1].wait_recv()
        ring2_send(piece, 2, 1, 5, left2, [r2.at[1, piece]])

    travel = {}

    def dp_first(piece):
        for h, device in ((0, up2), (1, down2)):
            n = 2 * piece + h
            ring2[piece, 2 + h].wait_recv()
            ring2[piece, 4 + h].wait_recv()
            reduced(dp_s.at[n], block(p2, piece, h) + [r2.at[2 + h, piece], r2.at[4 + h, piece]], 128)
            travel[0, n] = start(dp_s.at[n], dp_z.at[n], DP + n, device)

    def dp_second(piece):
        for h, device in ((0, up2), (1, down2)):
            n = 2 * piece + h
            travel[0, n].wait_recv()
            travel[1, n] = start(dp_z.at[n], dp_r.at[n], DP + 4 + n, device)

    def keep_mine(first_row, count):
        def keep(inner, value):
            it_own[first_row:first_row + count, inner] = value
        return keep

    group(0, 0)
    group(0, 1)
    first(0)
    group(0, 2)
    second(0)
    group(1, 0)
    for k in (3, 2, 1):
        back_first(k, 1)
    third(0)
    group(1, 1)
    first(1)
    group(1, 2)
    second(1)
    group(0, 3)
    ring2_first(0)
    group(1, 3)
    third(1)
    ring2_second(0)
    back_on(2, 0)
    for j in range(2):
        terms(c, j, keep_mine(*CHUNKS[j]))
    ring2_first(1)
    dp_first(0)
    back_on(1, 0)
    ring2_second(1)
    back_on(2, 1)
    dp_second(0)
    dp_first(1)
    back_on(1, 1)
    dp_second(1)

    for leftward in (0, 1):
        @pl.when((c < 3) if leftward else (c > 0))
        def _(leftward=leftward):
            for j in range(2):
                back_arrived(leftward, 0, j)
            reduced(it_own, [it_own, back_r.at[leftward, 0]], TOK)

    reduced(ig_s, [it_own], TOK)
    ig_out = pltpu.make_async_copy(ig_s, ig_ref, local.at[4])
    ig_out.start()

    def across_start(place, number, count, device, value):
        place[...] = value
        return [start(place, place, number + k - 1, device(k)) for k in range(1, count + 1)]

    def added(values):
        while len(values) > 1:
            values = [values[i] + values[i + 1] for i in range(0, len(values), 2)]
        return values[0]

    def across_end(copies):
        for copy in copies:
            copy.wait_recv()

    mom.wait_recv()
    lane = lax.broadcasted_iota(jnp.int32, (8, 128), 1)
    old_d = jnp.where((lane // 64) == core, dmom_ref[m], dmom_in[...])[0:1, :]
    old_f = jnp.where(core == 0, in_col_ref[...], out_row_ref[...])
    old_f_sum = jnp.sum(old_f, axis=1, keepdims=True)
    old_d_sum = jnp.sum(old_d, axis=1, keepdims=True)
    col_sums = []
    lanes = None
    for n in range(4):
        travel[1, n].wait_recv()
        grad = dp_s[n].astype(F32) + dp_r[n].astype(F32)
        ratio[n] = grad
        squared = grad * grad
        col_sums.append(jnp.sum(squared, axis=0, keepdims=True))
        folded = squared[:, 0:128] + squared[:, 128:256]
        lanes = folded if n == 0 else lanes + folded
    sub = lax.broadcasted_iota(jnp.int32, (8, 256), 0)
    payload = jnp.where(sub == 4, old_d_sum, 0.0)
    for n in range(4):
        payload = jnp.where(sub == n, col_sums[n], payload)
    sent_xy = across_start(xa.at[chip], SUMS, 15, along_xy, payload)
    row_sums = jnp.sum(lanes.T, axis=0, keepdims=True)
    total = jnp.sum(row_sums, axis=1, keepdims=True)
    sub = lax.broadcasted_iota(jnp.int32, (8, 128), 0)
    sent_z = across_start(za.at[c], SUMS + 15, 3, along_z, jnp.where(sub == 0, row_sums, old_f_sum))
    across_end(sent_z)
    over_z = added([za[i] for i in range(4)])
    d_new = MOMENT_DECAY * old_d + (1.0 - MOMENT_DECAY) * (over_z[0:1, :] / ALL_UNITS + EPSILON_SQ)
    d_column = jnp.broadcast_to(1.0 / jnp.sqrt(d_new), (128, 128)).T[:, 0:1]
    across_end(sent_xy)
    over_xy = added([xa[i] for i in range(16)])
    old_mean = jnp.where(core == 0, over_xy[4:5, 0:1] / WIDTH, over_z[1:2, 0:1] / ALL_UNITS)
    f_new = [
        MOMENT_DECAY * old_f[:, n * 256:(n + 1) * 256]
        + (1.0 - MOMENT_DECAY) * (over_xy[n:n + 1, :] / WIDTH + EPSILON_SQ)
        for n in range(4)
    ]
    lanes = None
    for n in range(4):
        value = ratio[n] * (d_column * (1.0 / jnp.sqrt(f_new[n])))
        ratio[n] = value
        folded = value[:, 0:128] * value[:, 0:128] + value[:, 128:256] * value[:, 128:256]
        lanes = folded if n == 0 else lanes + folded
    folded = lanes[0:8]
    for i in range(1, 16):
        folded += lanes[i * 8:(i + 1) * 8]
    payload = jnp.concatenate([folded, jnp.where(sub == 0, total, old_mean)], axis=0)
    sent_z = across_start(zb.at[core, c], SUMS + 18, 7, along_z_and_cores, payload)

    theirs_at = pl.ds(pl.multiple_of(other * 64, 64), 64)
    swap_v[0] = jnp.zeros((8, UNITS), F32)
    for n in range(4):
        swap_u[0, :, n * 256:(n + 1) * 256] = ratio[n, theirs_at, :]
        swap_v[0, 0:1, n * 256:(n + 1) * 256] = f_new[n]
    swap_v[0, 1:2, 0:128] = d_new
    sent_u = start(swap_u.at[0], swap_u.at[1], SWAP, partner)
    sent_v = start(swap_v.at[0], swap_v.at[1], SWAP + 1, partner)

    across_end(sent_z)
    payload = jnp.stack([added([zb[i, j] for j in range(4)]) for i in range(2)])
    sent_xy = across_start(xb.at[chip], SUMS + 25, 15, along_xy, payload)
    across_end(sent_xy)
    factors = []
    for i in range(2):
        over_all = added([xb[j, i] for j in range(16)])
        mean = MOMENT_DECAY * (over_all[9:10, 0:1] / 64.0) + (1.0 - MOMENT_DECAY) * (
            over_all[8:9, 0:1] / ENTRIES + EPSILON_SQ)
        rms = jnp.sqrt(mean * (jnp.sum(over_all[0:8], keepdims=True) / ENTRIES))
        factors.append(jnp.sqrt(mean) / jnp.maximum(1.0, rms / CLIP_LIMIT))

    def own_lanes(value):
        return jnp.where(core == 0, value[:, 0:64], value[:, 64:128])

    sent_v.wait_recv()
    sent_u.wait_recv()

    def finish(update, row_of, d_out, f_out, which, scale):
        d_out[...] = own_lanes(swap_v[which, 1:2, 0:128])
        f_out[...] = swap_v[which, 0:1, :]
        for n in range(4):
            update[:, n * 256:(n + 1) * 256] = row_of(n) * scale

    def theirs(n):
        return swap_u[1, :, n * 256:(n + 1) * 256]

    @pl.when(core == 0)
    def _():
        finish(in_upd_ref, lambda n: ratio[n, 0:64, :], in_row_out, in_col_out, 0, factors[0])
        finish(out_upd_ref, theirs, out_col_out, out_row_out, 1, factors[1])

    @pl.when(core == 1)
    def _():
        finish(out_upd_ref, lambda n: ratio[n, 64:128, :], out_col_out, out_row_out, 0, factors[1])
        finish(in_upd_ref, theirs, in_row_out, in_col_out, 1, factors[0])

    ig_out.wait()
    for copy in pending:
        copy.wait_send()
    for leftward in (0, 1):
        for k in (1, 2, 3):
            @pl.when(line_sends(leftward, k))
            def _(leftward=leftward, k=k):
                for j in range(2):
                    for i in range(2):
                        line_copy(leftward, k, i, j).wait_send()

            @pl.when((c - k >= 0) if leftward else (c + k <= 3))
            def _(leftward=leftward, k=k):
                for j in range(2):
                    back_copy(leftward, k, j).wait_send()


def fused(*operands):
    vmem = pl.BlockSpec(memory_space=pltpu.VMEM)
    anywhere = pl.BlockSpec(memory_space=pl.ANY)
    return pl.pallas_call(
        kernel,
        out_shape=(
            jax.ShapeDtypeStruct((TOK, BLK), BF16),
            jax.ShapeDtypeStruct((64, UNITS), F32),
            jax.ShapeDtypeStruct((64, UNITS), F32),
            jax.ShapeDtypeStruct((1, 64), F32),
            jax.ShapeDtypeStruct((1, UNITS), F32),
            jax.ShapeDtypeStruct((1, UNITS), F32),
            jax.ShapeDtypeStruct((1, 64), F32),
        ),
        in_specs=[anywhere] * 4 + [vmem] * 4,
        out_specs=(anywhere,) + (vmem,) * 6,
        scratch_shapes=[
            pltpu.VMEM((2, 8, 128), F32),
            pltpu.VMEM((2, 4, TOK, BLK), BF16),
            pltpu.VMEM((2, WIDTH, UNITS), BF16),
            pltpu.VMEM((2, TOK, UNITS), F32),
            pltpu.VMEM((2, 16, 128, TOK), BF16),
            pltpu.VMEM((2, TOK, UNITS), BF16),
            pltpu.VMEM((4, 4, 512, 256), F32),
            pltpu.VMEM((4, 4, 512, 256), BF16),
            pltpu.VMEM((4, 4, 512, 256), BF16),
            pltpu.VMEM((3, 4, 512, 256), BF16),
            pltpu.VMEM((6, 2, 512, 256), BF16),
            pltpu.VMEM((3, 4, 128, 256), BF16),
            pltpu.VMEM((6, 2, 128, 256), BF16),
            pltpu.VMEM((4, 128, 256), BF16),
            pltpu.VMEM((4, 128, 256), BF16),
            pltpu.VMEM((4, 128, 256), BF16),
            pltpu.VMEM((8, 128), F32),
            pltpu.VMEM((4, 8, 128), F32),
            pltpu.VMEM((16, 8, 256), F32),
            pltpu.VMEM((2, 4, 16, 128), F32),
            pltpu.VMEM((16, 2, 16, 128), F32),
            pltpu.VMEM((4, 128, 256), F32),
            pltpu.VMEM((2, 64, UNITS), F32),
            pltpu.VMEM((2, 8, UNITS), F32),
            pltpu.VMEM((2, 3, TOK, BLK), BF16),
            pltpu.VMEM((2, 3, TOK, BLK), BF16),
            pltpu.VMEM((TOK, BLK), F32),
            pltpu.VMEM((TOK, BLK), BF16),
            pltpu.SemaphoreType.DMA((N_SEM,)),
            pltpu.SemaphoreType.DMA((N_SEM,)),
            pltpu.SemaphoreType.DMA((5,)),
        ],
        compiler_params=pltpu.CompilerParams(
            collective_id=0, has_side_effects=True, vmem_limit_bytes=60 * 1024 * 1024
        ),
        cost_estimate=pl.CostEstimate(
            flops=10 * TOK * WIDTH * UNITS, bytes_accessed=16 * 2**20, transcendentals=TOK * UNITS
        ),
    )(*operands)


def handed_out_kernel(*refs):
    count = len(refs) // 2
    for i in range(count):
        refs[count + i][...] = refs[i][...]


def handed_out(*results):
    vmem = pl.BlockSpec(memory_space=pltpu.VMEM)
    return pl.pallas_call(
        handed_out_kernel,
        out_shape=tuple(jax.ShapeDtypeStruct(result.shape, result.dtype) for result in results),
        in_specs=[vmem] * len(results),
        out_specs=(vmem,) * len(results),
        compiler_params=pltpu.CompilerParams(vmem_limit_bytes=60 * 1024 * 1024),
    )(*results)


def per_device(
    saved_input, cotangent, weight_in, weight_out, in_row_moment, in_col_moment, out_row_moment, out_col_moment
):
    input_grad, in_update, out_update_t, in_row, in_col, out_row, out_col = handed_out(*fused(
        saved_input, cotangent, weight_in, weight_out.T, in_row_moment.reshape(1, 64), in_col_moment.reshape(1, UNITS),
        out_row_moment.reshape(1, UNITS), out_col_moment.reshape(1, 64),
    ))
    return (
        input_grad, in_update, out_update_t.T, in_row.reshape(64), in_col.reshape(UNITS), out_row.reshape(UNITS),
        out_col.reshape(64),
    )


def solution(mesh):
    placed = (
        P(("dp", "row"), "col"), P(("dp", "row"), "col"), P("row", "col"), P("col", "row"),
        P("row"), P("col"), P("col"), P("row"),
    )
    return jax.shard_map(
        per_device,
        mesh=mesh,
        in_specs=placed,
        out_specs=(
            P(("dp", "row"), "col"), P("row", "col"), P("col", "row"), P("row"), P("col"), P("col"), P("row"),
        ),
        check_vma=False,
    )
```

```python
import jax
import jax.numpy as jnp
from jax import lax
from jax.experimental import pallas as pl
from jax.experimental.pallas import tpu as pltpu
from jax.sharding import PartitionSpec as P

MESH = pl.DeviceIdType.MESH
F32 = jnp.float32
BF16 = jnp.bfloat16

GELU_SCALE = 0.7978845608028654
GELU_CUBIC = 0.044715
MOMENT_DECAY = 0.8
CLIP_LIMIT = 1.0
EPSILON_SQ = 1e-30

TOK, WIDTH, UNITS, BLK = 384, 2048, 1024, 512
ALL_UNITS = 4096
ENTRIES = WIDTH * ALL_UNITS

CORE_G, STAGE1, STAGE2, DP, SUMS, SWAP, MOM = 0, 8, 20, 32, 40, 80, 82
W_SWAP, W_RING1, W_RING2, W_PART, LINE, BACK = 83, 85, 89, 105, 121, 145
N_SEM = 157
CHUNKS = ((0, 256), (256, 128), (0, 384))


def gelu_parts(values):
    inner = GELU_SCALE * (values + GELU_CUBIC * values * values * values)
    tangent = jnp.tanh(inner)
    output = 0.5 * values * (1.0 + tangent)
    slope = 0.5 * (1.0 + tangent) + 0.5 * values * (1.0 - tangent * tangent) * GELU_SCALE * (
        1.0 + 3.0 * GELU_CUBIC * values * values
    )
    return (output, slope)


def kernel(
    x_ref, cot_ref, win_ref, wout_ref, in_row_hbm, in_col_hbm, out_row_hbm, out_col_hbm,
    ig_ref, in_upd_ref, out_upd_ref, in_row_out, in_col_out, out_row_out, out_col_out,
    in_row_ref, in_col_ref, out_row_ref, out_col_ref, dmom_ref, full, w_ref, acc, tr, act, g_own, g_send, g_recv, s1, r1, s2, r2, dp_s, dp_z, dp_r, dmom_in,
    za, xa, zb, xb, ratio, swap_u, swap_v, back_s, back_r, it_own, ig_s,
    ss, rs, local,
):
    d = lax.axis_index("dp")
    r = lax.axis_index("row")
    c = lax.axis_index("col")
    core = lax.rem(r, 2)
    x = lax.rem(r // 2, 4)
    y = r // 8
    p1 = x + core * (y - x)
    p2 = y + core * (x - y)
    k1, k2 = 2 + 6 * core, 8 - 6 * core
    t1, t2 = 1 + 3 * core, 4 - 3 * core
    m = core
    other = 1 - core

    def ring(position, step):
        return lax.rem(position + step, 4)

    def rowdev(q1, q2):
        return {"row": q1 * k1 + q2 * k2 + core}

    partner = {"row": r + 1 - 2 * core}
    right1, left1 = rowdev(ring(p1, 1), p2), rowdev(ring(p1, 3), p2)
    right2, left2 = rowdev(p1, ring(p2, 1)), rowdev(p1, ring(p2, 3))
    up2 = {"dp": lax.rem(d + c // 2, 2), "col": ring(c, 2)}
    down2 = {"dp": lax.rem(d + 1 - c // 2, 2), "col": ring(c, 2)}

    chip = y * 4 + x

    def along_xy(k):
        return {"row": lax.rem(chip + k, 16) * 2 + core}

    def along_z(k):
        return {"col": ring(c, k)}

    def along_z_and_cores(k):
        place = lax.rem(core * 4 + c + k, 8)
        return {"row": r - core + place // 4, "col": lax.rem(place, 4)}

    barrier = pltpu.get_barrier_semaphore()
    peers = [{"dp": 1 - d, "col": ring(c, 2)}]
    peers += [along_z_and_cores(k) for k in range(1, 8)]
    peers += [along_xy(k) for k in range(1, 16)]
    for peer in peers:
        pl.semaphore_signal(barrier, inc=1, device_id=peer, device_id_type=MESH)

    def chip_rows(q1, q2):
        return pl.ds(pl.multiple_of((q1 * t1 + q2 * t2) * 128, 128), 128)

    def half_rows(q1, q2, h):
        return pl.ds(pl.multiple_of((q1 * t1 + q2 * t2) * 128 + h * 64, 64), 64)

    own_rows = half_rows(p1, p2, core)
    loads = [
        pltpu.make_async_copy(x_ref, full.at[0, c], local.at[0]),
        pltpu.make_async_copy(cot_ref, full.at[1, c], local.at[1]),
        pltpu.make_async_copy(win_ref, w_ref.at[0, own_rows, :], local.at[2]),
        pltpu.make_async_copy(wout_ref, w_ref.at[1, own_rows, :], local.at[3]),
        pltpu.make_async_copy(in_row_hbm, in_row_ref, local.at[5]),
        pltpu.make_async_copy(in_col_hbm, in_col_ref, local.at[6]),
        pltpu.make_async_copy(out_row_hbm, out_row_ref, local.at[7]),
        pltpu.make_async_copy(out_col_hbm, out_col_ref, local.at[8]),
    ]
    for copy in loads:
        copy.start()
    for copy in loads:
        copy.wait()
    for i, ref in enumerate((in_row_ref, out_col_ref)):
        dmom_ref[i] = jnp.broadcast_to(jnp.concatenate([ref[...], ref[...]], axis=1), (8, 128))
    pl.semaphore_wait(barrier, len(peers))

    def send(src, dst, number, device):
        copy = pltpu.make_async_remote_copy(
            src_ref=src, dst_ref=dst, send_sem=ss.at[number], recv_sem=rs.at[number],
            device_id=device, device_id_type=MESH,
        )
        copy.start()
        return copy

    pending = []

    def start(src, dst, number, device):
        copy = send(src, dst, number, device)
        pending.append(copy)
        return copy

    def arrived(dst, number):
        pltpu.make_async_remote_copy(
            src_ref=dst, dst_ref=dst, send_sem=ss.at[number], recv_sem=rs.at[number],
            device_id=partner, device_id_type=MESH,
        ).wait_recv()

    def line_number(leftward, k, i, j):
        return LINE + ((leftward * 3 + k - 1) * 2 + j) * 2 + i

    def line_copy(leftward, k, i, j):
        rows = pl.ds(*CHUNKS[j])
        owner = c + (k - 1) if leftward else c - (k - 1)
        number = line_number(leftward, k, i, j)
        return pltpu.make_async_remote_copy(
            src_ref=full.at[i, owner, rows, :], dst_ref=full.at[i, owner, rows, :], send_sem=ss.at[number], recv_sem=rs.at[number],
            device_id={"col": ring(c, 3 if leftward else 1)}, device_id_type=MESH,
        )

    def line_sends(leftward, k):
        return (c > 0) & (c + (k - 1) <= 3) if leftward else (c < 3) & (c - (k - 1) >= 0)

    def line_gets(leftward, k):
        return c + k <= 3 if leftward else c - k >= 0

    def line_start(k, j):
        for leftward in (0, 1):
            @pl.when(line_sends(leftward, k))
            def _(leftward=leftward):
                for i in range(2):
                    line_copy(leftward, k, i, j).start()

    def hand_on(k, j):
        for i in range(2):
            for leftward in (0, 1):
                @pl.when(line_gets(leftward, k))
                def _(i=i, leftward=leftward):
                    owner = c + k if leftward else c - k
                    arrived(full.at[i, owner, pl.ds(*CHUNKS[j]), :], line_number(leftward, k, i, j))

                if k < 3:
                    @pl.when(line_sends(leftward, k + 1))
                    def _(i=i, leftward=leftward):
                        line_copy(leftward, k + 1, i, j).start()

    line_start(1, 0)

    swaps = [start(w_ref.at[i, own_rows, :], w_ref.at[i, own_rows, :], W_SWAP + i, partner) for i in range(2)]
    mom = start(dmom_ref.at[other], dmom_in, MOM, partner)
    def weight_copy(q1, q2, number, device):
        block = w_ref.at[m, chip_rows(q1, q2), :]
        return start(block, block, number, device)

    def half_copy(q1, q2, h, number, device):
        block = w_ref.at[m, half_rows(q1, q2, h), :]
        return start(block, block, number, device)

    def second_ring(e):
        q1 = ring(p1, e)
        weight_copy(q1, p2, W_RING2 + e, right2)
        weight_copy(q1, p2, W_RING2 + 4 + e, left2)

    def second_ring_on(e):
        q1 = ring(p1, e)
        arrived(w_ref.at[m, chip_rows(q1, ring(p2, 3)), :], W_RING2 + e)
        half_copy(q1, ring(p2, 3), 0, W_RING2 + 8 + e, right2)
        arrived(w_ref.at[m, chip_rows(q1, ring(p2, 1)), :], W_RING2 + 4 + e)
        half_copy(q1, ring(p2, 1), 1, W_RING2 + 12 + e, left2)
        to_partner(e, 3)
        to_partner(e, 1)

    def to_partner(e, f):
        weight_copy(ring(p1, e), ring(p2, f), W_PART + 4 * e + f, partner)

    for i in range(2):
        swaps[i].wait_recv()
    weight_copy(p1, p2, W_RING1, right1)
    weight_copy(p1, p2, W_RING1 + 1, left1)
    second_ring(0)

    def transposed(b, j):
        first, count = CHUNKS[j]
        for i in range(2):
            for n in range(4):
                tr[i, b * 4 + n, :, first:first + count] = full[i, b, first:first + count, n * 128:(n + 1) * 128].T

    transposed(c, 0)
    arrived(w_ref.at[m, chip_rows(ring(p1, 3), p2), :], W_RING1)
    half_copy(ring(p1, 3), p2, 0, W_RING1 + 2, right1)
    arrived(w_ref.at[m, chip_rows(ring(p1, 1), p2), :], W_RING1 + 1)
    half_copy(ring(p1, 1), p2, 1, W_RING1 + 3, left1)
    second_ring(3)
    second_ring(1)
    to_partner(3, 0)
    to_partner(1, 0)
    second_ring_on(0)
    line_start(1, 1)
    hand_on(1, 0)
    for h in range(2):
        arrived(w_ref.at[m, half_rows(ring(p1, 2), p2, h), :], W_RING1 + 2 + h)
    second_ring(2)
    to_partner(2, 0)
    transposed(c, 1)
    second_ring_on(3)
    second_ring_on(1)
    hand_on(1, 1)
    second_ring_on(2)

    def both_sides(k, j, *work):
        for owner, there in ((c - k, c - k >= 0), (c + k, c + k <= 3)):
            @pl.when(there)
            def _(owner=owner):
                for part in work:
                    part(owner, j)

    hand_on(2, 0)
    both_sides(1, 0, transposed)
    for e in (0, 3, 1, 2):
        for h in range(2):
            arrived(w_ref.at[m, half_rows(ring(p1, e), ring(p2, 2), h), :], W_RING2 + 8 + 4 * h + e)
        to_partner(e, 2)
    both_sides(1, 1, transposed)
    both_sides(2, 0, transposed)

    def products(b, j, first=False):
        part = pl.ds(pl.multiple_of(b * BLK, BLK), BLK)
        rows = pl.ds(*CHUNKS[j])

        @pl.loop(0, 4)
        def _(n):
            cols = pl.ds(pl.multiple_of(n * 256, 256), 256)
            for i in range(2):
                value = jnp.dot(full[i, b, rows, :], w_ref[i, part, cols], preferred_element_type=F32)
                if first:
                    acc[i, rows, cols] = value
                else:
                    acc[i, rows, cols] += value

    def activate(j):
        rows = pl.ds(*CHUNKS[j])

        @pl.loop(0, 4)
        def _(n):
            cols = pl.ds(pl.multiple_of(n * 256, 256), 256)
            output, slope = gelu_parts(acc[0, rows, cols])
            act[1, rows, cols] = output.astype(BF16)
            act[0, rows, cols] = (acc[1, rows, cols] * slope).astype(BF16)

    def terms(t, j, store):
        rows = pl.ds(*CHUNKS[j])

        @pl.loop(0, 2)
        def _(n):
            inner = pl.ds(pl.multiple_of(n * 256, 256), 256)
            part = pl.ds(pl.multiple_of(t * BLK + n * 256, 256), 256)
            store(inner, lax.dot_general(
                act[0, rows, :], w_ref[0, part, :], (((1,), (1,)), ((), ())), preferred_element_type=F32))

    def keep_mine(first_row, count):
        def keep(inner, value):
            it_own[first_row:first_row + count, inner] = value
        return keep

    def back_copy(leftward, k, j):
        rows = pl.ds(*CHUNKS[j])
        number = BACK + (leftward * 3 + k - 1) * 2 + j
        return pltpu.make_async_remote_copy(
            src_ref=back_s.at[leftward, k - 1, rows, :], dst_ref=back_r.at[leftward, k - 1, rows, :],
            send_sem=ss.at[number], recv_sem=rs.at[number],
            device_id={"col": ring(c, 3 if leftward else 1)}, device_id_type=MESH,
        )

    def back_arrived(leftward, k, j):
        arrived(back_r.at[leftward, k, pl.ds(*CHUNKS[j]), :], BACK + (leftward * 3 + k) * 2 + j)

    def back_first(k, j):
        rows = pl.ds(*CHUNKS[j])
        for leftward in (0, 1):
            @pl.when(c == (3 if leftward else 0))
            def _(leftward=leftward):
                def keep(inner, value):
                    back_s[leftward, k - 1, rows, inner] = value.astype(BF16)

                terms(c - k if leftward else c + k, j, keep)
                back_copy(leftward, k, j).start()

    def back_on(k, j):
        rows = pl.ds(*CHUNKS[j])
        for leftward in (0, 1):
            sends = (c < 3) & (c - k >= 0) if leftward else (c > 0) & (c + k <= 3)

            @pl.when(sends)
            def _(leftward=leftward):
                back_arrived(leftward, k, j)

                def keep(inner, value):
                    back_s[leftward, k - 1, rows, inner] = (
                        value + back_r[leftward, k, rows, inner].astype(F32)).astype(BF16)

                terms(c - k if leftward else c + k, j, keep)
                back_copy(leftward, k, j).start()

    for e in range(4):
        for f in range(4):
            if e or f:
                there = pl.ds(pl.multiple_of((ring(p2, e) * t2 + ring(p1, f) * t1) * 128, 128), 128)
                arrived(w_ref.at[other, there, :], W_PART + 4 * e + f)
    products(c, 2, first=True)
    hand_on(2, 1)
    both_sides(1, 2, products)
    both_sides(2, 1, transposed)
    both_sides(2, 2, products)
    hand_on(3, 0)
    both_sides(3, 0, products)
    activate(0)
    for k in (3, 2, 1):
        back_first(k, 0)
    both_sides(3, 0, transposed)
    hand_on(3, 1)
    both_sides(3, 1, products)
    activate(1)
    both_sides(3, 1, transposed)

    offsets = (2, 1, 3, 0)

    def group_product(matrix, chips, piece, store):
        lhs = jnp.concatenate([tr[matrix, chip] for chip in chips], axis=0)

        @pl.loop(2 * piece, 2 * piece + 2)
        def _(n):
            cols = pl.ds(pl.multiple_of(n * 256, 256), 256)
            store(n, jnp.dot(lhs, act[matrix, :, cols], preferred_element_type=F32))

    core_copies = {}

    def group_theirs(piece, g):
        theirs = ring(p2, offsets[g])

        def keep_sent(n, value):
            g_send[g, n] = value.astype(BF16)

        group_product(other, [theirs * t2 + q * t1 for q in range(4)], piece, keep_sent)
        pair = pl.ds(2 * piece, 2)
        core_copies[piece, g] = start(g_send.at[g, pair], g_recv.at[g, pair], CORE_G + 2 * g + piece, partner)

    def group_own(piece, g):
        mine = ring(p1, offsets[g])

        def keep_own(n, value):
            g_own[g, n] = value

        group_product(m, [mine * t1 + q * t2 for q in range(4)], piece, keep_own)

    def reduced(dst, parts, rows):
        @pl.loop(0, rows // 128)
        def _(i):
            at = pl.ds(pl.multiple_of(i * 128, 128), 128)
            total = parts[0][at, :].astype(F32)
            for part in parts[1:]:
                total += part[at, :].astype(F32)
            dst[at, :] = total.astype(dst.dtype)

    ring1 = {}

    def chip_sum(g, n):
        return [g_own.at[g, n], g_recv.at[g, n]]

    def ring1_send(piece, g, h, which, device, extra=()):
        n = 2 * piece + h
        reduced(s1.at[g, n], chip_sum(g, n) + list(extra), BLK)
        ring1[piece, which] = start(s1.at[g, n], r1.at[which, piece], STAGE1 + 2 * which + piece, device)

    def first(piece):
        core_copies[piece, 0].wait_recv()
        ring1_send(piece, 0, 0, 0, right1)
        ring1_send(piece, 0, 1, 1, left1)

    def second(piece):
        core_copies[piece, 1].wait_recv()
        ring1_send(piece, 1, 1, 3, right1)
        core_copies[piece, 2].wait_recv()
        ring1_send(piece, 2, 0, 4, left1)

    def third(piece):
        ring1[piece, 0].wait_recv()
        ring1_send(piece, 1, 0, 2, right1, [r1.at[0, piece]])
        ring1[piece, 1].wait_recv()
        ring1_send(piece, 2, 1, 5, left1, [r1.at[1, piece]])

    ring2 = {}
    opp, nxt, prv = ring(p2, 2), ring(p2, 1), ring(p2, 3)

    def block(q, piece, h):
        at = pl.ds(pl.multiple_of(q * 128, 128), 128)
        return [
            ref.at[at, :] for ref in chip_sum(3, 2 * piece + h) + [r1.at[2 + h, piece], r1.at[4 + h, piece]]
        ]

    def ring2_send(piece, g, h, which, device, extra=()):
        n = 2 * piece + h
        reduced(s2.at[g, n], block((opp, nxt, prv)[g], piece, h) + list(extra), 128)
        ring2[piece, which] = start(s2.at[g, n], r2.at[which, piece], STAGE2 + 2 * which + piece, device)

    def ring2_first(piece):
        core_copies[piece, 3].wait_recv()
        for which in (3, 4, 2, 5):
            ring1[piece, which].wait_recv()
        ring2_send(piece, 0, 0, 0, right2)
        ring2_send(piece, 0, 1, 1, left2)
        ring2_send(piece, 1, 1, 3, right2)
        ring2_send(piece, 2, 0, 4, left2)

    def ring2_second(piece):
        ring2[piece, 0].wait_recv()
        ring2_send(piece, 1, 0, 2, right2, [r2.at[0, piece]])
        ring2[piece, 1].wait_recv()
        ring2_send(piece, 2, 1, 5, left2, [r2.at[1, piece]])

    travel = {}

    def dp_first(piece):
        for h, device in ((0, up2), (1, down2)):
            n = 2 * piece + h
            ring2[piece, 2 + h].wait_recv()
            ring2[piece, 4 + h].wait_recv()
            reduced(dp_s.at[n], block(p2, piece, h) + [r2.at[2 + h, piece], r2.at[4 + h, piece]], 128)
            travel[0, n] = start(dp_s.at[n], dp_z.at[n], DP + n, device)

    def dp_second(piece):
        for h, device in ((0, up2), (1, down2)):
            n = 2 * piece + h
            travel[0, n].wait_recv()
            travel[1, n] = start(dp_z.at[n], dp_r.at[n], DP + 4 + n, device)

    group_theirs(0, 0)
    group_theirs(0, 1)
    group_own(0, 0)
    group_theirs(0, 2)
    group_own(0, 1)
    group_own(0, 2)
    first(0)
    second(0)
    group_theirs(1, 0)
    group_own(1, 0)
    for k in (3, 2, 1):
        back_first(k, 1)
    third(0)
    group_theirs(1, 1)
    group_own(1, 1)
    first(1)
    group_theirs(1, 2)
    group_own(1, 2)
    second(1)
    group_theirs(0, 3)
    group_own(0, 3)
    ring2_first(0)
    group_theirs(1, 3)
    group_own(1, 3)
    third(1)
    ring2_second(0)
    back_on(2, 0)
    terms(c, 2, keep_mine(*CHUNKS[2]))
    dp_first(0)
    ring2_first(1)
    back_on(1, 0)
    ring2_second(1)
    back_on(2, 1)
    dp_second(0)
    dp_first(1)
    back_on(1, 1)
    dp_second(1)

    for leftward in (0, 1):
        @pl.when((c < 3) if leftward else (c > 0))
        def _(leftward=leftward):
            for j in range(2):
                back_arrived(leftward, 0, j)
            reduced(it_own, [it_own, back_r.at[leftward, 0]], TOK)

    reduced(ig_s, [it_own], TOK)
    ig_out = pltpu.make_async_copy(ig_s, ig_ref, local.at[4])
    ig_out.start()

    def across_start(place, number, count, device, value):
        place[...] = value
        return [start(place, place, number + k - 1, device(k)) for k in range(1, count + 1)]

    def added(values):
        while len(values) > 1:
            values = [values[i] + values[i + 1] for i in range(0, len(values), 2)]
        return values[0]

    def across_end(copies):
        for copy in copies:
            copy.wait_recv()

    mom.wait_recv()
    lane = lax.broadcasted_iota(jnp.int32, (8, 128), 1)
    old_d = jnp.where((lane // 64) == core, dmom_ref[m], dmom_in[...])[0:1, :]
    old_f = jnp.where(core == 0, in_col_ref[...], out_row_ref[...])
    old_f_sum = jnp.sum(old_f, axis=1, keepdims=True)
    old_d_sum = jnp.sum(old_d, axis=1, keepdims=True)
    col_sums = []
    lanes = None
    for n in range(4):
        travel[1, n].wait_recv()
        grad = dp_s[n].astype(F32) + dp_r[n].astype(F32)
        ratio[n] = grad
        squared = grad * grad
        col_sums.append(jnp.sum(squared, axis=0, keepdims=True))
        folded = squared[:, 0:128] + squared[:, 128:256]
        lanes = folded if n == 0 else lanes + folded
    sub = lax.broadcasted_iota(jnp.int32, (8, 256), 0)
    payload = jnp.where(sub == 4, old_d_sum, 0.0)
    for n in range(4):
        payload = jnp.where(sub == n, col_sums[n], payload)
    sent_xy = across_start(xa.at[chip], SUMS, 15, along_xy, payload)
    row_sums = jnp.sum(lanes.T, axis=0, keepdims=True)
    total = jnp.sum(row_sums, axis=1, keepdims=True)
    sub = lax.broadcasted_iota(jnp.int32, (8, 128), 0)
    sent_z = across_start(za.at[c], SUMS + 15, 3, along_z, jnp.where(sub == 0, row_sums, old_f_sum))
    across_end(sent_z)
    over_z = added([za[i] for i in range(4)])
    d_new = MOMENT_DECAY * old_d + (1.0 - MOMENT_DECAY) * (over_z[0:1, :] / ALL_UNITS + EPSILON_SQ)
    d_column = jnp.broadcast_to(1.0 / jnp.sqrt(d_new), (128, 128)).T[:, 0:1]
    across_end(sent_xy)
    over_xy = added([xa[i] for i in range(16)])
    old_mean = jnp.where(core == 0, over_xy[4:5, 0:1] / WIDTH, over_z[1:2, 0:1] / ALL_UNITS)
    f_new = [
        MOMENT_DECAY * old_f[:, n * 256:(n + 1) * 256]
        + (1.0 - MOMENT_DECAY) * (over_xy[n:n + 1, :] / WIDTH + EPSILON_SQ)
        for n in range(4)
    ]
    lanes = None
    for n in range(4):
        value = ratio[n] * (d_column * (1.0 / jnp.sqrt(f_new[n])))
        ratio[n] = value
        folded = value[:, 0:128] * value[:, 0:128] + value[:, 128:256] * value[:, 128:256]
        lanes = folded if n == 0 else lanes + folded
    folded = lanes[0:8]
    for i in range(1, 16):
        folded += lanes[i * 8:(i + 1) * 8]
    payload = jnp.concatenate([folded, jnp.where(sub == 0, total, old_mean)], axis=0)
    sent_z = across_start(zb.at[core, c], SUMS + 18, 7, along_z_and_cores, payload)

    theirs_at = pl.ds(pl.multiple_of(other * 64, 64), 64)
    swap_v[0] = jnp.zeros((8, UNITS), F32)
    for n in range(4):
        swap_u[0, :, n * 256:(n + 1) * 256] = ratio[n, theirs_at, :]
        swap_v[0, 0:1, n * 256:(n + 1) * 256] = f_new[n]
    swap_v[0, 1:2, 0:128] = d_new
    sent_u = start(swap_u.at[0], swap_u.at[1], SWAP, partner)
    sent_v = start(swap_v.at[0], swap_v.at[1], SWAP + 1, partner)

    across_end(sent_z)
    payload = jnp.stack([added([zb[i, j] for j in range(4)]) for i in range(2)])
    sent_xy = across_start(xb.at[chip], SUMS + 25, 15, along_xy, payload)
    across_end(sent_xy)
    factors = []
    for i in range(2):
        over_all = added([xb[j, i] for j in range(16)])
        mean = MOMENT_DECAY * (over_all[9:10, 0:1] / 64.0) + (1.0 - MOMENT_DECAY) * (
            over_all[8:9, 0:1] / ENTRIES + EPSILON_SQ)
        rms = jnp.sqrt(mean * (jnp.sum(over_all[0:8], keepdims=True) / ENTRIES))
        factors.append(jnp.sqrt(mean) / jnp.maximum(1.0, rms / CLIP_LIMIT))

    def own_lanes(value):
        return jnp.where(core == 0, value[:, 0:64], value[:, 64:128])

    sent_v.wait_recv()
    sent_u.wait_recv()

    def finish(update, row_of, d_out, f_out, which, scale):
        d_out[...] = own_lanes(swap_v[which, 1:2, 0:128])
        f_out[...] = swap_v[which, 0:1, :]
        for n in range(4):
            update[:, n * 256:(n + 1) * 256] = row_of(n) * scale

    def theirs(n):
        return swap_u[1, :, n * 256:(n + 1) * 256]

    @pl.when(core == 0)
    def _():
        finish(in_upd_ref, lambda n: ratio[n, 0:64, :], in_row_out, in_col_out, 0, factors[0])
        finish(out_upd_ref, theirs, out_col_out, out_row_out, 1, factors[1])

    @pl.when(core == 1)
    def _():
        finish(out_upd_ref, lambda n: ratio[n, 64:128, :], out_col_out, out_row_out, 0, factors[1])
        finish(in_upd_ref, theirs, in_row_out, in_col_out, 1, factors[0])

    ig_out.wait()
    for copy in pending:
        copy.wait_send()
    for leftward in (0, 1):
        for k in (1, 2, 3):
            @pl.when(line_sends(leftward, k))
            def _(leftward=leftward, k=k):
                for j in range(2):
                    for i in range(2):
                        line_copy(leftward, k, i, j).wait_send()

            @pl.when((c - k >= 0) if leftward else (c + k <= 3))
            def _(leftward=leftward, k=k):
                for j in range(2):
                    back_copy(leftward, k, j).wait_send()


def fused(*operands):
    vmem = pl.BlockSpec(memory_space=pltpu.VMEM)
    anywhere = pl.BlockSpec(memory_space=pl.ANY)
    return pl.pallas_call(
        kernel,
        out_shape=(
            jax.ShapeDtypeStruct((TOK, BLK), BF16),
            jax.ShapeDtypeStruct((64, UNITS), F32),
            jax.ShapeDtypeStruct((64, UNITS), F32),
            jax.ShapeDtypeStruct((1, 64), F32),
            jax.ShapeDtypeStruct((1, UNITS), F32),
            jax.ShapeDtypeStruct((1, UNITS), F32),
            jax.ShapeDtypeStruct((1, 64), F32),
        ),
        in_specs=[anywhere] * 8,
        out_specs=(anywhere,) + (vmem,) * 6,
        scratch_shapes=[
            pltpu.VMEM((1, 64), F32),
            pltpu.VMEM((1, UNITS), F32),
            pltpu.VMEM((1, UNITS), F32),
            pltpu.VMEM((1, 64), F32),
            pltpu.VMEM((2, 8, 128), F32),
            pltpu.VMEM((2, 4, TOK, BLK), BF16),
            pltpu.VMEM((2, WIDTH, UNITS), BF16),
            pltpu.VMEM((2, TOK, UNITS), F32),
            pltpu.VMEM((2, 16, 128, TOK), BF16),
            pltpu.VMEM((2, TOK, UNITS), BF16),
            pltpu.VMEM((4, 4, 512, 256), F32),
            pltpu.VMEM((4, 4, 512, 256), BF16),
            pltpu.VMEM((4, 4, 512, 256), BF16),
            pltpu.VMEM((3, 4, 512, 256), BF16),
            pltpu.VMEM((6, 2, 512, 256), BF16),
            pltpu.VMEM((3, 4, 128, 256), BF16),
            pltpu.VMEM((6, 2, 128, 256), BF16),
            pltpu.VMEM((4, 128, 256), BF16),
            pltpu.VMEM((4, 128, 256), BF16),
            pltpu.VMEM((4, 128, 256), BF16),
            pltpu.VMEM((8, 128), F32),
            pltpu.VMEM((4, 8, 128), F32),
            pltpu.VMEM((16, 8, 256), F32),
            pltpu.VMEM((2, 4, 16, 128), F32),
            pltpu.VMEM((16, 2, 16, 128), F32),
            pltpu.VMEM((4, 128, 256), F32),
            pltpu.VMEM((2, 64, UNITS), F32),
            pltpu.VMEM((2, 8, UNITS), F32),
            pltpu.VMEM((2, 3, TOK, BLK), BF16),
            pltpu.VMEM((2, 3, TOK, BLK), BF16),
            pltpu.VMEM((TOK, BLK), F32),
            pltpu.VMEM((TOK, BLK), BF16),
            pltpu.SemaphoreType.DMA((N_SEM,)),
            pltpu.SemaphoreType.DMA((N_SEM,)),
            pltpu.SemaphoreType.DMA((9,)),
        ],
        compiler_params=pltpu.CompilerParams(
            collective_id=0, has_side_effects=True, vmem_limit_bytes=60 * 1024 * 1024
        ),
        cost_estimate=pl.CostEstimate(
            flops=10 * TOK * WIDTH * UNITS, bytes_accessed=16 * 2**20, transcendentals=TOK * UNITS
        ),
    )(*operands)


def handed_out_kernel(*refs):
    count = len(refs) // 2
    for i in range(count):
        refs[count + i][...] = refs[i][...]


def handed_out(*results):
    vmem = pl.BlockSpec(memory_space=pltpu.VMEM)
    return pl.pallas_call(
        handed_out_kernel,
        out_shape=tuple(jax.ShapeDtypeStruct(result.shape, result.dtype) for result in results),
        in_specs=[vmem] * len(results),
        out_specs=(vmem,) * len(results),
        compiler_params=pltpu.CompilerParams(vmem_limit_bytes=60 * 1024 * 1024),
    )(*results)


def per_device(
    saved_input, cotangent, weight_in, weight_out, in_row_moment, in_col_moment, out_row_moment, out_col_moment
):
    input_grad, in_update, out_update_t, in_row, in_col, out_row, out_col = handed_out(*fused(
        saved_input, cotangent, weight_in, weight_out.T, in_row_moment.reshape(1, 64), in_col_moment.reshape(1, UNITS),
        out_row_moment.reshape(1, UNITS), out_col_moment.reshape(1, 64),
    ))
    return (
        input_grad, in_update, out_update_t.T, in_row.reshape(64), in_col.reshape(UNITS), out_row.reshape(UNITS),
        out_col.reshape(64),
    )


def solution(mesh):
    placed = (
        P(("dp", "row"), "col"), P(("dp", "row"), "col"), P("row", "col"), P("col", "row"),
        P("row"), P("col"), P("col"), P("row"),
    )
    return jax.shard_map(
        per_device,
        mesh=mesh,
        in_specs=placed,
        out_specs=(
            P(("dp", "row"), "col"), P("row", "col"), P("col", "row"), P("row"), P("col"), P("col"), P("row"),
        ),
        check_vma=False,
    )
```

```python
import jax
import jax.numpy as jnp
from jax import lax
from jax.experimental import pallas as pl
from jax.experimental.pallas import tpu as pltpu
from jax.sharding import PartitionSpec as P

MESH = pl.DeviceIdType.MESH
F32 = jnp.float32
BF16 = jnp.bfloat16

GELU_SCALE = 0.7978845608028654
GELU_CUBIC = 0.044715
MOMENT_DECAY = 0.8
CLIP_LIMIT = 1.0
EPSILON_SQ = 1e-30

TOK, WIDTH, UNITS, BLK = 384, 2048, 1024, 512
ALL_UNITS = 4096
ENTRIES = WIDTH * ALL_UNITS

CORE_G, STAGE1, STAGE2, DP, SUMS, SWAP, MOM = 0, 8, 20, 32, 40, 80, 82
W_SWAP, W_RING1, W_RING2, W_PART, LINE, BACK = 83, 85, 89, 105, 121, 145
N_SEM = 157
CHUNKS = ((0, 256), (256, 128), (0, 384))


def gelu_parts(values):
    inner = GELU_SCALE * (values + GELU_CUBIC * values * values * values)
    tangent = jnp.tanh(inner)
    output = 0.5 * values * (1.0 + tangent)
    slope = 0.5 * (1.0 + tangent) + 0.5 * values * (1.0 - tangent * tangent) * GELU_SCALE * (
        1.0 + 3.0 * GELU_CUBIC * values * values
    )
    return (output, slope)


def kernel(
    x_ref, cot_ref, win_ref, wout_ref, in_row_hbm, in_col_hbm, out_row_hbm, out_col_hbm,
    ig_ref, in_upd_ref, out_upd_ref, in_row_out, in_col_out, out_row_out, out_col_out,
    in_row_ref, in_col_ref, out_row_ref, out_col_ref, dmom_ref, full, w_ref, acc, tr, act, g_own, g_send, g_recv, s1, r1, s2, r2, dp_s, dp_z, dp_r, dmom_in,
    za, xa, zb, xb, ratio, swap_u, swap_v, back_s, back_r, it_own, ig_s,
    ss, rs, local,
):
    d = lax.axis_index("dp")
    r = lax.axis_index("row")
    c = lax.axis_index("col")
    core = lax.rem(r, 2)
    x = lax.rem(r // 2, 4)
    y = r // 8
    p1 = x + core * (y - x)
    p2 = y + core * (x - y)
    k1, k2 = 2 + 6 * core, 8 - 6 * core
    t1, t2 = 1 + 3 * core, 4 - 3 * core
    m = core
    other = 1 - core

    def ring(position, step):
        return lax.rem(position + step, 4)

    def rowdev(q1, q2):
        return {"row": q1 * k1 + q2 * k2 + core}

    partner = {"row": r + 1 - 2 * core}
    right1, left1 = rowdev(ring(p1, 1), p2), rowdev(ring(p1, 3), p2)
    right2, left2 = rowdev(p1, ring(p2, 1)), rowdev(p1, ring(p2, 3))
    up2 = {"dp": lax.rem(d + c // 2, 2), "col": ring(c, 2)}
    down2 = {"dp": lax.rem(d + 1 - c // 2, 2), "col": ring(c, 2)}

    chip = y * 4 + x

    def along_xy(k):
        return {"row": lax.rem(chip + k, 16) * 2 + core}

    def along_z(k):
        return {"col": ring(c, k)}

    def along_z_and_cores(k):
        place = lax.rem(core * 4 + c + k, 8)
        return {"row": r - core + place // 4, "col": lax.rem(place, 4)}

    barrier = pltpu.get_barrier_semaphore()
    peers = [{"dp": 1 - d, "col": ring(c, 2)}]
    peers += [along_z_and_cores(k) for k in range(1, 8)]
    peers += [along_xy(k) for k in range(1, 16)]
    for peer in peers:
        pl.semaphore_signal(barrier, inc=1, device_id=peer, device_id_type=MESH)

    def chip_rows(q1, q2):
        return pl.ds(pl.multiple_of((q1 * t1 + q2 * t2) * 128, 128), 128)

    def half_rows(q1, q2, h):
        return pl.ds(pl.multiple_of((q1 * t1 + q2 * t2) * 128 + h * 64, 64), 64)

    own_rows = half_rows(p1, p2, core)
    loads = [
        pltpu.make_async_copy(x_ref, full.at[0, c], local.at[0]),
        pltpu.make_async_copy(cot_ref, full.at[1, c], local.at[1]),
        pltpu.make_async_copy(win_ref, w_ref.at[0, own_rows, :], local.at[2]),
        pltpu.make_async_copy(wout_ref, w_ref.at[1, own_rows, :], local.at[3]),
        pltpu.make_async_copy(in_row_hbm, in_row_ref, local.at[5]),
        pltpu.make_async_copy(in_col_hbm, in_col_ref, local.at[6]),
        pltpu.make_async_copy(out_row_hbm, out_row_ref, local.at[7]),
        pltpu.make_async_copy(out_col_hbm, out_col_ref, local.at[8]),
    ]
    for copy in loads:
        copy.start()
    for copy in loads:
        copy.wait()
    for i, ref in enumerate((in_row_ref, out_col_ref)):
        dmom_ref[i] = jnp.broadcast_to(jnp.concatenate([ref[...], ref[...]], axis=1), (8, 128))
    pl.semaphore_wait(barrier, len(peers))

    def send(src, dst, number, device):
        copy = pltpu.make_async_remote_copy(
            src_ref=src, dst_ref=dst, send_sem=ss.at[number], recv_sem=rs.at[number],
            device_id=device, device_id_type=MESH,
        )
        copy.start()
        return copy

    pending = []

    def start(src, dst, number, device):
        copy = send(src, dst, number, device)
        pending.append(copy)
        return copy

    def arrived(dst, number):
        pltpu.make_async_remote_copy(
            src_ref=dst, dst_ref=dst, send_sem=ss.at[number], recv_sem=rs.at[number],
            device_id=partner, device_id_type=MESH,
        ).wait_recv()

    def line_number(leftward, k, i, j):
        return LINE + ((leftward * 3 + k - 1) * 2 + j) * 2 + i

    def line_copy(leftward, k, i, j):
        rows = pl.ds(*CHUNKS[j])
        owner = c + (k - 1) if leftward else c - (k - 1)
        number = line_number(leftward, k, i, j)
        return pltpu.make_async_remote_copy(
            src_ref=full.at[i, owner, rows, :], dst_ref=full.at[i, owner, rows, :], send_sem=ss.at[number], recv_sem=rs.at[number],
            device_id={"col": ring(c, 3 if leftward else 1)}, device_id_type=MESH,
        )

    def line_sends(leftward, k):
        return (c > 0) & (c + (k - 1) <= 3) if leftward else (c < 3) & (c - (k - 1) >= 0)

    def line_gets(leftward, k):
        return c + k <= 3 if leftward else c - k >= 0

    def line_start(k, j):
        for leftward in (0, 1):
            @pl.when(line_sends(leftward, k))
            def _(leftward=leftward):
                for i in range(2):
                    line_copy(leftward, k, i, j).start()

    def hand_on(k, j):
        for i in range(2):
            for leftward in (0, 1):
                @pl.when(line_gets(leftward, k))
                def _(i=i, leftward=leftward):
                    owner = c + k if leftward else c - k
                    arrived(full.at[i, owner, pl.ds(*CHUNKS[j]), :], line_number(leftward, k, i, j))

                if k < 3:
                    @pl.when(line_sends(leftward, k + 1))
                    def _(i=i, leftward=leftward):
                        line_copy(leftward, k + 1, i, j).start()

    line_start(1, 0)

    swaps = [start(w_ref.at[i, own_rows, :], w_ref.at[i, own_rows, :], W_SWAP + i, partner) for i in range(2)]
    mom = start(dmom_ref.at[other], dmom_in, MOM, partner)
    def weight_copy(q1, q2, number, device):
        block = w_ref.at[m, chip_rows(q1, q2), :]
        return start(block, block, number, device)

    def half_copy(q1, q2, h, number, device):
        block = w_ref.at[m, half_rows(q1, q2, h), :]
        return start(block, block, number, device)

    def second_ring(e):
        q1 = ring(p1, e)
        weight_copy(q1, p2, W_RING2 + e, right2)
        weight_copy(q1, p2, W_RING2 + 4 + e, left2)

    def second_ring_on(e):
        q1 = ring(p1, e)
        arrived(w_ref.at[m, chip_rows(q1, ring(p2, 3)), :], W_RING2 + e)
        half_copy(q1, ring(p2, 3), 0, W_RING2 + 8 + e, right2)
        arrived(w_ref.at[m, chip_rows(q1, ring(p2, 1)), :], W_RING2 + 4 + e)
        half_copy(q1, ring(p2, 1), 1, W_RING2 + 12 + e, left2)
        to_partner(e, 3)
        to_partner(e, 1)

    def to_partner(e, f):
        weight_copy(ring(p1, e), ring(p2, f), W_PART + 4 * e + f, partner)

    for i in range(2):
        swaps[i].wait_recv()
    weight_copy(p1, p2, W_RING1, right1)
    weight_copy(p1, p2, W_RING1 + 1, left1)
    second_ring(0)

    def transposed(b, j):
        first, count = CHUNKS[j]
        for i in range(2):
            for n in range(4):
                tr[i, b * 4 + n, :, first:first + count] = full[i, b, first:first + count, n * 128:(n + 1) * 128].T

    transposed(c, 0)
    arrived(w_ref.at[m, chip_rows(ring(p1, 3), p2), :], W_RING1)
    half_copy(ring(p1, 3), p2, 0, W_RING1 + 2, right1)
    arrived(w_ref.at[m, chip_rows(ring(p1, 1), p2), :], W_RING1 + 1)
    half_copy(ring(p1, 1), p2, 1, W_RING1 + 3, left1)
    second_ring(3)
    second_ring(1)
    to_partner(3, 0)
    to_partner(1, 0)
    second_ring_on(0)
    line_start(1, 1)
    hand_on(1, 0)
    for h in range(2):
        arrived(w_ref.at[m, half_rows(ring(p1, 2), p2, h), :], W_RING1 + 2 + h)
    second_ring(2)
    to_partner(2, 0)
    transposed(c, 1)
    second_ring_on(3)
    second_ring_on(1)
    hand_on(1, 1)
    second_ring_on(2)

    def both_sides(k, j, *work):
        for owner, there in ((c - k, c - k >= 0), (c + k, c + k <= 3)):
            @pl.when(there)
            def _(owner=owner):
                for part in work:
                    part(owner, j)

    hand_on(2, 0)
    both_sides(1, 0, transposed)
    for e in (0, 3, 1, 2):
        for h in range(2):
            arrived(w_ref.at[m, half_rows(ring(p1, e), ring(p2, 2), h), :], W_RING2 + 8 + 4 * h + e)
        to_partner(e, 2)
    both_sides(1, 1, transposed)
    both_sides(2, 0, transposed)

    def products(b, j, first=False):
        part = pl.ds(pl.multiple_of(b * BLK, BLK), BLK)
        rows = pl.ds(*CHUNKS[j])

        @pl.loop(0, 4, unroll=2)
        def _(n):
            cols = pl.ds(pl.multiple_of(n * 256, 256), 256)
            for i in range(2):
                value = jnp.dot(full[i, b, rows, :], w_ref[i, part, cols], preferred_element_type=F32)
                if first:
                    acc[i, rows, cols] = value
                else:
                    acc[i, rows, cols] += value

    def activate(j):
        rows = pl.ds(*CHUNKS[j])

        @pl.loop(0, 4)
        def _(n):
            cols = pl.ds(pl.multiple_of(n * 256, 256), 256)
            output, slope = gelu_parts(acc[0, rows, cols])
            act[1, rows, cols] = output.astype(BF16)
            act[0, rows, cols] = (acc[1, rows, cols] * slope).astype(BF16)

    def terms(t, j, store):
        rows = pl.ds(*CHUNKS[j])

        @pl.loop(0, 2, unroll=True)
        def _(n):
            inner = pl.ds(pl.multiple_of(n * 256, 256), 256)
            part = pl.ds(pl.multiple_of(t * BLK + n * 256, 256), 256)
            store(inner, lax.dot_general(
                act[0, rows, :], w_ref[0, part, :], (((1,), (1,)), ((), ())), preferred_element_type=F32))

    def keep_mine(first_row, count):
        def keep(inner, value):
            it_own[first_row:first_row + count, inner] = value
        return keep

    def back_copy(leftward, k, j):
        rows = pl.ds(*CHUNKS[j])
        number = BACK + (leftward * 3 + k - 1) * 2 + j
        return pltpu.make_async_remote_copy(
            src_ref=back_s.at[leftward, k - 1, rows, :], dst_ref=back_r.at[leftward, k - 1, rows, :],
            send_sem=ss.at[number], recv_sem=rs.at[number],
            device_id={"col": ring(c, 3 if leftward else 1)}, device_id_type=MESH,
        )

    def back_arrived(leftward, k, j):
        arrived(back_r.at[leftward, k, pl.ds(*CHUNKS[j]), :], BACK + (leftward * 3 + k) * 2 + j)

    def back_first(k, j):
        rows = pl.ds(*CHUNKS[j])
        for leftward in (0, 1):
            @pl.when(c == (3 if leftward else 0))
            def _(leftward=leftward):
                def keep(inner, value):
                    back_s[leftward, k - 1, rows, inner] = value.astype(BF16)

                terms(c - k if leftward else c + k, j, keep)
                back_copy(leftward, k, j).start()

    def back_on(k, j):
        rows = pl.ds(*CHUNKS[j])
        for leftward in (0, 1):
            sends = (c < 3) & (c - k >= 0) if leftward else (c > 0) & (c + k <= 3)

            @pl.when(sends)
            def _(leftward=leftward):
                back_arrived(leftward, k, j)

                def keep(inner, value):
                    back_s[leftward, k - 1, rows, inner] = (
                        value + back_r[leftward, k, rows, inner].astype(F32)).astype(BF16)

                terms(c - k if leftward else c + k, j, keep)
                back_copy(leftward, k, j).start()

    for e in range(4):
        for f in range(4):
            if e or f:
                there = pl.ds(pl.multiple_of((ring(p2, e) * t2 + ring(p1, f) * t1) * 128, 128), 128)
                arrived(w_ref.at[other, there, :], W_PART + 4 * e + f)
    products(c, 2, first=True)
    hand_on(2, 1)
    both_sides(1, 2, products)
    both_sides(2, 1, transposed)
    both_sides(2, 2, products)
    hand_on(3, 0)
    both_sides(3, 0, products)
    activate(0)
    for k in (3, 2, 1):
        back_first(k, 0)
    both_sides(3, 0, transposed)
    hand_on(3, 1)
    both_sides(3, 1, products)
    activate(1)
    both_sides(3, 1, transposed)

    offsets = (2, 1, 3, 0)

    def group_product(matrix, chips, piece, store):
        lhs = jnp.concatenate([tr[matrix, chip] for chip in chips], axis=0)

        @pl.loop(2 * piece, 2 * piece + 2, unroll=True)
        def _(n):
            cols = pl.ds(pl.multiple_of(n * 256, 256), 256)
            store(n, jnp.dot(lhs, act[matrix, :, cols], preferred_element_type=F32))

    core_copies = {}

    def group_theirs(piece, g):
        theirs = ring(p2, offsets[g])

        def keep_sent(n, value):
            g_send[g, n] = value.astype(BF16)

        group_product(other, [theirs * t2 + q * t1 for q in range(4)], piece, keep_sent)
        pair = pl.ds(2 * piece, 2)
        core_copies[piece, g] = start(g_send.at[g, pair], g_recv.at[g, pair], CORE_G + 2 * g + piece, partner)

    def group_own(piece, g):
        mine = ring(p1, offsets[g])

        def keep_own(n, value):
            g_own[g, n] = value

        group_product(m, [mine * t1 + q * t2 for q in range(4)], piece, keep_own)

    def reduced(dst, parts, rows):
        @pl.loop(0, rows // 128, unroll=True)
        def _(i):
            at = pl.ds(pl.multiple_of(i * 128, 128), 128)
            total = parts[0][at, :].astype(F32)
            for part in parts[1:]:
                total += part[at, :].astype(F32)
            dst[at, :] = total.astype(dst.dtype)

    ring1 = {}

    def chip_sum(g, n):
        return [g_own.at[g, n], g_recv.at[g, n]]

    def ring1_send(piece, g, h, which, device, extra=()):
        n = 2 * piece + h
        reduced(s1.at[g, n], chip_sum(g, n) + list(extra), BLK)
        ring1[piece, which] = start(s1.at[g, n], r1.at[which, piece], STAGE1 + 2 * which + piece, device)

    def first(piece):
        core_copies[piece, 0].wait_recv()
        ring1_send(piece, 0, 0, 0, right1)
        ring1_send(piece, 0, 1, 1, left1)

    def second(piece):
        core_copies[piece, 1].wait_recv()
        ring1_send(piece, 1, 1, 3, right1)
        core_copies[piece, 2].wait_recv()
        ring1_send(piece, 2, 0, 4, left1)

    def third(piece):
        ring1[piece, 0].wait_recv()
        ring1_send(piece, 1, 0, 2, right1, [r1.at[0, piece]])
        ring1[piece, 1].wait_recv()
        ring1_send(piece, 2, 1, 5, left1, [r1.at[1, piece]])

    ring2 = {}
    opp, nxt, prv = ring(p2, 2), ring(p2, 1), ring(p2, 3)

    def block(q, piece, h):
        at = pl.ds(pl.multiple_of(q * 128, 128), 128)
        return [
            ref.at[at, :] for ref in chip_sum(3, 2 * piece + h) + [r1.at[2 + h, piece], r1.at[4 + h, piece]]
        ]

    def ring2_send(piece, g, h, which, device, extra=()):
        n = 2 * piece + h
        reduced(s2.at[g, n], block((opp, nxt, prv)[g], piece, h) + list(extra), 128)
        ring2[piece, which] = start(s2.at[g, n], r2.at[which, piece], STAGE2 + 2 * which + piece, device)

    def ring2_first(piece):
        core_copies[piece, 3].wait_recv()
        for which in (3, 4, 2, 5):
            ring1[piece, which].wait_recv()
        ring2_send(piece, 0, 0, 0, right2)
        ring2_send(piece, 0, 1, 1, left2)
        ring2_send(piece, 1, 1, 3, right2)
        ring2_send(piece, 2, 0, 4, left2)

    def ring2_second(piece):
        ring2[piece, 0].wait_recv()
        ring2_send(piece, 1, 0, 2, right2, [r2.at[0, piece]])
        ring2[piece, 1].wait_recv()
        ring2_send(piece, 2, 1, 5, left2, [r2.at[1, piece]])

    travel = {}

    def dp_first(piece):
        for h, device in ((0, up2), (1, down2)):
            n = 2 * piece + h
            ring2[piece, 2 + h].wait_recv()
            ring2[piece, 4 + h].wait_recv()
            reduced(dp_s.at[n], block(p2, piece, h) + [r2.at[2 + h, piece], r2.at[4 + h, piece]], 128)
            travel[0, n] = start(dp_s.at[n], dp_z.at[n], DP + n, device)

    def dp_second(piece):
        for h, device in ((0, up2), (1, down2)):
            n = 2 * piece + h
            travel[0, n].wait_recv()
            travel[1, n] = start(dp_z.at[n], dp_r.at[n], DP + 4 + n, device)

    group_theirs(0, 0)
    group_theirs(0, 1)
    group_own(0, 0)
    group_theirs(0, 2)
    group_own(0, 1)
    group_own(0, 2)
    first(0)
    second(0)
    group_theirs(1, 0)
    group_own(1, 0)
    for k in (3, 2, 1):
        back_first(k, 1)
    third(0)
    group_theirs(1, 1)
    group_own(1, 1)
    first(1)
    group_theirs(1, 2)
    group_own(1, 2)
    second(1)
    group_theirs(0, 3)
    group_own(0, 3)
    ring2_first(0)
    group_theirs(1, 3)
    group_own(1, 3)
    third(1)
    ring2_second(0)
    back_on(2, 0)
    terms(c, 2, keep_mine(*CHUNKS[2]))
    dp_first(0)
    ring2_first(1)
    back_on(1, 0)
    ring2_second(1)
    back_on(2, 1)
    dp_second(0)
    dp_first(1)
    back_on(1, 1)
    dp_second(1)

    for leftward in (0, 1):
        @pl.when((c < 3) if leftward else (c > 0))
        def _(leftward=leftward):
            for j in range(2):
                back_arrived(leftward, 0, j)
            reduced(it_own, [it_own, back_r.at[leftward, 0]], TOK)

    reduced(ig_s, [it_own], TOK)
    ig_out = pltpu.make_async_copy(ig_s, ig_ref, local.at[4])
    ig_out.start()

    def across_start(place, number, count, device, value):
        place[...] = value
        return [start(place, place, number + k - 1, device(k)) for k in range(1, count + 1)]

    def added(values):
        while len(values) > 1:
            values = [values[i] + values[i + 1] for i in range(0, len(values), 2)]
        return values[0]

    def across_end(copies):
        for copy in copies:
            copy.wait_recv()

    mom.wait_recv()
    lane = lax.broadcasted_iota(jnp.int32, (8, 128), 1)
    old_d = jnp.where((lane // 64) == core, dmom_ref[m], dmom_in[...])[0:1, :]
    old_f = jnp.where(core == 0, in_col_ref[...], out_row_ref[...])
    old_f_sum = jnp.sum(old_f, axis=1, keepdims=True)
    old_d_sum = jnp.sum(old_d, axis=1, keepdims=True)
    col_sums = []
    lanes = None
    for n in range(4):
        travel[1, n].wait_recv()
        grad = dp_s[n].astype(F32) + dp_r[n].astype(F32)
        ratio[n] = grad
        squared = grad * grad
        col_sums.append(jnp.sum(squared, axis=0, keepdims=True))
        folded = squared[:, 0:128] + squared[:, 128:256]
        lanes = folded if n == 0 else lanes + folded
    sub = lax.broadcasted_iota(jnp.int32, (8, 256), 0)
    payload = jnp.where(sub == 4, old_d_sum, 0.0)
    for n in range(4):
        payload = jnp.where(sub == n, col_sums[n], payload)
    sent_xy = across_start(xa.at[chip], SUMS, 15, along_xy, payload)
    row_sums = jnp.sum(lanes.T, axis=0, keepdims=True)
    total = jnp.sum(row_sums, axis=1, keepdims=True)
    sub = lax.broadcasted_iota(jnp.int32, (8, 128), 0)
    sent_z = across_start(za.at[c], SUMS + 15, 3, along_z, jnp.where(sub == 0, row_sums, old_f_sum))
    across_end(sent_z)
    over_z = added([za[i] for i in range(4)])
    d_new = MOMENT_DECAY * old_d + (1.0 - MOMENT_DECAY) * (over_z[0:1, :] / ALL_UNITS + EPSILON_SQ)
    d_column = jnp.broadcast_to(1.0 / jnp.sqrt(d_new), (128, 128)).T[:, 0:1]
    across_end(sent_xy)
    over_xy = added([xa[i] for i in range(16)])
    old_mean = jnp.where(core == 0, over_xy[4:5, 0:1] / WIDTH, over_z[1:2, 0:1] / ALL_UNITS)
    f_new = [
        MOMENT_DECAY * old_f[:, n * 256:(n + 1) * 256]
        + (1.0 - MOMENT_DECAY) * (over_xy[n:n + 1, :] / WIDTH + EPSILON_SQ)
        for n in range(4)
    ]
    lanes = None
    for n in range(4):
        value = ratio[n] * (d_column * (1.0 / jnp.sqrt(f_new[n])))
        ratio[n] = value
        folded = value[:, 0:128] * value[:, 0:128] + value[:, 128:256] * value[:, 128:256]
        lanes = folded if n == 0 else lanes + folded
    folded = lanes[0:8]
    for i in range(1, 16):
        folded += lanes[i * 8:(i + 1) * 8]
    payload = jnp.concatenate([folded, jnp.where(sub == 0, total, old_mean)], axis=0)
    sent_z = across_start(zb.at[core, c], SUMS + 18, 7, along_z_and_cores, payload)

    theirs_at = pl.ds(pl.multiple_of(other * 64, 64), 64)
    swap_v[0] = jnp.zeros((8, UNITS), F32)
    for n in range(4):
        swap_u[0, :, n * 256:(n + 1) * 256] = ratio[n, theirs_at, :]
        swap_v[0, 0:1, n * 256:(n + 1) * 256] = f_new[n]
    swap_v[0, 1:2, 0:128] = d_new
    sent_u = start(swap_u.at[0], swap_u.at[1], SWAP, partner)
    sent_v = start(swap_v.at[0], swap_v.at[1], SWAP + 1, partner)

    across_end(sent_z)
    payload = jnp.stack([added([zb[i, j] for j in range(4)]) for i in range(2)])
    sent_xy = across_start(xb.at[chip], SUMS + 25, 15, along_xy, payload)
    across_end(sent_xy)
    factors = []
    for i in range(2):
        over_all = added([xb[j, i] for j in range(16)])
        mean = MOMENT_DECAY * (over_all[9:10, 0:1] / 64.0) + (1.0 - MOMENT_DECAY) * (
            over_all[8:9, 0:1] / ENTRIES + EPSILON_SQ)
        rms = jnp.sqrt(mean * (jnp.sum(over_all[0:8], keepdims=True) / ENTRIES))
        factors.append(jnp.sqrt(mean) / jnp.maximum(1.0, rms / CLIP_LIMIT))

    def own_lanes(value):
        return jnp.where(core == 0, value[:, 0:64], value[:, 64:128])

    sent_v.wait_recv()
    sent_u.wait_recv()

    def finish(update, row_of, d_out, f_out, which, scale):
        d_out[...] = own_lanes(swap_v[which, 1:2, 0:128])
        f_out[...] = swap_v[which, 0:1, :]
        for n in range(4):
            update[:, n * 256:(n + 1) * 256] = row_of(n) * scale

    def theirs(n):
        return swap_u[1, :, n * 256:(n + 1) * 256]

    @pl.when(core == 0)
    def _():
        finish(in_upd_ref, lambda n: ratio[n, 0:64, :], in_row_out, in_col_out, 0, factors[0])
        finish(out_upd_ref, theirs, out_col_out, out_row_out, 1, factors[1])

    @pl.when(core == 1)
    def _():
        finish(out_upd_ref, lambda n: ratio[n, 64:128, :], out_col_out, out_row_out, 0, factors[1])
        finish(in_upd_ref, theirs, in_row_out, in_col_out, 1, factors[0])

    ig_out.wait()
    for copy in pending:
        copy.wait_send()
    for leftward in (0, 1):
        for k in (1, 2, 3):
            @pl.when(line_sends(leftward, k))
            def _(leftward=leftward, k=k):
                for j in range(2):
                    for i in range(2):
                        line_copy(leftward, k, i, j).wait_send()

            @pl.when((c - k >= 0) if leftward else (c + k <= 3))
            def _(leftward=leftward, k=k):
                for j in range(2):
                    back_copy(leftward, k, j).wait_send()


def fused(*operands):
    vmem = pl.BlockSpec(memory_space=pltpu.VMEM)
    anywhere = pl.BlockSpec(memory_space=pl.ANY)
    return pl.pallas_call(
        kernel,
        out_shape=(
            jax.ShapeDtypeStruct((TOK, BLK), BF16),
            jax.ShapeDtypeStruct((64, UNITS), F32),
            jax.ShapeDtypeStruct((64, UNITS), F32),
            jax.ShapeDtypeStruct((1, 64), F32),
            jax.ShapeDtypeStruct((1, UNITS), F32),
            jax.ShapeDtypeStruct((1, UNITS), F32),
            jax.ShapeDtypeStruct((1, 64), F32),
        ),
        in_specs=[anywhere] * 8,
        out_specs=(anywhere,) + (vmem,) * 6,
        scratch_shapes=[
            pltpu.VMEM((1, 64), F32),
            pltpu.VMEM((1, UNITS), F32),
            pltpu.VMEM((1, UNITS), F32),
            pltpu.VMEM((1, 64), F32),
            pltpu.VMEM((2, 8, 128), F32),
            pltpu.VMEM((2, 4, TOK, BLK), BF16),
            pltpu.VMEM((2, WIDTH, UNITS), BF16),
            pltpu.VMEM((2, TOK, UNITS), F32),
            pltpu.VMEM((2, 16, 128, TOK), BF16),
            pltpu.VMEM((2, TOK, UNITS), BF16),
            pltpu.VMEM((4, 4, 512, 256), F32),
            pltpu.VMEM((4, 4, 512, 256), BF16),
            pltpu.VMEM((4, 4, 512, 256), BF16),
            pltpu.VMEM((3, 4, 512, 256), BF16),
            pltpu.VMEM((6, 2, 512, 256), BF16),
            pltpu.VMEM((3, 4, 128, 256), BF16),
            pltpu.VMEM((6, 2, 128, 256), BF16),
            pltpu.VMEM((4, 128, 256), BF16),
            pltpu.VMEM((4, 128, 256), BF16),
            pltpu.VMEM((4, 128, 256), BF16),
            pltpu.VMEM((8, 128), F32),
            pltpu.VMEM((4, 8, 128), F32),
            pltpu.VMEM((16, 8, 256), F32),
            pltpu.VMEM((2, 4, 16, 128), F32),
            pltpu.VMEM((16, 2, 16, 128), F32),
            pltpu.VMEM((4, 128, 256), F32),
            pltpu.VMEM((2, 64, UNITS), F32),
            pltpu.VMEM((2, 8, UNITS), F32),
            pltpu.VMEM((2, 3, TOK, BLK), BF16),
            pltpu.VMEM((2, 3, TOK, BLK), BF16),
            pltpu.VMEM((TOK, BLK), F32),
            pltpu.VMEM((TOK, BLK), BF16),
            pltpu.SemaphoreType.DMA((N_SEM,)),
            pltpu.SemaphoreType.DMA((N_SEM,)),
            pltpu.SemaphoreType.DMA((9,)),
        ],
        compiler_params=pltpu.CompilerParams(
            collective_id=0, has_side_effects=True, vmem_limit_bytes=60 * 1024 * 1024
        ),
        cost_estimate=pl.CostEstimate(
            flops=10 * TOK * WIDTH * UNITS, bytes_accessed=16 * 2**20, transcendentals=TOK * UNITS
        ),
    )(*operands)


def handed_out_kernel(*refs):
    count = len(refs) // 2
    for i in range(count):
        refs[count + i][...] = refs[i][...]


def handed_out(*results):
    vmem = pl.BlockSpec(memory_space=pltpu.VMEM)
    return pl.pallas_call(
        handed_out_kernel,
        out_shape=tuple(jax.ShapeDtypeStruct(result.shape, result.dtype) for result in results),
        in_specs=[vmem] * len(results),
        out_specs=(vmem,) * len(results),
        compiler_params=pltpu.CompilerParams(vmem_limit_bytes=60 * 1024 * 1024),
    )(*results)


def per_device(
    saved_input, cotangent, weight_in, weight_out, in_row_moment, in_col_moment, out_row_moment, out_col_moment
):
    input_grad, in_update, out_update_t, in_row, in_col, out_row, out_col = handed_out(*fused(
        saved_input, cotangent, weight_in, weight_out.T, in_row_moment.reshape(1, 64), in_col_moment.reshape(1, UNITS),
        out_row_moment.reshape(1, UNITS), out_col_moment.reshape(1, 64),
    ))
    return (
        input_grad, in_update, out_update_t.T, in_row.reshape(64), in_col.reshape(UNITS), out_row.reshape(UNITS),
        out_col.reshape(64),
    )


def solution(mesh):
    placed = (
        P(("dp", "row"), "col"), P(("dp", "row"), "col"), P("row", "col"), P("col", "row"),
        P("row"), P("col"), P("col"), P("row"),
    )
    return jax.shard_map(
        per_device,
        mesh=mesh,
        in_specs=placed,
        out_specs=(
            P(("dp", "row"), "col"), P("row", "col"), P("col", "row"), P("row"), P("col"), P("col"), P("row"),
        ),
        check_vma=False,
    )
```

```python
import jax
import jax.numpy as jnp
from jax import lax
from jax.experimental import pallas as pl
from jax.experimental.pallas import tpu as pltpu
from jax.sharding import PartitionSpec as P

MESH = pl.DeviceIdType.MESH
F32 = jnp.float32
BF16 = jnp.bfloat16

GELU_SCALE = 0.7978845608028654
GELU_CUBIC = 0.044715
MOMENT_DECAY = 0.8
CLIP_LIMIT = 1.0
EPSILON_SQ = 1e-30

TOK, WIDTH, UNITS, BLK = 384, 2048, 1024, 512
ALL_UNITS = 4096
ENTRIES = WIDTH * ALL_UNITS

CORE_G, STAGE1, STAGE2, DP, SUMS, SWAP, MOM = 0, 8, 20, 32, 40, 80, 82
W_SWAP, W_RING1, W_RING2, W_PART, LINE, BACK = 83, 85, 89, 105, 121, 145
N_SEM = 157
CHUNKS = ((0, 256), (256, 128), (0, 384))


def gelu_parts(values):
    inner = GELU_SCALE * (values + GELU_CUBIC * values * values * values)
    tangent = jnp.tanh(inner)
    output = 0.5 * values * (1.0 + tangent)
    slope = 0.5 * (1.0 + tangent) + 0.5 * values * (1.0 - tangent * tangent) * GELU_SCALE * (
        1.0 + 3.0 * GELU_CUBIC * values * values
    )
    return (output, slope)


def kernel(
    x_ref, cot_ref, win_ref, wout_ref, in_row_hbm, in_col_hbm, out_row_hbm, out_col_hbm,
    ig_ref, in_upd_ref, out_upd_ref, in_row_out, in_col_out, out_row_out, out_col_out,
    in_row_ref, in_col_ref, out_row_ref, out_col_ref, dmom_ref, full, w_ref, acc, tr, act, g_own, g_send, g_recv, s1, r1, s2, r2, dp_s, dp_z, dp_r, dmom_in,
    za, xa, zb, xb, ratio, swap_u, swap_v, back_s, back_r, it_own, ig_s,
    ss, rs, local,
):
    d = lax.axis_index("dp")
    r = lax.axis_index("row")
    c = lax.axis_index("col")
    core = lax.rem(r, 2)
    x = lax.rem(r // 2, 4)
    y = r // 8
    p1 = x + core * (y - x)
    p2 = y + core * (x - y)
    k1, k2 = 2 + 6 * core, 8 - 6 * core
    t1, t2 = 1 + 3 * core, 4 - 3 * core
    m = core
    other = 1 - core

    def ring(position, step):
        return lax.rem(position + step, 4)

    def rowdev(q1, q2):
        return {"row": q1 * k1 + q2 * k2 + core}

    partner = {"row": r + 1 - 2 * core}
    right1, left1 = rowdev(ring(p1, 1), p2), rowdev(ring(p1, 3), p2)
    right2, left2 = rowdev(p1, ring(p2, 1)), rowdev(p1, ring(p2, 3))
    up2 = {"dp": lax.rem(d + c // 2, 2), "col": ring(c, 2)}
    down2 = {"dp": lax.rem(d + 1 - c // 2, 2), "col": ring(c, 2)}

    chip = y * 4 + x

    def along_xy(k):
        return {"row": lax.rem(chip + k, 16) * 2 + core}

    def along_z(k):
        return {"col": ring(c, k)}

    def along_z_and_cores(k):
        place = lax.rem(core * 4 + c + k, 8)
        return {"row": r - core + place // 4, "col": lax.rem(place, 4)}

    barrier = pltpu.get_barrier_semaphore()
    peers = [{"dp": 1 - d, "col": ring(c, 2)}]
    peers += [along_z_and_cores(k) for k in range(1, 8)]
    peers += [along_xy(k) for k in range(1, 16)]
    for peer in peers:
        pl.semaphore_signal(barrier, inc=1, device_id=peer, device_id_type=MESH)

    def chip_rows(q1, q2):
        return pl.ds(pl.multiple_of((q1 * t1 + q2 * t2) * 128, 128), 128)

    def half_rows(q1, q2, h):
        return pl.ds(pl.multiple_of((q1 * t1 + q2 * t2) * 128 + h * 64, 64), 64)

    own_rows = half_rows(p1, p2, core)
    loads = [
        pltpu.make_async_copy(x_ref, full.at[0, c], local.at[0]),
        pltpu.make_async_copy(cot_ref, full.at[1, c], local.at[1]),
        pltpu.make_async_copy(win_ref, w_ref.at[0, own_rows, :], local.at[2]),
        pltpu.make_async_copy(wout_ref, w_ref.at[1, own_rows, :], local.at[3]),
        pltpu.make_async_copy(in_row_hbm, in_row_ref, local.at[5]),
        pltpu.make_async_copy(in_col_hbm, in_col_ref, local.at[6]),
        pltpu.make_async_copy(out_row_hbm, out_row_ref, local.at[7]),
        pltpu.make_async_copy(out_col_hbm, out_col_ref, local.at[8]),
    ]
    for copy in loads:
        copy.start()
    for copy in loads:
        copy.wait()
    for i, ref in enumerate((in_row_ref, out_col_ref)):
        dmom_ref[i] = jnp.broadcast_to(jnp.concatenate([ref[...], ref[...]], axis=1), (8, 128))
    pl.semaphore_wait(barrier, len(peers))

    def send(src, dst, number, device):
        copy = pltpu.make_async_remote_copy(
            src_ref=src, dst_ref=dst, send_sem=ss.at[number], recv_sem=rs.at[number],
            device_id=device, device_id_type=MESH,
        )
        copy.start()
        return copy

    pending = []

    def start(src, dst, number, device):
        copy = send(src, dst, number, device)
        pending.append(copy)
        return copy

    def arrived(dst, number):
        pltpu.make_async_remote_copy(
            src_ref=dst, dst_ref=dst, send_sem=ss.at[number], recv_sem=rs.at[number],
            device_id=partner, device_id_type=MESH,
        ).wait_recv()

    def line_number(leftward, k, i, j):
        return LINE + ((leftward * 3 + k - 1) * 2 + j) * 2 + i

    def line_copy(leftward, k, i, j):
        rows = pl.ds(*CHUNKS[j])
        owner = c + (k - 1) if leftward else c - (k - 1)
        number = line_number(leftward, k, i, j)
        return pltpu.make_async_remote_copy(
            src_ref=full.at[i, owner, rows, :], dst_ref=full.at[i, owner, rows, :], send_sem=ss.at[number], recv_sem=rs.at[number],
            device_id={"col": ring(c, 3 if leftward else 1)}, device_id_type=MESH,
        )

    def line_sends(leftward, k):
        return (c > 0) & (c + (k - 1) <= 3) if leftward else (c < 3) & (c - (k - 1) >= 0)

    def line_gets(leftward, k):
        return c + k <= 3 if leftward else c - k >= 0

    def line_start(k, j):
        for leftward in (0, 1):
            @pl.when(line_sends(leftward, k))
            def _(leftward=leftward):
                for i in range(2):
                    line_copy(leftward, k, i, j).start()

    def hand_on(k, j):
        for i in range(2):
            for leftward in (0, 1):
                @pl.when(line_gets(leftward, k))
                def _(i=i, leftward=leftward):
                    owner = c + k if leftward else c - k
                    arrived(full.at[i, owner, pl.ds(*CHUNKS[j]), :], line_number(leftward, k, i, j))

                if k < 3:
                    @pl.when(line_sends(leftward, k + 1))
                    def _(i=i, leftward=leftward):
                        line_copy(leftward, k + 1, i, j).start()

    line_start(1, 0)

    swaps = [start(w_ref.at[i, own_rows, :], w_ref.at[i, own_rows, :], W_SWAP + i, partner) for i in range(2)]
    mom = start(dmom_ref.at[other], dmom_in, MOM, partner)
    def weight_copy(q1, q2, number, device):
        block = w_ref.at[m, chip_rows(q1, q2), :]
        return start(block, block, number, device)

    def half_copy(q1, q2, h, number, device):
        block = w_ref.at[m, half_rows(q1, q2, h), :]
        return start(block, block, number, device)

    def second_ring(e):
        q1 = ring(p1, e)
        weight_copy(q1, p2, W_RING2 + e, right2)
        weight_copy(q1, p2, W_RING2 + 4 + e, left2)

    def second_ring_on(e):
        q1 = ring(p1, e)
        arrived(w_ref.at[m, chip_rows(q1, ring(p2, 3)), :], W_RING2 + e)
        half_copy(q1, ring(p2, 3), 0, W_RING2 + 8 + e, right2)
        arrived(w_ref.at[m, chip_rows(q1, ring(p2, 1)), :], W_RING2 + 4 + e)
        half_copy(q1, ring(p2, 1), 1, W_RING2 + 12 + e, left2)
        to_partner(e, 3)
        to_partner(e, 1)

    def to_partner(e, f):
        weight_copy(ring(p1, e), ring(p2, f), W_PART + 4 * e + f, partner)

    for i in range(2):
        swaps[i].wait_recv()
    weight_copy(p1, p2, W_RING1, right1)
    weight_copy(p1, p2, W_RING1 + 1, left1)
    second_ring(0)

    def transposed(b, j):
        first, count = CHUNKS[j]
        for i in range(2):
            for n in range(4):
                tr[i, b * 4 + n, :, first:first + count] = full[i, b, first:first + count, n * 128:(n + 1) * 128].T

    transposed(c, 0)
    arrived(w_ref.at[m, chip_rows(ring(p1, 3), p2), :], W_RING1)
    half_copy(ring(p1, 3), p2, 0, W_RING1 + 2, right1)
    arrived(w_ref.at[m, chip_rows(ring(p1, 1), p2), :], W_RING1 + 1)
    half_copy(ring(p1, 1), p2, 1, W_RING1 + 3, left1)
    second_ring(3)
    second_ring(1)
    to_partner(3, 0)
    to_partner(1, 0)
    second_ring_on(0)
    line_start(1, 1)
    hand_on(1, 0)
    for h in range(2):
        arrived(w_ref.at[m, half_rows(ring(p1, 2), p2, h), :], W_RING1 + 2 + h)
    second_ring(2)
    to_partner(2, 0)
    transposed(c, 1)
    second_ring_on(3)
    second_ring_on(1)
    hand_on(1, 1)
    second_ring_on(2)

    def both_sides(k, j, *work):
        for owner, there in ((c - k, c - k >= 0), (c + k, c + k <= 3)):
            @pl.when(there)
            def _(owner=owner):
                for part in work:
                    part(owner, j)

    hand_on(2, 0)
    both_sides(1, 0, transposed)
    for e in (0, 3, 1, 2):
        for h in range(2):
            arrived(w_ref.at[m, half_rows(ring(p1, e), ring(p2, 2), h), :], W_RING2 + 8 + 4 * h + e)
        to_partner(e, 2)
    both_sides(1, 1, transposed)
    both_sides(2, 0, transposed)

    def products(b, j, first=False):
        part = pl.ds(pl.multiple_of(b * BLK, BLK), BLK)
        rows = pl.ds(*CHUNKS[j])

        @pl.loop(0, 4, unroll=2)
        def _(n):
            cols = pl.ds(pl.multiple_of(n * 256, 256), 256)
            for i in range(2):
                value = jnp.dot(full[i, b, rows, :], w_ref[i, part, cols], preferred_element_type=F32)
                if first:
                    acc[i, rows, cols] = value
                else:
                    acc[i, rows, cols] += value

    def activate(j):
        rows = pl.ds(*CHUNKS[j])

        @pl.loop(0, 4)
        def _(n):
            cols = pl.ds(pl.multiple_of(n * 256, 256), 256)
            output, slope = gelu_parts(acc[0, rows, cols])
            act[1, rows, cols] = output.astype(BF16)
            act[0, rows, cols] = (acc[1, rows, cols] * slope).astype(BF16)

    def terms(t, j, store):
        rows = pl.ds(*CHUNKS[j])

        @pl.loop(0, 2, unroll=True)
        def _(n):
            inner = pl.ds(pl.multiple_of(n * 256, 256), 256)
            part = pl.ds(pl.multiple_of(t * BLK + n * 256, 256), 256)
            store(inner, lax.dot_general(
                act[0, rows, :], w_ref[0, part, :], (((1,), (1,)), ((), ())), preferred_element_type=F32))

    def keep_mine(first_row, count):
        def keep(inner, value):
            it_own[first_row:first_row + count, inner] = value
        return keep

    def back_copy(leftward, k, j):
        rows = pl.ds(*CHUNKS[j])
        number = BACK + (leftward * 3 + k - 1) * 2 + j
        return pltpu.make_async_remote_copy(
            src_ref=back_s.at[leftward, k - 1, rows, :], dst_ref=back_r.at[leftward, k - 1, rows, :],
            send_sem=ss.at[number], recv_sem=rs.at[number],
            device_id={"col": ring(c, 3 if leftward else 1)}, device_id_type=MESH,
        )

    def back_arrived(leftward, k, j):
        arrived(back_r.at[leftward, k, pl.ds(*CHUNKS[j]), :], BACK + (leftward * 3 + k) * 2 + j)

    def back_first(k, j):
        rows = pl.ds(*CHUNKS[j])
        for leftward in (0, 1):
            @pl.when(c == (3 if leftward else 0))
            def _(leftward=leftward):
                def keep(inner, value):
                    back_s[leftward, k - 1, rows, inner] = value.astype(BF16)

                terms(c - k if leftward else c + k, j, keep)
                back_copy(leftward, k, j).start()

    def back_on(k, j):
        rows = pl.ds(*CHUNKS[j])
        for leftward in (0, 1):
            sends = (c < 3) & (c - k >= 0) if leftward else (c > 0) & (c + k <= 3)

            @pl.when(sends)
            def _(leftward=leftward):
                back_arrived(leftward, k, j)

                def keep(inner, value):
                    back_s[leftward, k - 1, rows, inner] = (
                        value + back_r[leftward, k, rows, inner].astype(F32)).astype(BF16)

                terms(c - k if leftward else c + k, j, keep)
                back_copy(leftward, k, j).start()

    for e in range(4):
        for f in range(4):
            if e or f:
                there = pl.ds(pl.multiple_of((ring(p2, e) * t2 + ring(p1, f) * t1) * 128, 128), 128)
                arrived(w_ref.at[other, there, :], W_PART + 4 * e + f)
    products(c, 2, first=True)
    hand_on(2, 1)
    both_sides(1, 2, products)
    both_sides(2, 1, transposed)
    both_sides(2, 2, products)
    hand_on(3, 0)
    both_sides(3, 0, products)
    activate(0)
    for k in (3, 2, 1):
        back_first(k, 0)
    both_sides(3, 0, transposed)
    hand_on(3, 1)
    both_sides(3, 1, products)
    activate(1)
    both_sides(3, 1, transposed)

    offsets = (2, 1, 3, 0)

    def group_product(matrix, chips, piece, store):
        lhs = jnp.concatenate([tr[matrix, chip] for chip in chips], axis=0)

        @pl.loop(2 * piece, 2 * piece + 2, unroll=True)
        def _(n):
            cols = pl.ds(pl.multiple_of(n * 256, 256), 256)
            store(n, jnp.dot(lhs, act[matrix, :, cols], preferred_element_type=F32))

    core_copies = {}

    def group_theirs(piece, g):
        theirs = ring(p2, offsets[g])

        def keep_sent(n, value):
            g_send[g, n] = value.astype(BF16)

        group_product(other, [theirs * t2 + q * t1 for q in range(4)], piece, keep_sent)
        pair = pl.ds(2 * piece, 2)
        core_copies[piece, g] = start(g_send.at[g, pair], g_recv.at[g, pair], CORE_G + 2 * g + piece, partner)

    def group_own(piece, g):
        mine = ring(p1, offsets[g])

        def keep_own(n, value):
            g_own[g, n] = value

        group_product(m, [mine * t1 + q * t2 for q in range(4)], piece, keep_own)

    def reduced(dst, parts, rows):
        @pl.loop(0, rows // 128, unroll=True)
        def _(i):
            at = pl.ds(pl.multiple_of(i * 128, 128), 128)
            total = parts[0][at, :].astype(F32)
            for part in parts[1:]:
                total += part[at, :].astype(F32)
            dst[at, :] = total.astype(dst.dtype)

    ring1 = {}

    def chip_sum(g, n):
        return [g_own.at[g, n], g_recv.at[g, n]]

    def ring1_send(piece, g, h, which, device, extra=()):
        n = 2 * piece + h
        reduced(s1.at[g, n], chip_sum(g, n) + list(extra), BLK)
        ring1[piece, which] = start(s1.at[g, n], r1.at[which, piece], STAGE1 + 2 * which + piece, device)

    def first(piece):
        core_copies[piece, 0].wait_recv()
        ring1_send(piece, 0, 0, 0, right1)
        ring1_send(piece, 0, 1, 1, left1)

    def second(piece):
        core_copies[piece, 1].wait_recv()
        ring1_send(piece, 1, 1, 3, right1)
        core_copies[piece, 2].wait_recv()
        ring1_send(piece, 2, 0, 4, left1)

    def third(piece):
        ring1[piece, 0].wait_recv()
        ring1_send(piece, 1, 0, 2, right1, [r1.at[0, piece]])
        ring1[piece, 1].wait_recv()
        ring1_send(piece, 2, 1, 5, left1, [r1.at[1, piece]])

    ring2 = {}
    opp, nxt, prv = ring(p2, 2), ring(p2, 1), ring(p2, 3)

    def block(q, piece, h):
        at = pl.ds(pl.multiple_of(q * 128, 128), 128)
        return [
            ref.at[at, :] for ref in chip_sum(3, 2 * piece + h) + [r1.at[2 + h, piece], r1.at[4 + h, piece]]
        ]

    def ring2_send(piece, g, h, which, device, extra=()):
        n = 2 * piece + h
        reduced(s2.at[g, n], block((opp, nxt, prv)[g], piece, h) + list(extra), 128)
        ring2[piece, which] = start(s2.at[g, n], r2.at[which, piece], STAGE2 + 2 * which + piece, device)

    def ring2_first(piece):
        core_copies[piece, 3].wait_recv()
        for which in (3, 4, 2, 5):
            ring1[piece, which].wait_recv()
        ring2_send(piece, 0, 0, 0, right2)
        ring2_send(piece, 0, 1, 1, left2)
        ring2_send(piece, 1, 1, 3, right2)
        ring2_send(piece, 2, 0, 4, left2)

    def ring2_second(piece):
        ring2[piece, 0].wait_recv()
        ring2_send(piece, 1, 0, 2, right2, [r2.at[0, piece]])
        ring2[piece, 1].wait_recv()
        ring2_send(piece, 2, 1, 5, left2, [r2.at[1, piece]])

    travel = {}

    def dp_first(piece):
        for h, device in ((0, up2), (1, down2)):
            n = 2 * piece + h
            ring2[piece, 2 + h].wait_recv()
            ring2[piece, 4 + h].wait_recv()
            reduced(dp_s.at[n], block(p2, piece, h) + [r2.at[2 + h, piece], r2.at[4 + h, piece]], 128)
            travel[0, n] = start(dp_s.at[n], dp_z.at[n], DP + n, device)

    def dp_second(piece):
        for h, device in ((0, up2), (1, down2)):
            n = 2 * piece + h
            travel[0, n].wait_recv()
            travel[1, n] = start(dp_z.at[n], dp_r.at[n], DP + 4 + n, device)

    group_theirs(0, 0)
    group_theirs(0, 1)
    group_own(0, 0)
    group_theirs(0, 2)
    group_own(0, 1)
    group_own(0, 2)
    first(0)
    second(0)
    group_theirs(1, 0)
    group_own(1, 0)
    for k in (3, 2, 1):
        back_first(k, 1)
    third(0)
    group_theirs(1, 1)
    group_own(1, 1)
    first(1)
    group_theirs(1, 2)
    group_own(1, 2)
    second(1)
    group_theirs(0, 3)
    group_own(0, 3)
    ring2_first(0)
    group_theirs(1, 3)
    group_own(1, 3)
    third(1)
    ring2_second(0)
    back_on(2, 0)
    dp_first(0)
    ring2_first(1)
    back_on(1, 0)
    ring2_second(1)
    back_on(2, 1)
    dp_second(0)
    dp_first(1)
    back_on(1, 1)
    dp_second(1)

    def across_start(place, number, count, device, value):
        place[...] = value
        return [start(place, place, number + k - 1, device(k)) for k in range(1, count + 1)]

    def added(values):
        while len(values) > 1:
            values = [values[i] + values[i + 1] for i in range(0, len(values), 2)]
        return values[0]

    def across_end(copies):
        for copy in copies:
            copy.wait_recv()

    mom.wait_recv()
    lane = lax.broadcasted_iota(jnp.int32, (8, 128), 1)
    old_d = jnp.where((lane // 64) == core, dmom_ref[m], dmom_in[...])[0:1, :]
    old_f = jnp.where(core == 0, in_col_ref[...], out_row_ref[...])
    old_f_sum = jnp.sum(old_f, axis=1, keepdims=True)
    old_d_sum = jnp.sum(old_d, axis=1, keepdims=True)
    col_sums = []
    lanes = None
    for n in range(4):
        travel[1, n].wait_recv()
        grad = dp_s[n].astype(F32) + dp_r[n].astype(F32)
        ratio[n] = grad
        squared = grad * grad
        col_sums.append(jnp.sum(squared, axis=0, keepdims=True))
        folded = squared[:, 0:128] + squared[:, 128:256]
        lanes = folded if n == 0 else lanes + folded
    sub = lax.broadcasted_iota(jnp.int32, (8, 256), 0)
    payload = jnp.where(sub == 4, old_d_sum, 0.0)
    for n in range(4):
        payload = jnp.where(sub == n, col_sums[n], payload)
    sent_xy = across_start(xa.at[chip], SUMS, 15, along_xy, payload)
    row_sums = jnp.sum(lanes.T, axis=0, keepdims=True)
    total = jnp.sum(row_sums, axis=1, keepdims=True)
    sub = lax.broadcasted_iota(jnp.int32, (8, 128), 0)
    sent_z = across_start(za.at[c], SUMS + 15, 3, along_z, jnp.where(sub == 0, row_sums, old_f_sum))
    terms(c, 2, keep_mine(*CHUNKS[2]))
    across_end(sent_z)
    over_z = added([za[i] for i in range(4)])
    d_new = MOMENT_DECAY * old_d + (1.0 - MOMENT_DECAY) * (over_z[0:1, :] / ALL_UNITS + EPSILON_SQ)
    d_column = jnp.broadcast_to(1.0 / jnp.sqrt(d_new), (128, 128)).T[:, 0:1]
    across_end(sent_xy)
    over_xy = added([xa[i] for i in range(16)])
    old_mean = jnp.where(core == 0, over_xy[4:5, 0:1] / WIDTH, over_z[1:2, 0:1] / ALL_UNITS)
    f_new = [
        MOMENT_DECAY * old_f[:, n * 256:(n + 1) * 256]
        + (1.0 - MOMENT_DECAY) * (over_xy[n:n + 1, :] / WIDTH + EPSILON_SQ)
        for n in range(4)
    ]
    lanes = None
    for n in range(4):
        value = ratio[n] * (d_column * (1.0 / jnp.sqrt(f_new[n])))
        ratio[n] = value
        folded = value[:, 0:128] * value[:, 0:128] + value[:, 128:256] * value[:, 128:256]
        lanes = folded if n == 0 else lanes + folded
    folded = lanes[0:8]
    for i in range(1, 16):
        folded += lanes[i * 8:(i + 1) * 8]
    payload = jnp.concatenate([folded, jnp.where(sub == 0, total, old_mean)], axis=0)
    sent_z = across_start(zb.at[core, c], SUMS + 18, 7, along_z_and_cores, payload)

    theirs_at = pl.ds(pl.multiple_of(other * 64, 64), 64)
    swap_v[0] = jnp.zeros((8, UNITS), F32)
    for n in range(4):
        swap_u[0, :, n * 256:(n + 1) * 256] = ratio[n, theirs_at, :]
        swap_v[0, 0:1, n * 256:(n + 1) * 256] = f_new[n]
    swap_v[0, 1:2, 0:128] = d_new
    sent_u = start(swap_u.at[0], swap_u.at[1], SWAP, partner)
    sent_v = start(swap_v.at[0], swap_v.at[1], SWAP + 1, partner)

    for leftward in (0, 1):
        @pl.when((c < 3) if leftward else (c > 0))
        def _(leftward=leftward):
            for j in range(2):
                back_arrived(leftward, 0, j)
            reduced(it_own, [it_own, back_r.at[leftward, 0]], TOK)

    reduced(ig_s, [it_own], TOK)
    ig_out = pltpu.make_async_copy(ig_s, ig_ref, local.at[4])
    ig_out.start()

    across_end(sent_z)
    payload = jnp.stack([added([zb[i, j] for j in range(4)]) for i in range(2)])
    sent_xy = across_start(xb.at[chip], SUMS + 25, 15, along_xy, payload)
    across_end(sent_xy)
    factors = []
    for i in range(2):
        over_all = added([xb[j, i] for j in range(16)])
        mean = MOMENT_DECAY * (over_all[9:10, 0:1] / 64.0) + (1.0 - MOMENT_DECAY) * (
            over_all[8:9, 0:1] / ENTRIES + EPSILON_SQ)
        rms = jnp.sqrt(mean * (jnp.sum(over_all[0:8], keepdims=True) / ENTRIES))
        factors.append(jnp.sqrt(mean) / jnp.maximum(1.0, rms / CLIP_LIMIT))

    def own_lanes(value):
        return jnp.where(core == 0, value[:, 0:64], value[:, 64:128])

    sent_v.wait_recv()
    sent_u.wait_recv()

    def finish(update, row_of, d_out, f_out, which, scale):
        d_out[...] = own_lanes(swap_v[which, 1:2, 0:128])
        f_out[...] = swap_v[which, 0:1, :]
        for n in range(4):
            update[:, n * 256:(n + 1) * 256] = row_of(n) * scale

    def theirs(n):
        return swap_u[1, :, n * 256:(n + 1) * 256]

    @pl.when(core == 0)
    def _():
        finish(in_upd_ref, lambda n: ratio[n, 0:64, :], in_row_out, in_col_out, 0, factors[0])
        finish(out_upd_ref, theirs, out_col_out, out_row_out, 1, factors[1])

    @pl.when(core == 1)
    def _():
        finish(out_upd_ref, lambda n: ratio[n, 64:128, :], out_col_out, out_row_out, 0, factors[1])
        finish(in_upd_ref, theirs, in_row_out, in_col_out, 1, factors[0])

    ig_out.wait()
    for copy in pending:
        copy.wait_send()
    for leftward in (0, 1):
        for k in (1, 2, 3):
            @pl.when(line_sends(leftward, k))
            def _(leftward=leftward, k=k):
                for j in range(2):
                    for i in range(2):
                        line_copy(leftward, k, i, j).wait_send()

            @pl.when((c - k >= 0) if leftward else (c + k <= 3))
            def _(leftward=leftward, k=k):
                for j in range(2):
                    back_copy(leftward, k, j).wait_send()


def fused(*operands):
    vmem = pl.BlockSpec(memory_space=pltpu.VMEM)
    anywhere = pl.BlockSpec(memory_space=pl.ANY)
    return pl.pallas_call(
        kernel,
        out_shape=(
            jax.ShapeDtypeStruct((TOK, BLK), BF16),
            jax.ShapeDtypeStruct((64, UNITS), F32),
            jax.ShapeDtypeStruct((64, UNITS), F32),
            jax.ShapeDtypeStruct((1, 64), F32),
            jax.ShapeDtypeStruct((1, UNITS), F32),
            jax.ShapeDtypeStruct((1, UNITS), F32),
            jax.ShapeDtypeStruct((1, 64), F32),
        ),
        in_specs=[anywhere] * 8,
        out_specs=(anywhere,) + (vmem,) * 6,
        scratch_shapes=[
            pltpu.VMEM((1, 64), F32),
            pltpu.VMEM((1, UNITS), F32),
            pltpu.VMEM((1, UNITS), F32),
            pltpu.VMEM((1, 64), F32),
            pltpu.VMEM((2, 8, 128), F32),
            pltpu.VMEM((2, 4, TOK, BLK), BF16),
            pltpu.VMEM((2, WIDTH, UNITS), BF16),
            pltpu.VMEM((2, TOK, UNITS), F32),
            pltpu.VMEM((2, 16, 128, TOK), BF16),
            pltpu.VMEM((2, TOK, UNITS), BF16),
            pltpu.VMEM((4, 4, 512, 256), F32),
            pltpu.VMEM((4, 4, 512, 256), BF16),
            pltpu.VMEM((4, 4, 512, 256), BF16),
            pltpu.VMEM((3, 4, 512, 256), BF16),
            pltpu.VMEM((6, 2, 512, 256), BF16),
            pltpu.VMEM((3, 4, 128, 256), BF16),
            pltpu.VMEM((6, 2, 128, 256), BF16),
            pltpu.VMEM((4, 128, 256), BF16),
            pltpu.VMEM((4, 128, 256), BF16),
            pltpu.VMEM((4, 128, 256), BF16),
            pltpu.VMEM((8, 128), F32),
            pltpu.VMEM((4, 8, 128), F32),
            pltpu.VMEM((16, 8, 256), F32),
            pltpu.VMEM((2, 4, 16, 128), F32),
            pltpu.VMEM((16, 2, 16, 128), F32),
            pltpu.VMEM((4, 128, 256), F32),
            pltpu.VMEM((2, 64, UNITS), F32),
            pltpu.VMEM((2, 8, UNITS), F32),
            pltpu.VMEM((2, 3, TOK, BLK), BF16),
            pltpu.VMEM((2, 3, TOK, BLK), BF16),
            pltpu.VMEM((TOK, BLK), F32),
            pltpu.VMEM((TOK, BLK), BF16),
            pltpu.SemaphoreType.DMA((N_SEM,)),
            pltpu.SemaphoreType.DMA((N_SEM,)),
            pltpu.SemaphoreType.DMA((9,)),
        ],
        compiler_params=pltpu.CompilerParams(
            collective_id=0, has_side_effects=True, vmem_limit_bytes=60 * 1024 * 1024
        ),
        cost_estimate=pl.CostEstimate(
            flops=10 * TOK * WIDTH * UNITS, bytes_accessed=16 * 2**20, transcendentals=TOK * UNITS
        ),
    )(*operands)


def handed_out_kernel(*refs):
    count = len(refs) // 2
    for i in range(count):
        refs[count + i][...] = refs[i][...]


def handed_out(*results):
    vmem = pl.BlockSpec(memory_space=pltpu.VMEM)
    return pl.pallas_call(
        handed_out_kernel,
        out_shape=tuple(jax.ShapeDtypeStruct(result.shape, result.dtype) for result in results),
        in_specs=[vmem] * len(results),
        out_specs=(vmem,) * len(results),
        compiler_params=pltpu.CompilerParams(vmem_limit_bytes=60 * 1024 * 1024),
    )(*results)


def per_device(
    saved_input, cotangent, weight_in, weight_out, in_row_moment, in_col_moment, out_row_moment, out_col_moment
):
    input_grad, in_update, out_update_t, in_row, in_col, out_row, out_col = handed_out(*fused(
        saved_input, cotangent, weight_in, weight_out.T, in_row_moment.reshape(1, 64), in_col_moment.reshape(1, UNITS),
        out_row_moment.reshape(1, UNITS), out_col_moment.reshape(1, 64),
    ))
    return (
        input_grad, in_update, out_update_t.T, in_row.reshape(64), in_col.reshape(UNITS), out_row.reshape(UNITS),
        out_col.reshape(64),
    )


def solution(mesh):
    placed = (
        P(("dp", "row"), "col"), P(("dp", "row"), "col"), P("row", "col"), P("col", "row"),
        P("row"), P("col"), P("col"), P("row"),
    )
    return jax.shard_map(
        per_device,
        mesh=mesh,
        in_specs=placed,
        out_specs=(
            P(("dp", "row"), "col"), P("row", "col"), P("col", "row"), P("row"), P("col"), P("col"), P("row"),
        ),
        check_vma=False,
    )
```

```python
import jax
import jax.numpy as jnp
from jax import lax
from jax.experimental import pallas as pl
from jax.experimental.pallas import tpu as pltpu
from jax.sharding import PartitionSpec as P

MESH = pl.DeviceIdType.MESH
F32 = jnp.float32
BF16 = jnp.bfloat16

GELU_SCALE = 0.7978845608028654
GELU_CUBIC = 0.044715
MOMENT_DECAY = 0.8
CLIP_LIMIT = 1.0
EPSILON_SQ = 1e-30

TOK, WIDTH, UNITS, BLK = 384, 2048, 1024, 512
ALL_UNITS = 4096
ENTRIES = WIDTH * ALL_UNITS

CORE_G, STAGE1, STAGE2, DP, SUMS, SWAP, MOM = 0, 8, 20, 32, 40, 80, 82
W_SWAP, W_RING1, W_RING2, W_PART, LINE, BACK = 83, 85, 89, 105, 121, 133
N_SEM = 145
CHUNKS = ((0, 256), (256, 128), (0, 384))


def gelu_parts(values):
    inner = GELU_SCALE * (values + GELU_CUBIC * values * values * values)
    tangent = jnp.tanh(inner)
    output = 0.5 * values * (1.0 + tangent)
    slope = 0.5 * (1.0 + tangent) + 0.5 * values * (1.0 - tangent * tangent) * GELU_SCALE * (
        1.0 + 3.0 * GELU_CUBIC * values * values
    )
    return (output, slope)


def kernel(
    x_ref, cot_ref, win_ref, wout_ref, in_row_hbm, in_col_hbm, out_row_hbm, out_col_hbm,
    ig_ref, in_upd_ref, out_upd_ref, in_row_out, in_col_out, out_row_out, out_col_out,
    in_row_ref, in_col_ref, out_row_ref, out_col_ref, dmom_ref, full, w_ref, acc, tr, act, g_own, g_send, g_recv, s1, r1, s2, r2, dp_s, dp_z, dp_r, dmom_in,
    za, xa, zb, xb, ratio, swap_u, swap_v, back_s, back_r, it_own, ig_s,
    ss, rs, local,
):
    d = lax.axis_index("dp")
    r = lax.axis_index("row")
    c = lax.axis_index("col")
    core = lax.rem(r, 2)
    x = lax.rem(r // 2, 4)
    y = r // 8
    p1 = x + core * (y - x)
    p2 = y + core * (x - y)
    k1, k2 = 2 + 6 * core, 8 - 6 * core
    t1, t2 = 1 + 3 * core, 4 - 3 * core
    m = core
    other = 1 - core

    def ring(position, step):
        return lax.rem(position + step, 4)

    def rowdev(q1, q2):
        return {"row": q1 * k1 + q2 * k2 + core}

    partner = {"row": r + 1 - 2 * core}
    right1, left1 = rowdev(ring(p1, 1), p2), rowdev(ring(p1, 3), p2)
    right2, left2 = rowdev(p1, ring(p2, 1)), rowdev(p1, ring(p2, 3))
    up2 = {"dp": lax.rem(d + c // 2, 2), "col": ring(c, 2)}
    down2 = {"dp": lax.rem(d + 1 - c // 2, 2), "col": ring(c, 2)}

    chip = y * 4 + x

    def along_xy(k):
        return {"row": lax.rem(chip + k, 16) * 2 + core}

    def along_z(k):
        return {"col": ring(c, k)}

    def along_z_and_cores(k):
        place = lax.rem(core * 4 + c + k, 8)
        return {"row": r - core + place // 4, "col": lax.rem(place, 4)}

    barrier = pltpu.get_barrier_semaphore()
    peers = [{"dp": 1 - d, "col": ring(c, 2)}]
    peers += [along_z_and_cores(k) for k in range(1, 8)]
    peers += [along_xy(k) for k in range(1, 16)]
    for peer in peers:
        pl.semaphore_signal(barrier, inc=1, device_id=peer, device_id_type=MESH)

    def chip_rows(q1, q2):
        return pl.ds(pl.multiple_of((q1 * t1 + q2 * t2) * 128, 128), 128)

    def half_rows(q1, q2, h):
        return pl.ds(pl.multiple_of((q1 * t1 + q2 * t2) * 128 + h * 64, 64), 64)

    own_rows = half_rows(p1, p2, core)
    loads = [
        pltpu.make_async_copy(x_ref, full.at[0, c], local.at[0]),
        pltpu.make_async_copy(cot_ref, full.at[1, c], local.at[1]),
        pltpu.make_async_copy(win_ref, w_ref.at[0, own_rows, :], local.at[2]),
        pltpu.make_async_copy(wout_ref, w_ref.at[1, own_rows, :], local.at[3]),
        pltpu.make_async_copy(in_row_hbm, in_row_ref, local.at[5]),
        pltpu.make_async_copy(in_col_hbm, in_col_ref, local.at[6]),
        pltpu.make_async_copy(out_row_hbm, out_row_ref, local.at[7]),
        pltpu.make_async_copy(out_col_hbm, out_col_ref, local.at[8]),
    ]
    for copy in loads:
        copy.start()
    for copy in loads:
        copy.wait()
    for i, ref in enumerate((in_row_ref, out_col_ref)):
        dmom_ref[i] = jnp.broadcast_to(jnp.concatenate([ref[...], ref[...]], axis=1), (8, 128))
    pl.semaphore_wait(barrier, len(peers))

    def send(src, dst, number, device):
        copy = pltpu.make_async_remote_copy(
            src_ref=src, dst_ref=dst, send_sem=ss.at[number], recv_sem=rs.at[number],
            device_id=device, device_id_type=MESH,
        )
        copy.start()
        return copy

    pending = []

    def start(src, dst, number, device):
        copy = send(src, dst, number, device)
        pending.append(copy)
        return copy

    def arrived(dst, number):
        pltpu.make_async_remote_copy(
            src_ref=dst, dst_ref=dst, send_sem=ss.at[number], recv_sem=rs.at[number],
            device_id=partner, device_id_type=MESH,
        ).wait_recv()

    def line_number(leftward, k, j):
        return LINE + (leftward * 3 + k - 1) * 2 + j

    def line_copy(leftward, k, j):
        owner = c + (k - 1) if leftward else c - (k - 1)
        number = line_number(leftward, k, j)
        block = full.at[:, owner, pl.ds(*CHUNKS[j]), :]
        return pltpu.make_async_remote_copy(
            src_ref=block, dst_ref=block, send_sem=ss.at[number], recv_sem=rs.at[number],
            device_id={"col": ring(c, 3 if leftward else 1)}, device_id_type=MESH,
        )

    def line_sends(leftward, k):
        return (c > 0) & (c + (k - 1) <= 3) if leftward else (c < 3) & (c - (k - 1) >= 0)

    def line_gets(leftward, k):
        return c + k <= 3 if leftward else c - k >= 0

    def line_start(k, j):
        for leftward in (0, 1):
            @pl.when(line_sends(leftward, k))
            def _(leftward=leftward):
                line_copy(leftward, k, j).start()

    def hand_on(k, j):
        for leftward in (0, 1):
            @pl.when(line_gets(leftward, k))
            def _(leftward=leftward):
                owner = c + k if leftward else c - k
                arrived(full.at[:, owner, pl.ds(*CHUNKS[j]), :], line_number(leftward, k, j))

            if k < 3:
                @pl.when(line_sends(leftward, k + 1))
                def _(leftward=leftward):
                    line_copy(leftward, k + 1, j).start()

    line_start(1, 0)

    swaps = [start(w_ref.at[i, own_rows, :], w_ref.at[i, own_rows, :], W_SWAP + i, partner) for i in range(2)]
    mom = start(dmom_ref.at[other], dmom_in, MOM, partner)
    def weight_copy(q1, q2, number, device):
        block = w_ref.at[m, chip_rows(q1, q2), :]
        return start(block, block, number, device)

    def half_copy(q1, q2, h, number, device):
        block = w_ref.at[m, half_rows(q1, q2, h), :]
        return start(block, block, number, device)

    def second_ring(e):
        q1 = ring(p1, e)
        weight_copy(q1, p2, W_RING2 + e, right2)
        weight_copy(q1, p2, W_RING2 + 4 + e, left2)

    def second_ring_on(e):
        q1 = ring(p1, e)
        arrived(w_ref.at[m, chip_rows(q1, ring(p2, 3)), :], W_RING2 + e)
        half_copy(q1, ring(p2, 3), 0, W_RING2 + 8 + e, right2)
        arrived(w_ref.at[m, chip_rows(q1, ring(p2, 1)), :], W_RING2 + 4 + e)
        half_copy(q1, ring(p2, 1), 1, W_RING2 + 12 + e, left2)
        to_partner(e, 3)
        to_partner(e, 1)

    def to_partner(e, f):
        weight_copy(ring(p1, e), ring(p2, f), W_PART + 4 * e + f, partner)

    for i in range(2):
        swaps[i].wait_recv()
    weight_copy(p1, p2, W_RING1, right1)
    weight_copy(p1, p2, W_RING1 + 1, left1)
    second_ring(0)

    def transposed(b, j):
        first, count = CHUNKS[j]
        for i in range(2):
            for n in range(4):
                tr[i, b * 4 + n, :, first:first + count] = full[i, b, first:first + count, n * 128:(n + 1) * 128].T

    transposed(c, 0)
    arrived(w_ref.at[m, chip_rows(ring(p1, 3), p2), :], W_RING1)
    half_copy(ring(p1, 3), p2, 0, W_RING1 + 2, right1)
    arrived(w_ref.at[m, chip_rows(ring(p1, 1), p2), :], W_RING1 + 1)
    half_copy(ring(p1, 1), p2, 1, W_RING1 + 3, left1)
    second_ring(3)
    second_ring(1)
    to_partner(3, 0)
    to_partner(1, 0)
    second_ring_on(0)
    line_start(1, 1)
    hand_on(1, 0)
    for h in range(2):
        arrived(w_ref.at[m, half_rows(ring(p1, 2), p2, h), :], W_RING1 + 2 + h)
    second_ring(2)
    to_partner(2, 0)
    transposed(c, 1)
    second_ring_on(3)
    second_ring_on(1)
    hand_on(1, 1)
    second_ring_on(2)

    def both_sides(k, j, *work):
        for owner, there in ((c - k, c - k >= 0), (c + k, c + k <= 3)):
            @pl.when(there)
            def _(owner=owner):
                for part in work:
                    part(owner, j)

    hand_on(2, 0)
    both_sides(1, 0, transposed)
    for e in (0, 3, 1, 2):
        for h in range(2):
            arrived(w_ref.at[m, half_rows(ring(p1, e), ring(p2, 2), h), :], W_RING2 + 8 + 4 * h + e)
        to_partner(e, 2)
    both_sides(1, 1, transposed)
    both_sides(2, 0, transposed)

    def products(b, j, first=False):
        part = pl.ds(pl.multiple_of(b * BLK, BLK), BLK)
        rows = pl.ds(*CHUNKS[j])

        @pl.loop(0, 4, unroll=2)
        def _(n):
            cols = pl.ds(pl.multiple_of(n * 256, 256), 256)
            for i in range(2):
                value = jnp.dot(full[i, b, rows, :], w_ref[i, part, cols], preferred_element_type=F32)
                if first:
                    acc[i, rows, cols] = value
                else:
                    acc[i, rows, cols] += value

    def activate(j):
        rows = pl.ds(*CHUNKS[j])

        @pl.loop(0, 4)
        def _(n):
            cols = pl.ds(pl.multiple_of(n * 256, 256), 256)
            output, slope = gelu_parts(acc[0, rows, cols])
            act[1, rows, cols] = output.astype(BF16)
            act[0, rows, cols] = (acc[1, rows, cols] * slope).astype(BF16)

    def terms(t, j, store):
        rows = pl.ds(*CHUNKS[j])

        @pl.loop(0, 2, unroll=True)
        def _(n):
            inner = pl.ds(pl.multiple_of(n * 256, 256), 256)
            part = pl.ds(pl.multiple_of(t * BLK + n * 256, 256), 256)
            store(inner, lax.dot_general(
                act[0, rows, :], w_ref[0, part, :], (((1,), (1,)), ((), ())), preferred_element_type=F32))

    def keep_mine(first_row, count):
        def keep(inner, value):
            it_own[first_row:first_row + count, inner] = value
        return keep

    def back_copy(leftward, k, j):
        rows = pl.ds(*CHUNKS[j])
        number = BACK + (leftward * 3 + k - 1) * 2 + j
        return pltpu.make_async_remote_copy(
            src_ref=back_s.at[leftward, k - 1, rows, :], dst_ref=back_r.at[leftward, k - 1, rows, :],
            send_sem=ss.at[number], recv_sem=rs.at[number],
            device_id={"col": ring(c, 3 if leftward else 1)}, device_id_type=MESH,
        )

    def back_arrived(leftward, k, j):
        arrived(back_r.at[leftward, k, pl.ds(*CHUNKS[j]), :], BACK + (leftward * 3 + k) * 2 + j)

    def back_first(k, j):
        rows = pl.ds(*CHUNKS[j])
        for leftward in (0, 1):
            @pl.when(c == (3 if leftward else 0))
            def _(leftward=leftward):
                def keep(inner, value):
                    back_s[leftward, k - 1, rows, inner] = value.astype(BF16)

                terms(c - k if leftward else c + k, j, keep)
                back_copy(leftward, k, j).start()

    def back_on(k, j):
        rows = pl.ds(*CHUNKS[j])
        for leftward in (0, 1):
            sends = (c < 3) & (c - k >= 0) if leftward else (c > 0) & (c + k <= 3)

            @pl.when(sends)
            def _(leftward=leftward):
                back_arrived(leftward, k, j)

                def keep(inner, value):
                    back_s[leftward, k - 1, rows, inner] = (
                        value + back_r[leftward, k, rows, inner].astype(F32)).astype(BF16)

                terms(c - k if leftward else c + k, j, keep)
                back_copy(leftward, k, j).start()

    for e in range(4):
        for f in range(4):
            if e or f:
                there = pl.ds(pl.multiple_of((ring(p2, e) * t2 + ring(p1, f) * t1) * 128, 128), 128)
                arrived(w_ref.at[other, there, :], W_PART + 4 * e + f)
    products(c, 2, first=True)
    hand_on(2, 1)
    both_sides(1, 2, products)
    both_sides(2, 1, transposed)
    both_sides(2, 2, products)
    hand_on(3, 0)
    both_sides(3, 0, products)
    activate(0)
    for k in (3, 2, 1):
        back_first(k, 0)
    both_sides(3, 0, transposed)
    hand_on(3, 1)
    both_sides(3, 1, products)
    activate(1)
    both_sides(3, 1, transposed)

    offsets = (2, 1, 3, 0)

    def group_product(matrix, chips, piece, store):
        lhs = jnp.concatenate([tr[matrix, chip] for chip in chips], axis=0)

        @pl.loop(2 * piece, 2 * piece + 2, unroll=True)
        def _(n):
            cols = pl.ds(pl.multiple_of(n * 256, 256), 256)
            store(n, jnp.dot(lhs, act[matrix, :, cols], preferred_element_type=F32))

    core_copies = {}

    def group_theirs(piece, g):
        theirs = ring(p2, offsets[g])

        def keep_sent(n, value):
            g_send[g, n] = value.astype(BF16)

        group_product(other, [theirs * t2 + q * t1 for q in range(4)], piece, keep_sent)
        pair = pl.ds(2 * piece, 2)
        core_copies[piece, g] = start(g_send.at[g, pair], g_recv.at[g, pair], CORE_G + 2 * g + piece, partner)

    def group_own(piece, g):
        mine = ring(p1, offsets[g])

        def keep_own(n, value):
            g_own[g, n] = value

        group_product(m, [mine * t1 + q * t2 for q in range(4)], piece, keep_own)

    def reduced(dst, parts, rows):
        @pl.loop(0, rows // 128, unroll=True)
        def _(i):
            at = pl.ds(pl.multiple_of(i * 128, 128), 128)
            total = parts[0][at, :].astype(F32)
            for part in parts[1:]:
                total += part[at, :].astype(F32)
            dst[at, :] = total.astype(dst.dtype)

    ring1 = {}

    def chip_sum(g, n):
        return [g_own.at[g, n], g_recv.at[g, n]]

    def ring1_send(piece, g, h, which, device, extra=()):
        n = 2 * piece + h
        reduced(s1.at[g, n], chip_sum(g, n) + list(extra), BLK)
        ring1[piece, which] = start(s1.at[g, n], r1.at[which, piece], STAGE1 + 2 * which + piece, device)

    def first(piece):
        core_copies[piece, 0].wait_recv()
        ring1_send(piece, 0, 0, 0, right1)
        ring1_send(piece, 0, 1, 1, left1)

    def second(piece):
        core_copies[piece, 1].wait_recv()
        ring1_send(piece, 1, 1, 3, right1)
        core_copies[piece, 2].wait_recv()
        ring1_send(piece, 2, 0, 4, left1)

    def third(piece):
        ring1[piece, 0].wait_recv()
        ring1_send(piece, 1, 0, 2, right1, [r1.at[0, piece]])
        ring1[piece, 1].wait_recv()
        ring1_send(piece, 2, 1, 5, left1, [r1.at[1, piece]])

    ring2 = {}
    opp, nxt, prv = ring(p2, 2), ring(p2, 1), ring(p2, 3)

    def block(q, piece, h):
        at = pl.ds(pl.multiple_of(q * 128, 128), 128)
        return [
            ref.at[at, :] for ref in chip_sum(3, 2 * piece + h) + [r1.at[2 + h, piece], r1.at[4 + h, piece]]
        ]

    def ring2_send(piece, g, h, which, device, extra=()):
        n = 2 * piece + h
        reduced(s2.at[g, n], block((opp, nxt, prv)[g], piece, h) + list(extra), 128)
        ring2[piece, which] = start(s2.at[g, n], r2.at[which, piece], STAGE2 + 2 * which + piece, device)

    def ring2_first(piece):
        core_copies[piece, 3].wait_recv()
        for which in (3, 4, 2, 5):
            ring1[piece, which].wait_recv()
        ring2_send(piece, 0, 0, 0, right2)
        ring2_send(piece, 0, 1, 1, left2)
        ring2_send(piece, 1, 1, 3, right2)
        ring2_send(piece, 2, 0, 4, left2)

    def ring2_second(piece):
        ring2[piece, 0].wait_recv()
        ring2_send(piece, 1, 0, 2, right2, [r2.at[0, piece]])
        ring2[piece, 1].wait_recv()
        ring2_send(piece, 2, 1, 5, left2, [r2.at[1, piece]])

    travel = {}

    def dp_first(piece):
        for h, device in ((0, up2), (1, down2)):
            n = 2 * piece + h
            ring2[piece, 2 + h].wait_recv()
            ring2[piece, 4 + h].wait_recv()
            reduced(dp_s.at[n], block(p2, piece, h) + [r2.at[2 + h, piece], r2.at[4 + h, piece]], 128)
            travel[0, n] = start(dp_s.at[n], dp_z.at[n], DP + n, device)

    def dp_second(piece):
        for h, device in ((0, up2), (1, down2)):
            n = 2 * piece + h
            travel[0, n].wait_recv()
            travel[1, n] = start(dp_z.at[n], dp_r.at[n], DP + 4 + n, device)

    group_theirs(0, 0)
    group_theirs(0, 1)
    group_own(0, 0)
    group_theirs(0, 2)
    group_own(0, 1)
    group_own(0, 2)
    first(0)
    second(0)
    group_theirs(1, 0)
    group_own(1, 0)
    for k in (3, 2, 1):
        back_first(k, 1)
    third(0)
    group_theirs(1, 1)
    group_own(1, 1)
    first(1)
    group_theirs(1, 2)
    group_own(1, 2)
    second(1)
    group_theirs(0, 3)
    group_own(0, 3)
    ring2_first(0)
    group_theirs(1, 3)
    group_own(1, 3)
    third(1)
    ring2_second(0)
    back_on(2, 0)
    dp_first(0)
    ring2_first(1)
    back_on(1, 0)
    ring2_second(1)
    back_on(2, 1)
    dp_second(0)
    dp_first(1)
    back_on(1, 1)
    dp_second(1)

    def across_start(place, number, count, device, value):
        place[...] = value
        return [start(place, place, number + k - 1, device(k)) for k in range(1, count + 1)]

    def added(values):
        while len(values) > 1:
            values = [values[i] + values[i + 1] for i in range(0, len(values), 2)]
        return values[0]

    def across_end(copies):
        for copy in copies:
            copy.wait_recv()

    mom.wait_recv()
    lane = lax.broadcasted_iota(jnp.int32, (8, 128), 1)
    old_d = jnp.where((lane // 64) == core, dmom_ref[m], dmom_in[...])[0:1, :]
    old_f = jnp.where(core == 0, in_col_ref[...], out_row_ref[...])
    old_f_sum = jnp.sum(old_f, axis=1, keepdims=True)
    old_d_sum = jnp.sum(old_d, axis=1, keepdims=True)
    col_sums = []
    lanes = None
    for n in range(4):
        travel[1, n].wait_recv()
        grad = dp_s[n].astype(F32) + dp_r[n].astype(F32)
        ratio[n] = grad
        squared = grad * grad
        col_sums.append(jnp.sum(squared, axis=0, keepdims=True))
        folded = squared[:, 0:128] + squared[:, 128:256]
        lanes = folded if n == 0 else lanes + folded
    sub = lax.broadcasted_iota(jnp.int32, (8, 256), 0)
    payload = jnp.where(sub == 4, old_d_sum, 0.0)
    for n in range(4):
        payload = jnp.where(sub == n, col_sums[n], payload)
    sent_xy = across_start(xa.at[chip], SUMS, 15, along_xy, payload)
    row_sums = jnp.sum(lanes.T, axis=0, keepdims=True)
    total = jnp.sum(row_sums, axis=1, keepdims=True)
    sub = lax.broadcasted_iota(jnp.int32, (8, 128), 0)
    sent_z = across_start(za.at[c], SUMS + 15, 3, along_z, jnp.where(sub == 0, row_sums, old_f_sum))
    terms(c, 2, keep_mine(*CHUNKS[2]))
    across_end(sent_z)
    over_z = added([za[i] for i in range(4)])
    d_new = MOMENT_DECAY * old_d + (1.0 - MOMENT_DECAY) * (over_z[0:1, :] / ALL_UNITS + EPSILON_SQ)
    d_column = jnp.broadcast_to(1.0 / jnp.sqrt(d_new), (128, 128)).T[:, 0:1]
    across_end(sent_xy)
    over_xy = added([xa[i] for i in range(16)])
    old_mean = jnp.where(core == 0, over_xy[4:5, 0:1] / WIDTH, over_z[1:2, 0:1] / ALL_UNITS)
    f_new = [
        MOMENT_DECAY * old_f[:, n * 256:(n + 1) * 256]
        + (1.0 - MOMENT_DECAY) * (over_xy[n:n + 1, :] / WIDTH + EPSILON_SQ)
        for n in range(4)
    ]
    lanes = None
    for n in range(4):
        value = ratio[n] * (d_column * (1.0 / jnp.sqrt(f_new[n])))
        ratio[n] = value
        folded = value[:, 0:128] * value[:, 0:128] + value[:, 128:256] * value[:, 128:256]
        lanes = folded if n == 0 else lanes + folded
    folded = lanes[0:8]
    for i in range(1, 16):
        folded += lanes[i * 8:(i + 1) * 8]
    payload = jnp.concatenate([folded, jnp.where(sub == 0, total, old_mean)], axis=0)
    sent_z = across_start(zb.at[core, c], SUMS + 18, 7, along_z_and_cores, payload)

    theirs_at = pl.ds(pl.multiple_of(other * 64, 64), 64)
    swap_v[0] = jnp.zeros((8, UNITS), F32)
    for n in range(4):
        swap_u[0, :, n * 256:(n + 1) * 256] = ratio[n, theirs_at, :]
        swap_v[0, 0:1, n * 256:(n + 1) * 256] = f_new[n]
    swap_v[0, 1:2, 0:128] = d_new
    sent_u = start(swap_u.at[0], swap_u.at[1], SWAP, partner)
    sent_v = start(swap_v.at[0], swap_v.at[1], SWAP + 1, partner)

    for leftward in (0, 1):
        @pl.when((c < 3) if leftward else (c > 0))
        def _(leftward=leftward):
            for j in range(2):
                back_arrived(leftward, 0, j)
            reduced(it_own, [it_own, back_r.at[leftward, 0]], TOK)

    reduced(ig_s, [it_own], TOK)
    ig_out = pltpu.make_async_copy(ig_s, ig_ref, local.at[4])
    ig_out.start()

    across_end(sent_z)
    payload = jnp.stack([added([zb[i, j] for j in range(4)]) for i in range(2)])
    sent_xy = across_start(xb.at[chip], SUMS + 25, 15, along_xy, payload)
    across_end(sent_xy)
    factors = []
    for i in range(2):
        over_all = added([xb[j, i] for j in range(16)])
        mean = MOMENT_DECAY * (over_all[9:10, 0:1] / 64.0) + (1.0 - MOMENT_DECAY) * (
            over_all[8:9, 0:1] / ENTRIES + EPSILON_SQ)
        rms = jnp.sqrt(mean * (jnp.sum(over_all[0:8], keepdims=True) / ENTRIES))
        factors.append(jnp.sqrt(mean) / jnp.maximum(1.0, rms / CLIP_LIMIT))

    def own_lanes(value):
        return jnp.where(core == 0, value[:, 0:64], value[:, 64:128])

    sent_v.wait_recv()
    sent_u.wait_recv()

    def finish(update, row_of, d_out, f_out, which, scale):
        d_out[...] = own_lanes(swap_v[which, 1:2, 0:128])
        f_out[...] = swap_v[which, 0:1, :]
        for n in range(4):
            update[:, n * 256:(n + 1) * 256] = row_of(n) * scale

    def theirs(n):
        return swap_u[1, :, n * 256:(n + 1) * 256]

    @pl.when(core == 0)
    def _():
        finish(in_upd_ref, lambda n: ratio[n, 0:64, :], in_row_out, in_col_out, 0, factors[0])
        finish(out_upd_ref, theirs, out_col_out, out_row_out, 1, factors[1])

    @pl.when(core == 1)
    def _():
        finish(out_upd_ref, lambda n: ratio[n, 64:128, :], out_col_out, out_row_out, 0, factors[1])
        finish(in_upd_ref, theirs, in_row_out, in_col_out, 1, factors[0])

    ig_out.wait()
    for copy in pending:
        copy.wait_send()
    for leftward in (0, 1):
        for k in (1, 2, 3):
            @pl.when(line_sends(leftward, k))
            def _(leftward=leftward, k=k):
                for j in range(2):
                    line_copy(leftward, k, j).wait_send()

            @pl.when((c - k >= 0) if leftward else (c + k <= 3))
            def _(leftward=leftward, k=k):
                for j in range(2):
                    back_copy(leftward, k, j).wait_send()


def fused(*operands):
    vmem = pl.BlockSpec(memory_space=pltpu.VMEM)
    anywhere = pl.BlockSpec(memory_space=pl.ANY)
    return pl.pallas_call(
        kernel,
        out_shape=(
            jax.ShapeDtypeStruct((TOK, BLK), BF16),
            jax.ShapeDtypeStruct((64, UNITS), F32),
            jax.ShapeDtypeStruct((64, UNITS), F32),
            jax.ShapeDtypeStruct((1, 64), F32),
            jax.ShapeDtypeStruct((1, UNITS), F32),
            jax.ShapeDtypeStruct((1, UNITS), F32),
            jax.ShapeDtypeStruct((1, 64), F32),
        ),
        in_specs=[anywhere] * 8,
        out_specs=(anywhere,) + (vmem,) * 6,
        scratch_shapes=[
            pltpu.VMEM((1, 64), F32),
            pltpu.VMEM((1, UNITS), F32),
            pltpu.VMEM((1, UNITS), F32),
            pltpu.VMEM((1, 64), F32),
            pltpu.VMEM((2, 8, 128), F32),
            pltpu.VMEM((2, 4, TOK, BLK), BF16),
            pltpu.VMEM((2, WIDTH, UNITS), BF16),
            pltpu.VMEM((2, TOK, UNITS), F32),
            pltpu.VMEM((2, 16, 128, TOK), BF16),
            pltpu.VMEM((2, TOK, UNITS), BF16),
            pltpu.VMEM((4, 4, 512, 256), F32),
            pltpu.VMEM((4, 4, 512, 256), BF16),
            pltpu.VMEM((4, 4, 512, 256), BF16),
            pltpu.VMEM((3, 4, 512, 256), BF16),
            pltpu.VMEM((6, 2, 512, 256), BF16),
            pltpu.VMEM((3, 4, 128, 256), BF16),
            pltpu.VMEM((6, 2, 128, 256), BF16),
            pltpu.VMEM((4, 128, 256), BF16),
            pltpu.VMEM((4, 128, 256), BF16),
            pltpu.VMEM((4, 128, 256), BF16),
            pltpu.VMEM((8, 128), F32),
            pltpu.VMEM((4, 8, 128), F32),
            pltpu.VMEM((16, 8, 256), F32),
            pltpu.VMEM((2, 4, 16, 128), F32),
            pltpu.VMEM((16, 2, 16, 128), F32),
            pltpu.VMEM((4, 128, 256), F32),
            pltpu.VMEM((2, 64, UNITS), F32),
            pltpu.VMEM((2, 8, UNITS), F32),
            pltpu.VMEM((2, 3, TOK, BLK), BF16),
            pltpu.VMEM((2, 3, TOK, BLK), BF16),
            pltpu.VMEM((TOK, BLK), F32),
            pltpu.VMEM((TOK, BLK), BF16),
            pltpu.SemaphoreType.DMA((N_SEM,)),
            pltpu.SemaphoreType.DMA((N_SEM,)),
            pltpu.SemaphoreType.DMA((9,)),
        ],
        compiler_params=pltpu.CompilerParams(
            collective_id=0, has_side_effects=True, vmem_limit_bytes=60 * 1024 * 1024
        ),
        cost_estimate=pl.CostEstimate(
            flops=10 * TOK * WIDTH * UNITS, bytes_accessed=16 * 2**20, transcendentals=TOK * UNITS
        ),
    )(*operands)


def handed_out_kernel(*refs):
    count = len(refs) // 2
    for i in range(count):
        refs[count + i][...] = refs[i][...]


def handed_out(*results):
    vmem = pl.BlockSpec(memory_space=pltpu.VMEM)
    return pl.pallas_call(
        handed_out_kernel,
        out_shape=tuple(jax.ShapeDtypeStruct(result.shape, result.dtype) for result in results),
        in_specs=[vmem] * len(results),
        out_specs=(vmem,) * len(results),
        compiler_params=pltpu.CompilerParams(vmem_limit_bytes=60 * 1024 * 1024),
    )(*results)


def per_device(
    saved_input, cotangent, weight_in, weight_out, in_row_moment, in_col_moment, out_row_moment, out_col_moment
):
    input_grad, in_update, out_update_t, in_row, in_col, out_row, out_col = handed_out(*fused(
        saved_input, cotangent, weight_in, weight_out.T, in_row_moment.reshape(1, 64), in_col_moment.reshape(1, UNITS),
        out_row_moment.reshape(1, UNITS), out_col_moment.reshape(1, 64),
    ))
    return (
        input_grad, in_update, out_update_t.T, in_row.reshape(64), in_col.reshape(UNITS), out_row.reshape(UNITS),
        out_col.reshape(64),
    )


def solution(mesh):
    placed = (
        P(("dp", "row"), "col"), P(("dp", "row"), "col"), P("row", "col"), P("col", "row"),
        P("row"), P("col"), P("col"), P("row"),
    )
    return jax.shard_map(
        per_device,
        mesh=mesh,
        in_specs=placed,
        out_specs=(
            P(("dp", "row"), "col"), P("row", "col"), P("col", "row"), P("row"), P("col"), P("col"), P("row"),
        ),
        check_vma=False,
    )
```

```python
import jax
import jax.numpy as jnp
from jax import lax
from jax.experimental import pallas as pl
from jax.experimental.pallas import tpu as pltpu
from jax.sharding import PartitionSpec as P

MESH = pl.DeviceIdType.MESH
F32 = jnp.float32
BF16 = jnp.bfloat16

GELU_SCALE = 0.7978845608028654
GELU_CUBIC = 0.044715
MOMENT_DECAY = 0.8
CLIP_LIMIT = 1.0
EPSILON_SQ = 1e-30

TOK, WIDTH, UNITS, BLK = 384, 2048, 1024, 512
ALL_UNITS = 4096
ENTRIES = WIDTH * ALL_UNITS

CORE_G, STAGE1, STAGE2, DP, SUMS, SWAP, MOM = 0, 8, 20, 32, 40, 80, 82
W_SWAP, W_RING1, W_RING2, W_PART, LINE, BACK = 83, 85, 89, 105, 121, 133
N_SEM = 145
CHUNKS = ((0, 256), (256, 128), (0, 384))


def gelu_parts(values):
    inner = GELU_SCALE * (values + GELU_CUBIC * values * values * values)
    tangent = jnp.tanh(inner)
    output = 0.5 * values * (1.0 + tangent)
    slope = 0.5 * (1.0 + tangent) + 0.5 * values * (1.0 - tangent * tangent) * GELU_SCALE * (
        1.0 + 3.0 * GELU_CUBIC * values * values
    )
    return (output, slope)


def kernel(
    x_ref, cot_ref, win_ref, wout_ref, in_row_hbm, in_col_hbm, out_row_hbm, out_col_hbm,
    ig_ref, in_upd_ref, out_upd_ref, in_row_out, in_col_out, out_row_out, out_col_out,
    in_row_ref, in_col_ref, out_row_ref, out_col_ref, dmom_ref, full, w_ref, acc, tr, act, g_own, g_send, g_recv, s1, r1, s2, r2, dp_s, dp_z, dp_r, dmom_in,
    za, xa, zb, xb, ratio, swap_u, swap_v, back_s, back_r, it_own, ig_s,
    ss, rs, local,
):
    d = lax.axis_index("dp")
    r = lax.axis_index("row")
    c = lax.axis_index("col")
    core = lax.rem(r, 2)
    x = lax.rem(r // 2, 4)
    y = r // 8
    p1 = x + core * (y - x)
    p2 = y + core * (x - y)
    k1, k2 = 2 + 6 * core, 8 - 6 * core
    t1, t2 = 1 + 3 * core, 4 - 3 * core
    m = core
    other = 1 - core

    def ring(position, step):
        return lax.rem(position + step, 4)

    def rowdev(q1, q2):
        return {"row": q1 * k1 + q2 * k2 + core}

    partner = {"row": r + 1 - 2 * core}
    right1, left1 = rowdev(ring(p1, 1), p2), rowdev(ring(p1, 3), p2)
    right2, left2 = rowdev(p1, ring(p2, 1)), rowdev(p1, ring(p2, 3))
    up2 = {"dp": lax.rem(d + c // 2, 2), "col": ring(c, 2)}
    down2 = {"dp": lax.rem(d + 1 - c // 2, 2), "col": ring(c, 2)}

    chip = y * 4 + x

    def along_xy(k):
        return {"row": lax.rem(chip + k, 16) * 2 + core}

    def along_z(k):
        return {"col": ring(c, k)}

    def along_z_and_cores(k):
        place = lax.rem(core * 4 + c + k, 8)
        return {"row": r - core + place // 4, "col": lax.rem(place, 4)}

    barrier = pltpu.get_barrier_semaphore()
    peers = [{"dp": 1 - d, "col": ring(c, 2)}]
    peers += [along_z_and_cores(k) for k in range(1, 8)]
    peers += [along_xy(k) for k in range(1, 16)]
    for peer in peers:
        pl.semaphore_signal(barrier, inc=1, device_id=peer, device_id_type=MESH)

    def chip_rows(q1, q2):
        return pl.ds(pl.multiple_of((q1 * t1 + q2 * t2) * 128, 128), 128)

    def half_rows(q1, q2, h):
        return pl.ds(pl.multiple_of((q1 * t1 + q2 * t2) * 128 + h * 64, 64), 64)

    own_rows = half_rows(p1, p2, core)
    loads = [
        pltpu.make_async_copy(x_ref, full.at[0, c], local.at[0]),
        pltpu.make_async_copy(cot_ref, full.at[1, c], local.at[1]),
        pltpu.make_async_copy(win_ref, w_ref.at[0, own_rows, :], local.at[2]),
        pltpu.make_async_copy(wout_ref, w_ref.at[1, own_rows, :], local.at[3]),
        pltpu.make_async_copy(in_row_hbm, in_row_ref, local.at[5]),
        pltpu.make_async_copy(in_col_hbm, in_col_ref, local.at[6]),
        pltpu.make_async_copy(out_row_hbm, out_row_ref, local.at[7]),
        pltpu.make_async_copy(out_col_hbm, out_col_ref, local.at[8]),
    ]
    for copy in loads:
        copy.start()
    for copy in loads:
        copy.wait()
    for i, ref in enumerate((in_row_ref, out_col_ref)):
        dmom_ref[i] = jnp.broadcast_to(jnp.concatenate([ref[...], ref[...]], axis=1), (8, 128))
    pl.semaphore_wait(barrier, len(peers))

    def send(src, dst, number, device):
        copy = pltpu.make_async_remote_copy(
            src_ref=src, dst_ref=dst, send_sem=ss.at[number], recv_sem=rs.at[number],
            device_id=device, device_id_type=MESH,
        )
        copy.start()
        return copy

    pending = []

    def start(src, dst, number, device):
        copy = send(src, dst, number, device)
        pending.append(copy)
        return copy

    def arrived(dst, number):
        pltpu.make_async_remote_copy(
            src_ref=dst, dst_ref=dst, send_sem=ss.at[number], recv_sem=rs.at[number],
            device_id=partner, device_id_type=MESH,
        ).wait_recv()

    def line_number(leftward, k, j):
        return LINE + (leftward * 3 + k - 1) * 2 + j

    def line_copy(leftward, k, j):
        owner = c + (k - 1) if leftward else c - (k - 1)
        number = line_number(leftward, k, j)
        block = full.at[:, owner, pl.ds(*CHUNKS[j]), :]
        return pltpu.make_async_remote_copy(
            src_ref=block, dst_ref=block, send_sem=ss.at[number], recv_sem=rs.at[number],
            device_id={"col": ring(c, 3 if leftward else 1)}, device_id_type=MESH,
        )

    def line_sends(leftward, k):
        return (c > 0) & (c + (k - 1) <= 3) if leftward else (c < 3) & (c - (k - 1) >= 0)

    def line_gets(leftward, k):
        return c + k <= 3 if leftward else c - k >= 0

    def line_start(k, j):
        for leftward in (0, 1):
            @pl.when(line_sends(leftward, k))
            def _(leftward=leftward):
                line_copy(leftward, k, j).start()

    def hand_on(k, j):
        for leftward in (0, 1):
            @pl.when(line_gets(leftward, k))
            def _(leftward=leftward):
                owner = c + k if leftward else c - k
                arrived(full.at[:, owner, pl.ds(*CHUNKS[j]), :], line_number(leftward, k, j))

            if k < 3:
                @pl.when(line_sends(leftward, k + 1))
                def _(leftward=leftward):
                    line_copy(leftward, k + 1, j).start()

    line_start(1, 0)

    swaps = [start(w_ref.at[i, own_rows, :], w_ref.at[i, own_rows, :], W_SWAP + i, partner) for i in range(2)]
    mom = start(dmom_ref.at[other], dmom_in, MOM, partner)
    def weight_copy(q1, q2, number, device):
        block = w_ref.at[m, chip_rows(q1, q2), :]
        return start(block, block, number, device)

    def half_copy(q1, q2, h, number, device):
        block = w_ref.at[m, half_rows(q1, q2, h), :]
        return start(block, block, number, device)

    def second_ring(e):
        q1 = ring(p1, e)
        weight_copy(q1, p2, W_RING2 + e, right2)
        weight_copy(q1, p2, W_RING2 + 4 + e, left2)

    def second_ring_on(e):
        q1 = ring(p1, e)
        arrived(w_ref.at[m, chip_rows(q1, ring(p2, 3)), :], W_RING2 + e)
        half_copy(q1, ring(p2, 3), 0, W_RING2 + 8 + e, right2)
        arrived(w_ref.at[m, chip_rows(q1, ring(p2, 1)), :], W_RING2 + 4 + e)
        half_copy(q1, ring(p2, 1), 1, W_RING2 + 12 + e, left2)
        to_partner(e, 3)
        to_partner(e, 1)

    def to_partner(e, f):
        weight_copy(ring(p1, e), ring(p2, f), W_PART + 4 * e + f, partner)

    for i in range(2):
        swaps[i].wait_recv()
    weight_copy(p1, p2, W_RING1, right1)
    weight_copy(p1, p2, W_RING1 + 1, left1)
    second_ring(0)

    def transposed(b, j):
        first, count = CHUNKS[j]
        for i in range(2):
            for n in range(4):
                tr[i, b * 4 + n, :, first:first + count] = full[i, b, first:first + count, n * 128:(n + 1) * 128].T

    transposed(c, 0)
    arrived(w_ref.at[m, chip_rows(ring(p1, 3), p2), :], W_RING1)
    half_copy(ring(p1, 3), p2, 0, W_RING1 + 2, right1)
    arrived(w_ref.at[m, chip_rows(ring(p1, 1), p2), :], W_RING1 + 1)
    half_copy(ring(p1, 1), p2, 1, W_RING1 + 3, left1)
    second_ring(3)
    second_ring(1)
    to_partner(3, 0)
    to_partner(1, 0)
    second_ring_on(0)
    line_start(1, 1)
    hand_on(1, 0)
    for h in range(2):
        arrived(w_ref.at[m, half_rows(ring(p1, 2), p2, h), :], W_RING1 + 2 + h)
    second_ring(2)
    to_partner(2, 0)
    transposed(c, 1)
    second_ring_on(3)
    second_ring_on(1)
    hand_on(1, 1)
    second_ring_on(2)

    def both_sides(k, j, *work):
        for owner, there in ((c - k, c - k >= 0), (c + k, c + k <= 3)):
            @pl.when(there)
            def _(owner=owner):
                for part in work:
                    part(owner, j)

    hand_on(2, 0)
    both_sides(1, 0, transposed)
    for e in (0, 3, 1, 2):
        for h in range(2):
            arrived(w_ref.at[m, half_rows(ring(p1, e), ring(p2, 2), h), :], W_RING2 + 8 + 4 * h + e)
        to_partner(e, 2)
    both_sides(1, 1, transposed)
    both_sides(2, 0, transposed)

    def products(b, j, first=False):
        part = pl.ds(pl.multiple_of(b * BLK, BLK), BLK)
        rows = pl.ds(*CHUNKS[j])

        @pl.loop(0, 4, unroll=2)
        def _(n):
            cols = pl.ds(pl.multiple_of(n * 256, 256), 256)
            for i in range(2):
                value = jnp.dot(full[i, b, rows, :], w_ref[i, part, cols], preferred_element_type=F32)
                if first:
                    acc[i, rows, cols] = value
                else:
                    acc[i, rows, cols] += value

    def activate(j):
        rows = pl.ds(*CHUNKS[j])

        @pl.loop(0, 4)
        def _(n):
            cols = pl.ds(pl.multiple_of(n * 256, 256), 256)
            output, slope = gelu_parts(acc[0, rows, cols])
            act[1, rows, cols] = output.astype(BF16)
            act[0, rows, cols] = (acc[1, rows, cols] * slope).astype(BF16)

    def terms(t, j, store):
        rows = pl.ds(*CHUNKS[j])

        @pl.loop(0, 2, unroll=True)
        def _(n):
            inner = pl.ds(pl.multiple_of(n * 256, 256), 256)
            part = pl.ds(pl.multiple_of(t * BLK + n * 256, 256), 256)
            store(inner, lax.dot_general(
                act[0, rows, :], w_ref[0, part, :], (((1,), (1,)), ((), ())), preferred_element_type=F32))

    def keep_mine(first_row, count):
        def keep(inner, value):
            it_own[first_row:first_row + count, inner] = value
        return keep

    def back_copy(leftward, k, j):
        rows = pl.ds(*CHUNKS[j])
        number = BACK + (leftward * 3 + k - 1) * 2 + j
        return pltpu.make_async_remote_copy(
            src_ref=back_s.at[leftward, k - 1, rows, :], dst_ref=back_r.at[leftward, k - 1, rows, :],
            send_sem=ss.at[number], recv_sem=rs.at[number],
            device_id={"col": ring(c, 3 if leftward else 1)}, device_id_type=MESH,
        )

    def back_arrived(leftward, k, j):
        arrived(back_r.at[leftward, k, pl.ds(*CHUNKS[j]), :], BACK + (leftward * 3 + k) * 2 + j)

    def back_first(k, j):
        rows = pl.ds(*CHUNKS[j])
        for leftward in (0, 1):
            @pl.when(c == (3 if leftward else 0))
            def _(leftward=leftward):
                def keep(inner, value):
                    back_s[leftward, k - 1, rows, inner] = value.astype(BF16)

                terms(c - k if leftward else c + k, j, keep)
                back_copy(leftward, k, j).start()

    def back_on(k, j):
        rows = pl.ds(*CHUNKS[j])
        for leftward in (0, 1):
            sends = (c < 3) & (c - k >= 0) if leftward else (c > 0) & (c + k <= 3)

            @pl.when(sends)
            def _(leftward=leftward):
                back_arrived(leftward, k, j)

                def keep(inner, value):
                    back_s[leftward, k - 1, rows, inner] = (
                        value + back_r[leftward, k, rows, inner].astype(F32)).astype(BF16)

                terms(c - k if leftward else c + k, j, keep)
                back_copy(leftward, k, j).start()

    for e in range(4):
        for f in range(4):
            if e or f:
                there = pl.ds(pl.multiple_of((ring(p2, e) * t2 + ring(p1, f) * t1) * 128, 128), 128)
                arrived(w_ref.at[other, there, :], W_PART + 4 * e + f)
    products(c, 2, first=True)
    hand_on(2, 1)
    both_sides(1, 2, products)
    both_sides(2, 1, transposed)
    both_sides(2, 2, products)
    hand_on(3, 0)
    both_sides(3, 0, products)
    activate(0)
    for k in (3, 2, 1):
        back_first(k, 0)
    both_sides(3, 0, transposed)
    hand_on(3, 1)
    both_sides(3, 1, products)
    activate(1)
    both_sides(3, 1, transposed)

    offsets = (2, 1, 3, 0)

    def group_product(matrix, chips, piece, store):
        lhs = jnp.concatenate([tr[matrix, chip] for chip in chips], axis=0)

        @pl.loop(2 * piece, 2 * piece + 2, unroll=True)
        def _(n):
            cols = pl.ds(pl.multiple_of(n * 256, 256), 256)
            store(n, jnp.dot(lhs, act[matrix, :, cols], preferred_element_type=F32))

    core_copies = {}

    def group_theirs(piece, g):
        theirs = ring(p2, offsets[g])

        def keep_sent(n, value):
            g_send[g, n] = value.astype(BF16)

        group_product(other, [theirs * t2 + q * t1 for q in range(4)], piece, keep_sent)
        pair = pl.ds(2 * piece, 2)
        core_copies[piece, g] = start(g_send.at[g, pair], g_recv.at[g, pair], CORE_G + 2 * g + piece, partner)

    def group_own(piece, g):
        mine = ring(p1, offsets[g])

        def keep_own(n, value):
            g_own[g, n] = value

        group_product(m, [mine * t1 + q * t2 for q in range(4)], piece, keep_own)

    def reduced(dst, parts, rows):
        @pl.loop(0, rows // 128, unroll=True)
        def _(i):
            at = pl.ds(pl.multiple_of(i * 128, 128), 128)
            total = parts[0][at, :].astype(F32)
            for part in parts[1:]:
                total += part[at, :].astype(F32)
            dst[at, :] = total.astype(dst.dtype)

    ring1 = {}

    def chip_sum(g, n):
        return [g_own.at[g, n], g_recv.at[g, n]]

    def ring1_send(piece, g, h, which, device, extra=()):
        n = 2 * piece + h
        if (piece, g) == (0, 0):
            reduced(s1.at[g, n], chip_sum(g, n), BLK)
        else:
            mine = ring(p1, offsets[g])
            lhs = jnp.concatenate([tr[m, mine * t1 + q * t2] for q in range(4)], axis=0)
            total = jnp.dot(lhs, act[m, :, n * 256:(n + 1) * 256], preferred_element_type=F32)
            for part in [g_recv.at[g, n]] + list(extra):
                total += part[...].astype(F32)
            s1[g, n] = total.astype(BF16)
        ring1[piece, which] = start(s1.at[g, n], r1.at[which, piece], STAGE1 + 2 * which + piece, device)

    def first(piece):
        core_copies[piece, 0].wait_recv()
        ring1_send(piece, 0, 0, 0, right1)
        ring1_send(piece, 0, 1, 1, left1)

    def second(piece):
        core_copies[piece, 1].wait_recv()
        ring1_send(piece, 1, 1, 3, right1)
        core_copies[piece, 2].wait_recv()
        ring1_send(piece, 2, 0, 4, left1)

    def third(piece):
        ring1[piece, 0].wait_recv()
        ring1_send(piece, 1, 0, 2, right1, [r1.at[0, piece]])
        ring1[piece, 1].wait_recv()
        ring1_send(piece, 2, 1, 5, left1, [r1.at[1, piece]])

    ring2 = {}
    opp, nxt, prv = ring(p2, 2), ring(p2, 1), ring(p2, 3)

    def block(q, piece, h):
        at = pl.ds(pl.multiple_of(q * 128, 128), 128)
        return [
            ref.at[at, :] for ref in chip_sum(3, 2 * piece + h) + [r1.at[2 + h, piece], r1.at[4 + h, piece]]
        ]

    def ring2_send(piece, g, h, which, device, extra=()):
        n = 2 * piece + h
        reduced(s2.at[g, n], block((opp, nxt, prv)[g], piece, h) + list(extra), 128)
        ring2[piece, which] = start(s2.at[g, n], r2.at[which, piece], STAGE2 + 2 * which + piece, device)

    def ring2_first(piece):
        core_copies[piece, 3].wait_recv()
        for which in (3, 4, 2, 5):
            ring1[piece, which].wait_recv()
        ring2_send(piece, 0, 0, 0, right2)
        ring2_send(piece, 0, 1, 1, left2)
        ring2_send(piece, 1, 1, 3, right2)
        ring2_send(piece, 2, 0, 4, left2)

    def ring2_second(piece):
        ring2[piece, 0].wait_recv()
        ring2_send(piece, 1, 0, 2, right2, [r2.at[0, piece]])
        ring2[piece, 1].wait_recv()
        ring2_send(piece, 2, 1, 5, left2, [r2.at[1, piece]])

    travel = {}

    def dp_first(piece):
        for h, device in ((0, up2), (1, down2)):
            n = 2 * piece + h
            ring2[piece, 2 + h].wait_recv()
            ring2[piece, 4 + h].wait_recv()
            reduced(dp_s.at[n], block(p2, piece, h) + [r2.at[2 + h, piece], r2.at[4 + h, piece]], 128)
            travel[0, n] = start(dp_s.at[n], dp_z.at[n], DP + n, device)

    def dp_second(piece):
        for h, device in ((0, up2), (1, down2)):
            n = 2 * piece + h
            travel[0, n].wait_recv()
            travel[1, n] = start(dp_z.at[n], dp_r.at[n], DP + 4 + n, device)

    group_theirs(0, 0)
    group_theirs(0, 1)
    group_own(0, 0)
    group_theirs(0, 2)
    group_theirs(1, 0)
    first(0)
    second(0)
    for k in (3, 2, 1):
        back_first(k, 1)
    third(0)
    group_theirs(1, 1)
    first(1)
    group_theirs(1, 2)
    second(1)
    group_theirs(0, 3)
    group_own(0, 3)
    ring2_first(0)
    group_theirs(1, 3)
    group_own(1, 3)
    third(1)
    ring2_second(0)
    back_on(2, 0)
    dp_first(0)
    ring2_first(1)
    back_on(1, 0)
    ring2_second(1)
    back_on(2, 1)
    dp_second(0)
    dp_first(1)
    back_on(1, 1)
    dp_second(1)

    def across_start(place, number, count, device, value):
        place[...] = value
        return [start(place, place, number + k - 1, device(k)) for k in range(1, count + 1)]

    def added(values):
        while len(values) > 1:
            values = [values[i] + values[i + 1] for i in range(0, len(values), 2)]
        return values[0]

    def across_end(copies):
        for copy in copies:
            copy.wait_recv()

    mom.wait_recv()
    lane = lax.broadcasted_iota(jnp.int32, (8, 128), 1)
    old_d = jnp.where((lane // 64) == core, dmom_ref[m], dmom_in[...])[0:1, :]
    old_f = jnp.where(core == 0, in_col_ref[...], out_row_ref[...])
    old_f_sum = jnp.sum(old_f, axis=1, keepdims=True)
    old_d_sum = jnp.sum(old_d, axis=1, keepdims=True)
    col_sums = []
    lanes = None
    for n in range(4):
        travel[1, n].wait_recv()
        grad = dp_s[n].astype(F32) + dp_r[n].astype(F32)
        ratio[n] = grad
        squared = grad * grad
        col_sums.append(jnp.sum(squared, axis=0, keepdims=True))
        folded = squared[:, 0:128] + squared[:, 128:256]
        lanes = folded if n == 0 else lanes + folded
    sub = lax.broadcasted_iota(jnp.int32, (8, 256), 0)
    payload = jnp.where(sub == 4, old_d_sum, 0.0)
    for n in range(4):
        payload = jnp.where(sub == n, col_sums[n], payload)
    sent_xy = across_start(xa.at[chip], SUMS, 15, along_xy, payload)
    row_sums = jnp.sum(lanes.T, axis=0, keepdims=True)
    total = jnp.sum(row_sums, axis=1, keepdims=True)
    sub = lax.broadcasted_iota(jnp.int32, (8, 128), 0)
    sent_z = across_start(za.at[c], SUMS + 15, 3, along_z, jnp.where(sub == 0, row_sums, old_f_sum))
    terms(c, 2, keep_mine(*CHUNKS[2]))
    across_end(sent_z)
    over_z = added([za[i] for i in range(4)])
    d_new = MOMENT_DECAY * old_d + (1.0 - MOMENT_DECAY) * (over_z[0:1, :] / ALL_UNITS + EPSILON_SQ)
    d_column = jnp.broadcast_to(1.0 / jnp.sqrt(d_new), (128, 128)).T[:, 0:1]
    across_end(sent_xy)
    over_xy = added([xa[i] for i in range(16)])
    old_mean = jnp.where(core == 0, over_xy[4:5, 0:1] / WIDTH, over_z[1:2, 0:1] / ALL_UNITS)
    f_new = [
        MOMENT_DECAY * old_f[:, n * 256:(n + 1) * 256]
        + (1.0 - MOMENT_DECAY) * (over_xy[n:n + 1, :] / WIDTH + EPSILON_SQ)
        for n in range(4)
    ]
    lanes = None
    for n in range(4):
        value = ratio[n] * (d_column * (1.0 / jnp.sqrt(f_new[n])))
        ratio[n] = value
        folded = value[:, 0:128] * value[:, 0:128] + value[:, 128:256] * value[:, 128:256]
        lanes = folded if n == 0 else lanes + folded
    folded = lanes[0:8]
    for i in range(1, 16):
        folded += lanes[i * 8:(i + 1) * 8]
    payload = jnp.concatenate([folded, jnp.where(sub == 0, total, old_mean)], axis=0)
    sent_z = across_start(zb.at[core, c], SUMS + 18, 7, along_z_and_cores, payload)

    theirs_at = pl.ds(pl.multiple_of(other * 64, 64), 64)
    swap_v[0] = jnp.zeros((8, UNITS), F32)
    for n in range(4):
        swap_u[0, :, n * 256:(n + 1) * 256] = ratio[n, theirs_at, :]
        swap_v[0, 0:1, n * 256:(n + 1) * 256] = f_new[n]
    swap_v[0, 1:2, 0:128] = d_new
    sent_u = start(swap_u.at[0], swap_u.at[1], SWAP, partner)
    sent_v = start(swap_v.at[0], swap_v.at[1], SWAP + 1, partner)

    for leftward in (0, 1):
        @pl.when((c < 3) if leftward else (c > 0))
        def _(leftward=leftward):
            for j in range(2):
                back_arrived(leftward, 0, j)
            reduced(it_own, [it_own, back_r.at[leftward, 0]], TOK)

    reduced(ig_s, [it_own], TOK)
    ig_out = pltpu.make_async_copy(ig_s, ig_ref, local.at[4])
    ig_out.start()

    across_end(sent_z)
    payload = jnp.stack([added([zb[i, j] for j in range(4)]) for i in range(2)])
    sent_xy = across_start(xb.at[chip], SUMS + 25, 15, along_xy, payload)
    across_end(sent_xy)
    factors = []
    for i in range(2):
        over_all = added([xb[j, i] for j in range(16)])
        mean = MOMENT_DECAY * (over_all[9:10, 0:1] / 64.0) + (1.0 - MOMENT_DECAY) * (
            over_all[8:9, 0:1] / ENTRIES + EPSILON_SQ)
        rms = jnp.sqrt(mean * (jnp.sum(over_all[0:8], keepdims=True) / ENTRIES))
        factors.append(jnp.sqrt(mean) / jnp.maximum(1.0, rms / CLIP_LIMIT))

    def own_lanes(value):
        return jnp.where(core == 0, value[:, 0:64], value[:, 64:128])

    sent_v.wait_recv()
    sent_u.wait_recv()

    def finish(update, row_of, d_out, f_out, which, scale):
        d_out[...] = own_lanes(swap_v[which, 1:2, 0:128])
        f_out[...] = swap_v[which, 0:1, :]
        for n in range(4):
            update[:, n * 256:(n + 1) * 256] = row_of(n) * scale

    def theirs(n):
        return swap_u[1, :, n * 256:(n + 1) * 256]

    @pl.when(core == 0)
    def _():
        finish(in_upd_ref, lambda n: ratio[n, 0:64, :], in_row_out, in_col_out, 0, factors[0])
        finish(out_upd_ref, theirs, out_col_out, out_row_out, 1, factors[1])

    @pl.when(core == 1)
    def _():
        finish(out_upd_ref, lambda n: ratio[n, 64:128, :], out_col_out, out_row_out, 0, factors[1])
        finish(in_upd_ref, theirs, in_row_out, in_col_out, 1, factors[0])

    ig_out.wait()
    for copy in pending:
        copy.wait_send()
    for leftward in (0, 1):
        for k in (1, 2, 3):
            @pl.when(line_sends(leftward, k))
            def _(leftward=leftward, k=k):
                for j in range(2):
                    line_copy(leftward, k, j).wait_send()

            @pl.when((c - k >= 0) if leftward else (c + k <= 3))
            def _(leftward=leftward, k=k):
                for j in range(2):
                    back_copy(leftward, k, j).wait_send()


def fused(*operands):
    vmem = pl.BlockSpec(memory_space=pltpu.VMEM)
    anywhere = pl.BlockSpec(memory_space=pl.ANY)
    return pl.pallas_call(
        kernel,
        out_shape=(
            jax.ShapeDtypeStruct((TOK, BLK), BF16),
            jax.ShapeDtypeStruct((64, UNITS), F32),
            jax.ShapeDtypeStruct((64, UNITS), F32),
            jax.ShapeDtypeStruct((1, 64), F32),
            jax.ShapeDtypeStruct((1, UNITS), F32),
            jax.ShapeDtypeStruct((1, UNITS), F32),
            jax.ShapeDtypeStruct((1, 64), F32),
        ),
        in_specs=[anywhere] * 8,
        out_specs=(anywhere,) + (vmem,) * 6,
        scratch_shapes=[
            pltpu.VMEM((1, 64), F32),
            pltpu.VMEM((1, UNITS), F32),
            pltpu.VMEM((1, UNITS), F32),
            pltpu.VMEM((1, 64), F32),
            pltpu.VMEM((2, 8, 128), F32),
            pltpu.VMEM((2, 4, TOK, BLK), BF16),
            pltpu.VMEM((2, WIDTH, UNITS), BF16),
            pltpu.VMEM((2, TOK, UNITS), F32),
            pltpu.VMEM((2, 16, 128, TOK), BF16),
            pltpu.VMEM((2, TOK, UNITS), BF16),
            pltpu.VMEM((4, 4, 512, 256), F32),
            pltpu.VMEM((4, 4, 512, 256), BF16),
            pltpu.VMEM((4, 4, 512, 256), BF16),
            pltpu.VMEM((3, 4, 512, 256), BF16),
            pltpu.VMEM((6, 2, 512, 256), BF16),
            pltpu.VMEM((3, 4, 128, 256), BF16),
            pltpu.VMEM((6, 2, 128, 256), BF16),
            pltpu.VMEM((4, 128, 256), BF16),
            pltpu.VMEM((4, 128, 256), BF16),
            pltpu.VMEM((4, 128, 256), BF16),
            pltpu.VMEM((8, 128), F32),
            pltpu.VMEM((4, 8, 128), F32),
            pltpu.VMEM((16, 8, 256), F32),
            pltpu.VMEM((2, 4, 16, 128), F32),
            pltpu.VMEM((16, 2, 16, 128), F32),
            pltpu.VMEM((4, 128, 256), F32),
            pltpu.VMEM((2, 64, UNITS), F32),
            pltpu.VMEM((2, 8, UNITS), F32),
            pltpu.VMEM((2, 3, TOK, BLK), BF16),
            pltpu.VMEM((2, 3, TOK, BLK), BF16),
            pltpu.VMEM((TOK, BLK), F32),
            pltpu.VMEM((TOK, BLK), BF16),
            pltpu.SemaphoreType.DMA((N_SEM,)),
            pltpu.SemaphoreType.DMA((N_SEM,)),
            pltpu.SemaphoreType.DMA((9,)),
        ],
        compiler_params=pltpu.CompilerParams(
            collective_id=0, has_side_effects=True, vmem_limit_bytes=60 * 1024 * 1024
        ),
        cost_estimate=pl.CostEstimate(
            flops=10 * TOK * WIDTH * UNITS, bytes_accessed=16 * 2**20, transcendentals=TOK * UNITS
        ),
    )(*operands)


def handed_out_kernel(*refs):
    count = len(refs) // 2
    for i in range(count):
        refs[count + i][...] = refs[i][...]


def handed_out(*results):
    vmem = pl.BlockSpec(memory_space=pltpu.VMEM)
    return pl.pallas_call(
        handed_out_kernel,
        out_shape=tuple(jax.ShapeDtypeStruct(result.shape, result.dtype) for result in results),
        in_specs=[vmem] * len(results),
        out_specs=(vmem,) * len(results),
        compiler_params=pltpu.CompilerParams(vmem_limit_bytes=60 * 1024 * 1024),
    )(*results)


def per_device(
    saved_input, cotangent, weight_in, weight_out, in_row_moment, in_col_moment, out_row_moment, out_col_moment
):
    input_grad, in_update, out_update_t, in_row, in_col, out_row, out_col = handed_out(*fused(
        saved_input, cotangent, weight_in, weight_out.T, in_row_moment.reshape(1, 64), in_col_moment.reshape(1, UNITS),
        out_row_moment.reshape(1, UNITS), out_col_moment.reshape(1, 64),
    ))
    return (
        input_grad, in_update, out_update_t.T, in_row.reshape(64), in_col.reshape(UNITS), out_row.reshape(UNITS),
        out_col.reshape(64),
    )


def solution(mesh):
    placed = (
        P(("dp", "row"), "col"), P(("dp", "row"), "col"), P("row", "col"), P("col", "row"),
        P("row"), P("col"), P("col"), P("row"),
    )
    return jax.shard_map(
        per_device,
        mesh=mesh,
        in_specs=placed,
        out_specs=(
            P(("dp", "row"), "col"), P("row", "col"), P("col", "row"), P("row"), P("col"), P("col"), P("row"),
        ),
        check_vma=False,
    )
```

```python
import jax
import jax.numpy as jnp
from jax import lax
from jax.experimental import pallas as pl
from jax.experimental.pallas import tpu as pltpu
from jax.sharding import PartitionSpec as P

MESH = pl.DeviceIdType.MESH
F32 = jnp.float32
BF16 = jnp.bfloat16

GELU_SCALE = 0.7978845608028654
GELU_CUBIC = 0.044715
MOMENT_DECAY = 0.8
CLIP_LIMIT = 1.0
EPSILON_SQ = 1e-30

TOK, WIDTH, UNITS, BLK = 384, 2048, 1024, 512
ALL_UNITS = 4096
ENTRIES = WIDTH * ALL_UNITS

CORE_G, STAGE1, STAGE2, DP, SUMS, SWAP, MOM = 0, 8, 20, 32, 40, 80, 82
W_SWAP, W_RING1, W_RING2, W_PART, LINE, BACK = 83, 85, 89, 105, 121, 133
N_SEM = 145
CHUNKS = ((0, 256), (256, 128), (0, 384))


def gelu_parts(values):
    inner = GELU_SCALE * (values + GELU_CUBIC * values * values * values)
    tangent = jnp.tanh(inner)
    output = 0.5 * values * (1.0 + tangent)
    slope = 0.5 * (1.0 + tangent) + 0.5 * values * (1.0 - tangent * tangent) * GELU_SCALE * (
        1.0 + 3.0 * GELU_CUBIC * values * values
    )
    return (output, slope)


def kernel(
    x_ref, cot_ref, win_ref, wout_ref, in_row_hbm, in_col_hbm, out_row_hbm, out_col_hbm,
    ig_ref, in_upd_ref, out_upd_ref, in_row_out, in_col_out, out_row_out, out_col_out,
    in_row_ref, in_col_ref, out_row_ref, out_col_ref, dmom_ref, full, w_ref, acc, tr, act, g_own, g_send, g_recv, s1, r1, s2, r2, dp_s, dp_z, dp_r, dmom_in,
    za, xa, zb, xb, ratio, swap_u, swap_v, back_s, back_r, it_own, ig_s,
    ss, rs, local,
):
    d = lax.axis_index("dp")
    r = lax.axis_index("row")
    c = lax.axis_index("col")
    core = lax.rem(r, 2)
    x = lax.rem(r // 2, 4)
    y = r // 8
    p1 = x + core * (y - x)
    p2 = y + core * (x - y)
    k1, k2 = 2 + 6 * core, 8 - 6 * core
    t1, t2 = 1 + 3 * core, 4 - 3 * core
    m = core
    other = 1 - core

    def ring(position, step):
        return lax.rem(position + step, 4)

    def rowdev(q1, q2):
        return {"row": q1 * k1 + q2 * k2 + core}

    partner = {"row": r + 1 - 2 * core}
    right1, left1 = rowdev(ring(p1, 1), p2), rowdev(ring(p1, 3), p2)
    right2, left2 = rowdev(p1, ring(p2, 1)), rowdev(p1, ring(p2, 3))
    up2 = {"dp": lax.rem(d + c // 2, 2), "col": ring(c, 2)}
    down2 = {"dp": lax.rem(d + 1 - c // 2, 2), "col": ring(c, 2)}

    chip = y * 4 + x

    def along_xy(k):
        return {"row": lax.rem(chip + k, 16) * 2 + core}

    def along_z(k):
        return {"col": ring(c, k)}

    def along_z_and_cores(k):
        place = lax.rem(core * 4 + c + k, 8)
        return {"row": r - core + place // 4, "col": lax.rem(place, 4)}

    barrier = pltpu.get_barrier_semaphore()
    peers = [{"dp": 1 - d, "col": ring(c, 2)}]
    peers += [along_z_and_cores(k) for k in range(1, 8)]
    peers += [along_xy(k) for k in range(1, 16)]
    def chip_rows(q1, q2):
        return pl.ds(pl.multiple_of((q1 * t1 + q2 * t2) * 128, 128), 128)

    def half_rows(q1, q2, h):
        return pl.ds(pl.multiple_of((q1 * t1 + q2 * t2) * 128 + h * 64, 64), 64)

    own_rows = half_rows(p1, p2, core)
    loads = [
        pltpu.make_async_copy(x_ref, full.at[0, c], local.at[0]),
        pltpu.make_async_copy(cot_ref, full.at[1, c], local.at[1]),
        pltpu.make_async_copy(win_ref, w_ref.at[0, own_rows, :], local.at[2]),
        pltpu.make_async_copy(wout_ref, w_ref.at[1, own_rows, :], local.at[3]),
        pltpu.make_async_copy(in_row_hbm, in_row_ref, local.at[5]),
        pltpu.make_async_copy(in_col_hbm, in_col_ref, local.at[6]),
        pltpu.make_async_copy(out_row_hbm, out_row_ref, local.at[7]),
        pltpu.make_async_copy(out_col_hbm, out_col_ref, local.at[8]),
    ]
    for copy in loads[:4]:
        copy.start()
    for peer in peers:
        pl.semaphore_signal(barrier, inc=1, device_id=peer, device_id_type=MESH)
    for copy in loads[4:]:
        copy.start()
    for copy in loads:
        copy.wait()
    for i, ref in enumerate((in_row_ref, out_col_ref)):
        dmom_ref[i] = jnp.broadcast_to(jnp.concatenate([ref[...], ref[...]], axis=1), (8, 128))
    pl.semaphore_wait(barrier, len(peers))

    def send(src, dst, number, device):
        copy = pltpu.make_async_remote_copy(
            src_ref=src, dst_ref=dst, send_sem=ss.at[number], recv_sem=rs.at[number],
            device_id=device, device_id_type=MESH,
        )
        copy.start()
        return copy

    pending = []

    def start(src, dst, number, device):
        copy = send(src, dst, number, device)
        pending.append(copy)
        return copy

    def arrived(dst, number):
        pltpu.make_async_remote_copy(
            src_ref=dst, dst_ref=dst, send_sem=ss.at[number], recv_sem=rs.at[number],
            device_id=partner, device_id_type=MESH,
        ).wait_recv()

    def line_number(leftward, k, j):
        return LINE + (leftward * 3 + k - 1) * 2 + j

    def line_copy(leftward, k, j):
        owner = c + (k - 1) if leftward else c - (k - 1)
        number = line_number(leftward, k, j)
        block = full.at[:, owner, pl.ds(*CHUNKS[j]), :]
        return pltpu.make_async_remote_copy(
            src_ref=block, dst_ref=block, send_sem=ss.at[number], recv_sem=rs.at[number],
            device_id={"col": ring(c, 3 if leftward else 1)}, device_id_type=MESH,
        )

    def line_sends(leftward, k):
        return (c > 0) & (c + (k - 1) <= 3) if leftward else (c < 3) & (c - (k - 1) >= 0)

    def line_gets(leftward, k):
        return c + k <= 3 if leftward else c - k >= 0

    def line_start(k, j):
        for leftward in (0, 1):
            @pl.when(line_sends(leftward, k))
            def _(leftward=leftward):
                line_copy(leftward, k, j).start()

    def hand_on(k, j):
        for leftward in (0, 1):
            @pl.when(line_gets(leftward, k))
            def _(leftward=leftward):
                owner = c + k if leftward else c - k
                arrived(full.at[:, owner, pl.ds(*CHUNKS[j]), :], line_number(leftward, k, j))

            if k < 3:
                @pl.when(line_sends(leftward, k + 1))
                def _(leftward=leftward):
                    line_copy(leftward, k + 1, j).start()

    line_start(1, 0)

    swaps = [start(w_ref.at[i, own_rows, :], w_ref.at[i, own_rows, :], W_SWAP + i, partner) for i in range(2)]
    mom = start(dmom_ref.at[other], dmom_in, MOM, partner)
    def weight_copy(q1, q2, number, device):
        block = w_ref.at[m, chip_rows(q1, q2), :]
        return start(block, block, number, device)

    def half_copy(q1, q2, h, number, device):
        block = w_ref.at[m, half_rows(q1, q2, h), :]
        return start(block, block, number, device)

    def second_ring(e):
        q1 = ring(p1, e)
        weight_copy(q1, p2, W_RING2 + e, right2)
        weight_copy(q1, p2, W_RING2 + 4 + e, left2)

    def second_ring_on(e):
        q1 = ring(p1, e)
        arrived(w_ref.at[m, chip_rows(q1, ring(p2, 3)), :], W_RING2 + e)
        half_copy(q1, ring(p2, 3), 0, W_RING2 + 8 + e, right2)
        arrived(w_ref.at[m, chip_rows(q1, ring(p2, 1)), :], W_RING2 + 4 + e)
        half_copy(q1, ring(p2, 1), 1, W_RING2 + 12 + e, left2)
        to_partner(e, 3)
        to_partner(e, 1)

    def to_partner(e, f):
        weight_copy(ring(p1, e), ring(p2, f), W_PART + 4 * e + f, partner)

    for i in range(2):
        swaps[i].wait_recv()
    weight_copy(p1, p2, W_RING1, right1)
    weight_copy(p1, p2, W_RING1 + 1, left1)
    second_ring(0)

    def transposed(b, j):
        first, count = CHUNKS[j]
        for i in range(2):
            for n in range(4):
                tr[i, b * 4 + n, :, first:first + count] = full[i, b, first:first + count, n * 128:(n + 1) * 128].T

    transposed(c, 0)
    arrived(w_ref.at[m, chip_rows(ring(p1, 3), p2), :], W_RING1)
    half_copy(ring(p1, 3), p2, 0, W_RING1 + 2, right1)
    arrived(w_ref.at[m, chip_rows(ring(p1, 1), p2), :], W_RING1 + 1)
    half_copy(ring(p1, 1), p2, 1, W_RING1 + 3, left1)
    second_ring(3)
    second_ring(1)
    to_partner(3, 0)
    to_partner(1, 0)
    second_ring_on(0)
    line_start(1, 1)
    hand_on(1, 0)
    for h in range(2):
        arrived(w_ref.at[m, half_rows(ring(p1, 2), p2, h), :], W_RING1 + 2 + h)
    second_ring(2)
    to_partner(2, 0)
    transposed(c, 1)
    second_ring_on(3)
    second_ring_on(1)
    hand_on(1, 1)
    second_ring_on(2)

    def both_sides(k, j, *work):
        for owner, there in ((c - k, c - k >= 0), (c + k, c + k <= 3)):
            @pl.when(there)
            def _(owner=owner):
                for part in work:
                    part(owner, j)

    hand_on(2, 0)
    both_sides(1, 0, transposed)
    for e in (0, 3, 1, 2):
        for h in range(2):
            arrived(w_ref.at[m, half_rows(ring(p1, e), ring(p2, 2), h), :], W_RING2 + 8 + 4 * h + e)
        to_partner(e, 2)
    both_sides(1, 1, transposed)
    both_sides(2, 0, transposed)

    def products(b, j, first=False):
        part = pl.ds(pl.multiple_of(b * BLK, BLK), BLK)
        rows = pl.ds(*CHUNKS[j])

        @pl.loop(0, 4, unroll=2)
        def _(n):
            cols = pl.ds(pl.multiple_of(n * 256, 256), 256)
            for i in range(2):
                value = jnp.dot(full[i, b, rows, :], w_ref[i, part, cols], preferred_element_type=F32)
                if first:
                    acc[i, rows, cols] = value
                else:
                    acc[i, rows, cols] += value

    def activate(j):
        rows = pl.ds(*CHUNKS[j])

        @pl.loop(0, 4)
        def _(n):
            cols = pl.ds(pl.multiple_of(n * 256, 256), 256)
            output, slope = gelu_parts(acc[0, rows, cols])
            act[1, rows, cols] = output.astype(BF16)
            act[0, rows, cols] = (acc[1, rows, cols] * slope).astype(BF16)

    def terms(t, j, store):
        rows = pl.ds(*CHUNKS[j])

        @pl.loop(0, 2, unroll=True)
        def _(n):
            inner = pl.ds(pl.multiple_of(n * 256, 256), 256)
            part = pl.ds(pl.multiple_of(t * BLK + n * 256, 256), 256)
            store(inner, lax.dot_general(
                act[0, rows, :], w_ref[0, part, :], (((1,), (1,)), ((), ())), preferred_element_type=F32))

    def keep_mine(first_row, count):
        def keep(inner, value):
            it_own[first_row:first_row + count, inner] = value
        return keep

    def back_copy(leftward, k, j):
        rows = pl.ds(*CHUNKS[j])
        number = BACK + (leftward * 3 + k - 1) * 2 + j
        return pltpu.make_async_remote_copy(
            src_ref=back_s.at[leftward, k - 1, rows, :], dst_ref=back_r.at[leftward, k - 1, rows, :],
            send_sem=ss.at[number], recv_sem=rs.at[number],
            device_id={"col": ring(c, 3 if leftward else 1)}, device_id_type=MESH,
        )

    def back_arrived(leftward, k, j):
        arrived(back_r.at[leftward, k, pl.ds(*CHUNKS[j]), :], BACK + (leftward * 3 + k) * 2 + j)

    def back_first(k, j):
        rows = pl.ds(*CHUNKS[j])
        for leftward in (0, 1):
            @pl.when(c == (3 if leftward else 0))
            def _(leftward=leftward):
                def keep(inner, value):
                    back_s[leftward, k - 1, rows, inner] = value.astype(BF16)

                terms(c - k if leftward else c + k, j, keep)
                back_copy(leftward, k, j).start()

    def back_on(k, j):
        rows = pl.ds(*CHUNKS[j])
        for leftward in (0, 1):
            sends = (c < 3) & (c - k >= 0) if leftward else (c > 0) & (c + k <= 3)

            @pl.when(sends)
            def _(leftward=leftward):
                back_arrived(leftward, k, j)

                def keep(inner, value):
                    back_s[leftward, k - 1, rows, inner] = (
                        value + back_r[leftward, k, rows, inner].astype(F32)).astype(BF16)

                terms(c - k if leftward else c + k, j, keep)
                back_copy(leftward, k, j).start()

    for e in range(4):
        for f in range(4):
            if e or f:
                there = pl.ds(pl.multiple_of((ring(p2, e) * t2 + ring(p1, f) * t1) * 128, 128), 128)
                arrived(w_ref.at[other, there, :], W_PART + 4 * e + f)
    products(c, 2, first=True)
    hand_on(2, 1)
    both_sides(1, 2, products)
    both_sides(2, 1, transposed)
    both_sides(2, 2, products)
    hand_on(3, 0)
    both_sides(3, 0, products)
    activate(0)
    for k in (3, 2, 1):
        back_first(k, 0)
    both_sides(3, 0, transposed)
    hand_on(3, 1)
    both_sides(3, 1, products)
    activate(1)
    both_sides(3, 1, transposed)

    offsets = (2, 1, 3, 0)

    def group_product(matrix, chips, piece, store):
        lhs = jnp.concatenate([tr[matrix, chip] for chip in chips], axis=0)

        @pl.loop(2 * piece, 2 * piece + 2, unroll=True)
        def _(n):
            cols = pl.ds(pl.multiple_of(n * 256, 256), 256)
            store(n, jnp.dot(lhs, act[matrix, :, cols], preferred_element_type=F32))

    core_copies = {}

    def group_theirs(piece, g):
        theirs = ring(p2, offsets[g])

        def keep_sent(n, value):
            g_send[g, n] = value.astype(BF16)

        group_product(other, [theirs * t2 + q * t1 for q in range(4)], piece, keep_sent)
        pair = pl.ds(2 * piece, 2)
        core_copies[piece, g] = start(g_send.at[g, pair], g_recv.at[g, pair], CORE_G + 2 * g + piece, partner)

    def group_own(piece, g):
        mine = ring(p1, offsets[g])

        def keep_own(n, value):
            g_own[g, n] = value

        group_product(m, [mine * t1 + q * t2 for q in range(4)], piece, keep_own)

    def reduced(dst, parts, rows):
        @pl.loop(0, rows // 128, unroll=True)
        def _(i):
            at = pl.ds(pl.multiple_of(i * 128, 128), 128)
            total = parts[0][at, :].astype(F32)
            for part in parts[1:]:
                total += part[at, :].astype(F32)
            dst[at, :] = total.astype(dst.dtype)

    ring1 = {}

    def chip_sum(g, n):
        return [g_own.at[g, n], g_recv.at[g, n]]

    def ring1_send(piece, g, h, which, device, extra=()):
        n = 2 * piece + h
        reduced(s1.at[g, n], chip_sum(g, n) + list(extra), BLK)
        ring1[piece, which] = start(s1.at[g, n], r1.at[which, piece], STAGE1 + 2 * which + piece, device)

    def first(piece):
        core_copies[piece, 0].wait_recv()
        ring1_send(piece, 0, 0, 0, right1)
        ring1_send(piece, 0, 1, 1, left1)

    def second(piece):
        core_copies[piece, 1].wait_recv()
        ring1_send(piece, 1, 1, 3, right1)
        core_copies[piece, 2].wait_recv()
        ring1_send(piece, 2, 0, 4, left1)

    def third(piece):
        ring1[piece, 0].wait_recv()
        ring1_send(piece, 1, 0, 2, right1, [r1.at[0, piece]])
        ring1[piece, 1].wait_recv()
        ring1_send(piece, 2, 1, 5, left1, [r1.at[1, piece]])

    ring2 = {}
    opp, nxt, prv = ring(p2, 2), ring(p2, 1), ring(p2, 3)

    def block(q, piece, h):
        at = pl.ds(pl.multiple_of(q * 128, 128), 128)
        return [
            ref.at[at, :] for ref in chip_sum(3, 2 * piece + h) + [r1.at[2 + h, piece], r1.at[4 + h, piece]]
        ]

    def ring2_send(piece, g, h, which, device, extra=()):
        n = 2 * piece + h
        reduced(s2.at[g, n], block((opp, nxt, prv)[g], piece, h) + list(extra), 128)
        ring2[piece, which] = start(s2.at[g, n], r2.at[which, piece], STAGE2 + 2 * which + piece, device)

    def ring2_first(piece):
        core_copies[piece, 3].wait_recv()
        for which in (3, 4, 2, 5):
            ring1[piece, which].wait_recv()
        ring2_send(piece, 0, 0, 0, right2)
        ring2_send(piece, 0, 1, 1, left2)
        ring2_send(piece, 1, 1, 3, right2)
        ring2_send(piece, 2, 0, 4, left2)

    def ring2_second(piece):
        ring2[piece, 0].wait_recv()
        ring2_send(piece, 1, 0, 2, right2, [r2.at[0, piece]])
        ring2[piece, 1].wait_recv()
        ring2_send(piece, 2, 1, 5, left2, [r2.at[1, piece]])

    travel = {}

    def dp_first(piece):
        for h, device in ((0, up2), (1, down2)):
            n = 2 * piece + h
            ring2[piece, 2 + h].wait_recv()
            ring2[piece, 4 + h].wait_recv()
            reduced(dp_s.at[n], block(p2, piece, h) + [r2.at[2 + h, piece], r2.at[4 + h, piece]], 128)
            travel[0, n] = start(dp_s.at[n], dp_z.at[n], DP + n, device)

    def dp_second(piece):
        for h, device in ((0, up2), (1, down2)):
            n = 2 * piece + h
            travel[0, n].wait_recv()
            travel[1, n] = start(dp_z.at[n], dp_r.at[n], DP + 4 + n, device)

    group_theirs(0, 0)
    group_theirs(0, 1)
    group_own(0, 0)
    group_theirs(0, 2)
    group_own(0, 1)
    group_own(0, 2)
    first(0)
    second(0)
    group_theirs(1, 0)
    group_own(1, 0)
    for k in (3, 2, 1):
        back_first(k, 1)
    third(0)
    group_theirs(1, 1)
    group_own(1, 1)
    first(1)
    group_theirs(1, 2)
    group_own(1, 2)
    second(1)
    group_theirs(0, 3)
    group_own(0, 3)
    ring2_first(0)
    group_theirs(1, 3)
    group_own(1, 3)
    third(1)
    ring2_second(0)
    back_on(2, 0)
    dp_first(0)
    ring2_first(1)
    back_on(1, 0)
    ring2_second(1)
    back_on(2, 1)
    dp_second(0)
    dp_first(1)
    back_on(1, 1)
    dp_second(1)

    def across_start(place, number, count, device, value):
        place[...] = value
        return [start(place, place, number + k - 1, device(k)) for k in range(1, count + 1)]

    def added(values):
        while len(values) > 1:
            values = [values[i] + values[i + 1] for i in range(0, len(values), 2)]
        return values[0]

    def across_end(copies):
        for copy in copies:
            copy.wait_recv()

    mom.wait_recv()
    lane = lax.broadcasted_iota(jnp.int32, (8, 128), 1)
    old_d = jnp.where((lane // 64) == core, dmom_ref[m], dmom_in[...])[0:1, :]
    old_f = jnp.where(core == 0, in_col_ref[...], out_row_ref[...])
    old_f_sum = jnp.sum(old_f, axis=1, keepdims=True)
    old_d_sum = jnp.sum(old_d, axis=1, keepdims=True)
    col_sums = []
    lanes = None
    for n in range(4):
        travel[1, n].wait_recv()
        grad = dp_s[n].astype(F32) + dp_r[n].astype(F32)
        ratio[n] = grad
        squared = grad * grad
        col_sums.append(jnp.sum(squared, axis=0, keepdims=True))
        folded = squared[:, 0:128] + squared[:, 128:256]
        lanes = folded if n == 0 else lanes + folded
    row_sums = jnp.sum(lanes.T, axis=0, keepdims=True)
    total = jnp.sum(row_sums, axis=1, keepdims=True)
    sub8 = lax.broadcasted_iota(jnp.int32, (8, 128), 0)
    sent_z = across_start(za.at[c], SUMS + 15, 3, along_z, jnp.where(sub8 == 0, row_sums, old_f_sum))
    sub = lax.broadcasted_iota(jnp.int32, (8, 256), 0)
    payload = jnp.where(sub == 4, old_d_sum, 0.0)
    for n in range(4):
        payload = jnp.where(sub == n, col_sums[n], payload)
    sent_xy = across_start(xa.at[chip], SUMS, 15, along_xy, payload)
    terms(c, 2, keep_mine(*CHUNKS[2]))
    across_end(sent_z)
    over_z = added([za[i] for i in range(4)])
    d_new = MOMENT_DECAY * old_d + (1.0 - MOMENT_DECAY) * (over_z[0:1, :] / ALL_UNITS + EPSILON_SQ)
    d_column = jnp.broadcast_to(1.0 / jnp.sqrt(d_new), (128, 128)).T[:, 0:1]
    across_end(sent_xy)
    over_xy = added([xa[i] for i in range(16)])
    old_mean = jnp.where(core == 0, over_xy[4:5, 0:1] / WIDTH, over_z[1:2, 0:1] / ALL_UNITS)
    f_new = [
        MOMENT_DECAY * old_f[:, n * 256:(n + 1) * 256]
        + (1.0 - MOMENT_DECAY) * (over_xy[n:n + 1, :] / WIDTH + EPSILON_SQ)
        for n in range(4)
    ]
    lanes = None
    for n in range(4):
        value = ratio[n] * (d_column * (1.0 / jnp.sqrt(f_new[n])))
        ratio[n] = value
        folded = value[:, 0:128] * value[:, 0:128] + value[:, 128:256] * value[:, 128:256]
        lanes = folded if n == 0 else lanes + folded
    folded = lanes[0:8]
    for i in range(1, 16):
        folded += lanes[i * 8:(i + 1) * 8]
    payload = jnp.concatenate([folded, jnp.where(sub8 == 0, total, old_mean)], axis=0)
    sent_z = across_start(zb.at[core, c], SUMS + 18, 7, along_z_and_cores, payload)

    theirs_at = pl.ds(pl.multiple_of(other * 64, 64), 64)
    swap_v[0] = jnp.zeros((8, UNITS), F32)
    for n in range(4):
        swap_u[0, :, n * 256:(n + 1) * 256] = ratio[n, theirs_at, :]
        swap_v[0, 0:1, n * 256:(n + 1) * 256] = f_new[n]
    swap_v[0, 1:2, 0:128] = d_new
    sent_u = start(swap_u.at[0], swap_u.at[1], SWAP, partner)
    sent_v = start(swap_v.at[0], swap_v.at[1], SWAP + 1, partner)

    for leftward in (0, 1):
        @pl.when((c < 3) if leftward else (c > 0))
        def _(leftward=leftward):
            for j in range(2):
                back_arrived(leftward, 0, j)
            reduced(it_own, [it_own, back_r.at[leftward, 0]], TOK)

    reduced(ig_s, [it_own], TOK)
    ig_out = pltpu.make_async_copy(ig_s, ig_ref, local.at[4])
    ig_out.start()

    across_end(sent_z)
    payload = jnp.stack([added([zb[i, j] for j in range(4)]) for i in range(2)])
    sent_xy = across_start(xb.at[chip], SUMS + 25, 15, along_xy, payload)
    across_end(sent_xy)
    factors = []
    for i in range(2):
        over_all = added([xb[j, i] for j in range(16)])
        mean = MOMENT_DECAY * (over_all[9:10, 0:1] / 64.0) + (1.0 - MOMENT_DECAY) * (
            over_all[8:9, 0:1] / ENTRIES + EPSILON_SQ)
        rms = jnp.sqrt(mean * (jnp.sum(over_all[0:8], keepdims=True) / ENTRIES))
        factors.append(jnp.sqrt(mean) / jnp.maximum(1.0, rms / CLIP_LIMIT))

    def own_lanes(value):
        return jnp.where(core == 0, value[:, 0:64], value[:, 64:128])

    sent_v.wait_recv()
    sent_u.wait_recv()

    def finish(update, row_of, d_out, f_out, which, scale):
        d_out[...] = own_lanes(swap_v[which, 1:2, 0:128])
        f_out[...] = swap_v[which, 0:1, :]
        for n in range(4):
            update[:, n * 256:(n + 1) * 256] = row_of(n) * scale

    def theirs(n):
        return swap_u[1, :, n * 256:(n + 1) * 256]

    @pl.when(core == 0)
    def _():
        finish(in_upd_ref, lambda n: ratio[n, 0:64, :], in_row_out, in_col_out, 0, factors[0])
        finish(out_upd_ref, theirs, out_col_out, out_row_out, 1, factors[1])

    @pl.when(core == 1)
    def _():
        finish(out_upd_ref, lambda n: ratio[n, 64:128, :], out_col_out, out_row_out, 0, factors[1])
        finish(in_upd_ref, theirs, in_row_out, in_col_out, 1, factors[0])

    ig_out.wait()
    for copy in pending:
        copy.wait_send()
    for leftward in (0, 1):
        for k in (1, 2, 3):
            @pl.when(line_sends(leftward, k))
            def _(leftward=leftward, k=k):
                for j in range(2):
                    line_copy(leftward, k, j).wait_send()

            @pl.when((c - k >= 0) if leftward else (c + k <= 3))
            def _(leftward=leftward, k=k):
                for j in range(2):
                    back_copy(leftward, k, j).wait_send()


def fused(*operands):
    vmem = pl.BlockSpec(memory_space=pltpu.VMEM)
    anywhere = pl.BlockSpec(memory_space=pl.ANY)
    return pl.pallas_call(
        kernel,
        out_shape=(
            jax.ShapeDtypeStruct((TOK, BLK), BF16),
            jax.ShapeDtypeStruct((64, UNITS), F32),
            jax.ShapeDtypeStruct((64, UNITS), F32),
            jax.ShapeDtypeStruct((1, 64), F32),
            jax.ShapeDtypeStruct((1, UNITS), F32),
            jax.ShapeDtypeStruct((1, UNITS), F32),
            jax.ShapeDtypeStruct((1, 64), F32),
        ),
        in_specs=[anywhere] * 8,
        out_specs=(anywhere,) + (vmem,) * 6,
        scratch_shapes=[
            pltpu.VMEM((1, 64), F32),
            pltpu.VMEM((1, UNITS), F32),
            pltpu.VMEM((1, UNITS), F32),
            pltpu.VMEM((1, 64), F32),
            pltpu.VMEM((2, 8, 128), F32),
            pltpu.VMEM((2, 4, TOK, BLK), BF16),
            pltpu.VMEM((2, WIDTH, UNITS), BF16),
            pltpu.VMEM((2, TOK, UNITS), F32),
            pltpu.VMEM((2, 16, 128, TOK), BF16),
            pltpu.VMEM((2, TOK, UNITS), BF16),
            pltpu.VMEM((4, 4, 512, 256), F32),
            pltpu.VMEM((4, 4, 512, 256), BF16),
            pltpu.VMEM((4, 4, 512, 256), BF16),
            pltpu.VMEM((3, 4, 512, 256), BF16),
            pltpu.VMEM((6, 2, 512, 256), BF16),
            pltpu.VMEM((3, 4, 128, 256), BF16),
            pltpu.VMEM((6, 2, 128, 256), BF16),
            pltpu.VMEM((4, 128, 256), BF16),
            pltpu.VMEM((4, 128, 256), BF16),
            pltpu.VMEM((4, 128, 256), BF16),
            pltpu.VMEM((8, 128), F32),
            pltpu.VMEM((4, 8, 128), F32),
            pltpu.VMEM((16, 8, 256), F32),
            pltpu.VMEM((2, 4, 16, 128), F32),
            pltpu.VMEM((16, 2, 16, 128), F32),
            pltpu.VMEM((4, 128, 256), F32),
            pltpu.VMEM((2, 64, UNITS), F32),
            pltpu.VMEM((2, 8, UNITS), F32),
            pltpu.VMEM((2, 3, TOK, BLK), BF16),
            pltpu.VMEM((2, 3, TOK, BLK), BF16),
            pltpu.VMEM((TOK, BLK), F32),
            pltpu.VMEM((TOK, BLK), BF16),
            pltpu.SemaphoreType.DMA((N_SEM,)),
            pltpu.SemaphoreType.DMA((N_SEM,)),
            pltpu.SemaphoreType.DMA((9,)),
        ],
        compiler_params=pltpu.CompilerParams(
            collective_id=0, has_side_effects=True, vmem_limit_bytes=60 * 1024 * 1024
        ),
        cost_estimate=pl.CostEstimate(
            flops=10 * TOK * WIDTH * UNITS, bytes_accessed=16 * 2**20, transcendentals=TOK * UNITS
        ),
    )(*operands)


def handed_out_kernel(*refs):
    count = len(refs) // 2
    for i in range(count):
        refs[count + i][...] = refs[i][...]


def handed_out(*results):
    vmem = pl.BlockSpec(memory_space=pltpu.VMEM)
    return pl.pallas_call(
        handed_out_kernel,
        out_shape=tuple(jax.ShapeDtypeStruct(result.shape, result.dtype) for result in results),
        in_specs=[vmem] * len(results),
        out_specs=(vmem,) * len(results),
        compiler_params=pltpu.CompilerParams(vmem_limit_bytes=60 * 1024 * 1024),
    )(*results)


def per_device(
    saved_input, cotangent, weight_in, weight_out, in_row_moment, in_col_moment, out_row_moment, out_col_moment
):
    input_grad, in_update, out_update_t, in_row, in_col, out_row, out_col = handed_out(*fused(
        saved_input, cotangent, weight_in, weight_out.T, in_row_moment.reshape(1, 64), in_col_moment.reshape(1, UNITS),
        out_row_moment.reshape(1, UNITS), out_col_moment.reshape(1, 64),
    ))
    return (
        input_grad, in_update, out_update_t.T, in_row.reshape(64), in_col.reshape(UNITS), out_row.reshape(UNITS),
        out_col.reshape(64),
    )


def solution(mesh):
    placed = (
        P(("dp", "row"), "col"), P(("dp", "row"), "col"), P("row", "col"), P("col", "row"),
        P("row"), P("col"), P("col"), P("row"),
    )
    return jax.shard_map(
        per_device,
        mesh=mesh,
        in_specs=placed,
        out_specs=(
            P(("dp", "row"), "col"), P("row", "col"), P("col", "row"), P("row"), P("col"), P("col"), P("row"),
        ),
        check_vma=False,
    )
```
